256 devices in a mesh: dp: 8 (over x, core), expert: 32 (over y, z).
Axes of the slice: x: 4, y: 4, z: 8, core: 2. Of those that a mesh axis runs over, the one named last changes fastest.
Arguments:
- frames: bfloat16 [32768, 1024], P(('dp', 'expert')), may hold values from -6 to 6
- lengths: int32 [256, 4], P(('dp', 'expert')), may hold values from 1 to 80, 128 in all within a row
- w_qkv: bfloat16 [1024, 3072], P('expert'), may hold values from -4 to 4
- w_out: bfloat16 [1024, 1024], P('expert'), may hold values from -0.1875 to 0.1875
- conv_w: float32 [31, 1024], replicated, may hold values from -1 to 1
- w_router: bfloat16 [1024, 64], replicated, may hold values from -0.1875 to 0.1875
- expert_ids: int32 [32768, 2], P(('dp', 'expert')), may hold values from 0 to 63, all different within a row; in each aligned block of 128 rows (0 to 127, 128 to 255, ...) at most 5 rows name the same one
- w_up: bfloat16 [64, 1024, 4096], P('expert', None, 'dp'), may hold values from -0.1875 to 0.1875
- w_down: bfloat16 [64, 4096, 1024], P('expert', 'dp'), may hold values from -0.09375 to 0.09375
Outputs:
- block_out: bfloat16 [32768, 1024], P(('dp', 'expert'))
The draws below stay inside these ranges and needn't reach their ends.
Inputs may be any that keep to these rules, and one draw needn't show every extreme that they name: `expert_ids`: among the rows of one device no expert is named by more than 5 rows. `lengths`: each row sums to 128.
All inputs are finite; a program needn't handle non-finite values.
Results may differ from the reference program's by a relative error of at most 0.017.
Values may be sent and summed in bfloat16 or wider, within the bound.
A program may use at most 128 MiB of HBM per device.

```python
import math
import jax
import jax.numpy as jnp
import numpy as np
from jax import lax

D = 1024
HEADS = 16
HEAD_DIM = 64
FF = 4096
KW = 31
BLK = 128
TOP = 2
UTT = 4
TOK_DEV = 128
EXPERTS = 64
CAP = 5
TOKENS = 32768
N_DP = 8
DEVICES = 256


def draw_w_qkv(key, part):
    key = jax.random.fold_in(key, 7)
    entry_key = jax.random.fold_in(key, 0)
    base = jax.random.truncated_normal(entry_key, -4.0, 4.0, (D, 3 * D), jnp.float32) / math.sqrt(D)
    return base.astype(jnp.bfloat16)


def level_of(stream_key, extent, cuts, smallest, largest):
    def one(axis_at, parts):
        draws = jax.random.uniform(jax.random.fold_in(jax.random.fold_in(stream_key, 6), axis_at), (parts,), jnp.float32, smallest / len(cuts), largest / len(cuts))
        return jnp.repeat(jnp.exp(draws), extent[axis_at] // parts).reshape((-1,) + (1,) * (len(extent) - axis_at - 1))

    factor_of = one(*cuts[0])
    for cut in cuts[1:]:
        factor_of = factor_of * one(*cut)
    return factor_of


def split_up(amount, total, most, slope):
    portions = [(1 << 20) // math.isqrt(grade ** slope) + 1 for grade in range(2, amount + 1)]
    rest, holding = total - most - (amount - 1), [1] * (amount - 1)
    while rest > 0:
        free = [i for i in range(amount - 1) if holding[i] < most]
        mass, left = sum([portions[i] for i in free]), rest
        for i in free:
            more = min(most - holding[i], max(1, left * portions[i] // mass), rest)
            holding[i] = holding[i] + more
            rest = rest - more
    return np.array([most] + holding)


def ragged_sizes(rng, amount, total, reach, skew):
    if amount == 2:
        one = jax.random.randint(rng, (), max(1, total - reach), min(reach, total - 1) + 1)
        return jnp.stack([one, total - one])
    sizes = jnp.asarray(split_up(amount, total, reach, skew), jnp.int32)
    twos = (amount - 1) // 2
    source_of, sink = sizes[1:1 + 2 * twos:2], sizes[2:2 + 2 * twos:2]
    margin = jnp.minimum(source_of - 1, reach - sink)
    shifted = jax.random.randint(jax.random.fold_in(rng, 1), (twos,), 0, 1 << 20) % (margin + 1)
    sizes = sizes.at[1:1 + 2 * twos:2].set(source_of - shifted).at[2:2 + 2 * twos:2].set(sink + shifted)
    return sizes[jax.random.permutation(jax.random.fold_in(rng, 2), amount)]


def deal_out(key, own, number, rows, number_of, top, bound, slope):
    order = jax.random.permutation(key, number_of)
    crowded, usual = load_shares(number_of, rows * top, bound, slope, True), load_shares(number_of, rows * top, bound, slope, False)
    places = jnp.arange(number_of)

    def named(tallies, rotation):
        used = int((tallies > 0).sum())
        fixed = max(1, used // 4)
        moved = fixed + (places - fixed + rotation * (used - fixed)) % max(1, number_of - fixed)
        return jnp.zeros((number_of,), jnp.int32).at[order[jnp.where(places < fixed, places, moved)]].set(jnp.asarray(tallies, jnp.int32))

    tallies = jnp.where(number % 4 == 0, named(crowded, number // 4), named(usual, number - number // 4 - 1))
    mixed = jax.random.permutation(jax.random.fold_in(own, 3), number_of)
    giver, sink = mixed[0:number_of // 2 * 2:2], mixed[1:number_of // 2 * 2:2]
    slack = jnp.minimum(tallies[giver] - 1, bound - tallies[sink]) // 2
    slack = jnp.where((giver == order[0]) | (sink == order[0]) | (tallies[sink] == 0), 0, jnp.maximum(slack, 0))
    moved = jax.random.randint(jax.random.fold_in(own, 4), (number_of // 2,), 0, 1 << 20) % (slack + 1)
    tallies = tallies.at[giver].add(-moved).at[sink].add(moved)
    members = jnp.searchsorted(jnp.cumsum(tallies), jnp.arange(rows * top), side="right").astype(jnp.int32)
    grid = members.reshape(top, rows).T
    grid = grid[jax.random.permutation(jax.random.fold_in(own, 1), rows)]
    rotation = jax.random.randint(jax.random.fold_in(own, 2), (rows, 1), 0, top)
    return jnp.take_along_axis(grid, (jnp.arange(top)[None, :] + rotation) % top, axis=1)


def load_shares(count, total, bound, lean, full):
    loads = [(1 << 20) // math.isqrt(standing ** lean) + 1 for standing in range(1, count + 1)]
    largest = bound if full else min(bound, max(-(-total // count), total * loads[0] // sum(loads)))
    least = 1 if total - largest >= count - 1 else 0
    given, rest = [largest] + [least] * (count - 1), total - largest - least * (count - 1)
    while rest > 0:
        free = [i for i in range(1, count) if given[i] < largest] or [i for i in range(1, count) if given[i] < bound]
        pool, budget = sum([loads[i] for i in free]), rest
        for i in free:
            more = min(bound - given[i], max(1, budget * loads[i] // pool), rest)
            given[i] = given[i] + more
            rest = rest - more
    return np.array(given)


def bell_draw(key, dims, scale, limit, shards=(), kind=jnp.bfloat16):
    values = scale * jax.random.normal(key, dims, jnp.float32)
    if shards:
        values = values * level_of(key, dims, shards, -0.22, 0.18)
    return jnp.clip(values, -limit, limit).astype(kind)


def setup_inputs(seed: int = 0) -> dict:
    streams_of = jax.random.split(jax.random.key(seed), 10)
    frames = bell_draw(streams_of[0], (TOKENS, D), 1.0, 6.0, ((0, 256),))
    lengths = jax.vmap(lambda own: ragged_sizes(own, UTT, TOK_DEV, TOK_DEV * 5 // 8, 2))(jax.random.split(streams_of[1], DEVICES)).reshape((DEVICES, UTT)).astype(jnp.int32)
    w_qkv = draw_w_qkv(jax.random.fold_in(streams_of[9], 71), 0)
    w_out = bell_draw(streams_of[3], (D, D), D ** -0.5, 0.1875, ((0, 32),))
    conv_w = bell_draw(streams_of[4], (KW, D), KW ** -0.5, 1.0, (), jnp.float32)
    w_router = bell_draw(streams_of[5], (D, EXPERTS), D ** -0.5, 0.1875)
    expert_ids_keys = jax.random.split(jax.random.fold_in(streams_of[6], 1), TOKENS // TOK_DEV)
    expert_ids_turns = jax.random.permutation(jax.random.fold_in(streams_of[6], 3), TOKENS // TOK_DEV)
    expert_ids = jax.vmap(lambda own, number: deal_out(jax.random.fold_in(streams_of[6], 2), own, number, TOK_DEV, EXPERTS, TOP, CAP, 2))(expert_ids_keys, expert_ids_turns).reshape((TOKENS, TOP))
    w_up = bell_draw(streams_of[7], (EXPERTS, D, FF), D ** -0.5, 0.1875, ((0, 32), (2, 8)))
    w_down = bell_draw(streams_of[8], (EXPERTS, FF, D), FF ** -0.5, 0.09375, ((0, 32), (1, 8)))
    return {"frames": frames, "lengths": lengths, "w_qkv": w_qkv, "w_out": w_out, "conv_w": conv_w, "w_router": w_router, "expert_ids": expert_ids, "w_up": w_up, "w_down": w_down}


def normalize(values):
    mean_value = lax.optimization_barrier(jnp.mean(values, axis=-1, keepdims=True))
    centred = values - mean_value
    variance = lax.optimization_barrier(jnp.mean(centred * centred, axis=-1, keepdims=True))
    return centred * lax.rsqrt(variance + 1e-05)

def segment_rows(row_lengths, count_rows):
    ends = jnp.cumsum(row_lengths)
    offsets = jnp.arange(count_rows, dtype=jnp.int32)
    return lax.optimization_barrier(jnp.sum((offsets[:, None] >= ends[None, :]).astype(jnp.int32), axis=1))

def depthwise(normed, kernel, segments):
    half_width = (kernel.shape[0] - 1) // 2
    count_rows = normed.shape[0]
    padded = jnp.pad(normed, ((half_width, half_width), (0, 0)))
    seg_padded = jnp.pad(segments, (half_width, half_width), constant_values=-1)
    total = jnp.zeros_like(normed)
    for offset in range(kernel.shape[0]):
        window = padded[offset:offset + count_rows]
        same = (seg_padded[offset:offset + count_rows] == segments).astype(normed.dtype)
        total = total + kernel[offset][None, :] * window * same[:, None]
    return total

def block_attention(qkv, segments):
    count_rows = qkv.shape[0]
    blocks = count_rows // BLK
    pieces = qkv.reshape(blocks, BLK, 3, HEADS, HEAD_DIM).astype(jnp.float32)
    scores = jnp.einsum('cqhd,ckhd->chqk', pieces[:, :, 0], pieces[:, :, 1]) * HEAD_DIM ** (-0.5)
    seg_blocks = segments.reshape(blocks, BLK)
    allowed = seg_blocks[:, :, None] == seg_blocks[:, None, :]
    scores = jnp.where(allowed[:, None], scores, -1e+30)
    highest = lax.optimization_barrier(jnp.max(scores, axis=-1, keepdims=True))
    expo = jnp.exp(scores - highest)
    probs = (expo / lax.optimization_barrier(jnp.sum(expo, axis=-1, keepdims=True))).astype(jnp.bfloat16)
    mixed = jnp.einsum('chqk,ckhd->cqhd', probs.astype(jnp.float32), pieces[:, :, 2])
    return mixed.astype(jnp.bfloat16).reshape(count_rows, HEADS * HEAD_DIM)

def reference(frames, lengths, w_qkv, w_out, conv_w, w_router, expert_ids, w_up, w_down):
    device_count = lengths.shape[0]

    def front(inputs):
        block, row_lengths = inputs
        segments = segment_rows(row_lengths, TOK_DEV)
        normed_in = normalize(block.astype(jnp.float32)).astype(jnp.bfloat16)
        qkv = jnp.dot(normed_in, w_qkv, preferred_element_type=jnp.float32).astype(jnp.bfloat16)
        mixed = block_attention(qkv, segments)
        first = (block.astype(jnp.float32) + jnp.dot(mixed, w_out, preferred_element_type=jnp.float32)).astype(jnp.bfloat16)
        conv_in = normalize(first.astype(jnp.float32))
        conv_out = depthwise(conv_in, conv_w, segments)
        return (first.astype(jnp.float32) + jax.nn.silu(conv_out)).astype(jnp.bfloat16)
    second = lax.map(front, (frames.reshape(device_count, TOK_DEV, D), lengths)).reshape(TOKENS, D)
    hidden = normalize(second.astype(jnp.float32)).astype(jnp.bfloat16)
    logits = jnp.dot(hidden, w_router, preferred_element_type=jnp.float32)
    gates = jax.nn.sigmoid(jnp.take_along_axis(logits, expert_ids, axis=1))
    flat_ids = expert_ids.reshape(device_count, TOK_DEV * TOP)
    onehot = (flat_ids[:, :, None] == jnp.arange(EXPERTS, dtype=jnp.int32)[None, None, :]).astype(jnp.int32)
    slots = lax.optimization_barrier(jnp.sum(jnp.cumsum(onehot, axis=1) * onehot, axis=2)) - 1
    owners = jnp.arange(device_count, dtype=jnp.int32)[:, None]
    position = (owners * CAP + slots).reshape(-1).astype(jnp.int32)
    expert_flat = flat_ids.reshape(-1).astype(jnp.int32)
    source_row = (jnp.arange(TOKENS * TOP, dtype=jnp.int32) // TOP).astype(jnp.int32)
    table = jnp.full((EXPERTS, device_count * CAP), TOKENS, jnp.int32).at[expert_flat, position].set(source_row)
    padded = jnp.concatenate([hidden, jnp.zeros((1, D), jnp.bfloat16)], axis=0)

    def expert_pass(inputs):
        row_index, up_matrix, down_matrix = inputs
        routed = padded[row_index]
        activated = jax.nn.silu(jnp.dot(routed, up_matrix, preferred_element_type=jnp.float32)).astype(jnp.bfloat16)
        split_act = activated.reshape(activated.shape[0], N_DP, FF // N_DP).astype(jnp.float32)
        split_down = down_matrix.reshape(N_DP, FF // N_DP, D).astype(jnp.float32)
        partial_value = lax.optimization_barrier(jnp.einsum('rbf,bfd->brd', split_act, split_down).astype(jnp.bfloat16))
        return lax.optimization_barrier(jnp.sum(partial_value.astype(jnp.float32), axis=0)).astype(jnp.bfloat16)
    results = lax.map(expert_pass, (table, w_up, w_down))
    picked = results[expert_flat, position].reshape(TOKENS, TOP, D)
    combined = second.astype(jnp.float32) + lax.optimization_barrier(jnp.sum(gates[:, :, None] * picked.astype(jnp.float32), axis=1))
    return combined.astype(jnp.bfloat16)
```

```python
import functools

import jax
import jax.numpy as jnp
from jax import lax
from jax.experimental import pallas as pl
from jax.experimental.pallas import tpu as pltpu
from jax.sharding import PartitionSpec as P

HEADS = 16
HEAD_DIM = 64
ROWS = 128
D = 1024
TOP = 2
NX, NY, NZ = 4, 4, 8
EXPERT_DEVS = NY * NZ
CAP = 5
CELL = 2 * CAP
SUB = CELL * D // 128
QCOLS = 384
OCOLS = 512
WCOLS = QCOLS + OCOLS
XROWS = ROWS + 16
MESH = pl.DeviceIdType.MESH
ANY = pl.BlockSpec(memory_space=pl.ANY)
VMEM = pl.BlockSpec(memory_space=pltpu.VMEM)
BF = jnp.bfloat16
F32 = jnp.float32


def normalize(values):
    mean_value = jnp.mean(values, axis=-1, keepdims=True)
    centred = values - mean_value
    variance = jnp.mean(centred * centred, axis=-1, keepdims=True)
    return centred * lax.rsqrt(variance + 1e-05)


class Place:
    def __init__(self):
        dp, ex = lax.axis_index("dp"), lax.axis_index("expert")
        self.dp, self.ex = dp, ex
        self.x, self.c = dp // 2, dp % 2
        self.y, self.z = ex // NZ, ex % NZ

    def at(self, dx=0, dy=0, dz=0, other=False):
        x, y, z = (self.x + dx + NX) % NX, (self.y + dy + NY) % NY, (self.z + dz + NZ) % NZ
        c = 1 - self.c if other else self.c
        return (x * 2 + c, y * NZ + z)


class Sends:
    def __init__(self, send_sem, recv_sem):
        self.send_sem, self.recv_sem, self.copies = send_sem, recv_sem, []

    def start(self, src, dst, device):
        at = len(self.copies)
        copy = pltpu.make_async_remote_copy(
            src_ref=src,
            dst_ref=dst,
            send_sem=self.send_sem.at[at],
            recv_sem=self.recv_sem.at[at],
            device_id=device,
            device_id_type=MESH,
        )
        copy.start()
        self.copies.append(copy)
        return copy

    def finish(self):
        for copy in self.copies:
            copy.wait_send()


def greet(devices):
    barrier = pltpu.get_barrier_semaphore()
    for device in devices:
        pl.semaphore_signal(barrier, inc=1, device_id=device, device_id_type=MESH)
    pl.semaphore_wait(barrier, len(devices))


def run_tasks(tasks):
    waiting = [(task, next(task, None)) for task in tasks]
    while waiting:
        later = []
        for task, copy in waiting:
            if copy is None:
                continue
            copy.wait_recv()
            later.append((task, next(task, None)))
        waiting = later


GATHER_SENDS = 64


def gather_kernel(
    xc, wqkv, wout, wup, wdn, xg, wg, up2, dn2, send_sem, recv_sem, local_sem
):
    me = Place()
    x, c, y, z, dp = me.x, me.c, me.y, me.z, me.dp
    sib = me.at(other=True)
    xr, xl = me.at(dx=1), me.at(dx=-1)
    yu, yd = me.at(dy=1), me.at(dy=-1)
    zu, zd = me.at(dz=1), me.at(dz=-1)
    locals_ = []

    def local(src, dst):
        copy = pltpu.make_async_copy(src, dst, local_sem.at[len(locals_)])
        copy.start()
        locals_.append(copy)

    for part in range(3):
        columns = pl.ds(pl.multiple_of(part * D + dp * 128, 128), 128)
        local(wqkv.at[:, columns], wg.at[y, z, :, pl.ds(part * 128, 128)])
    local(
        wout.at[:, pl.ds(pl.multiple_of(c * OCOLS, 128), OCOLS)],
        wg.at[y, z, :, pl.ds(QCOLS, OCOLS)],
    )
    local(xc, xg.at[dp])
    local(wup.at[c], up2.at[c])
    local(wdn.at[c], dn2.at[c])

    greet([sib, xr, xl, yu, yd, zu, zd])
    sends = Sends(send_sem, recv_sem)
    start = sends.start
    first_sib = start(xc, xg.at[dp], sib)
    to_r = start(xc, xg.at[dp], xr)
    to_l = start(xc, xg.at[dp], xl)
    for copy in locals_[:4]:
        copy.wait()

    def yy(d):
        return (y + d + NY) % NY

    def zz(d):
        return (z + d + NZ) % NZ

    def x_chain():
        left = xg.at[((x + NX - 1) % NX) * 2 + c]
        right = xg.at[((x + 1) % NX) * 2 + c]
        across = xg.at[((x + 2) % NX) * 2 + c]
        yield to_r
        low = left.at[pl.ds(0, 80)]
        relay_r = start(low, low, xr)
        sib1 = start(left, left, sib)
        yield to_l
        high = right.at[pl.ds(80, 64)]
        relay_l = start(high, high, xl)
        sib2 = start(right, right, sib)
        yield relay_r
        yield relay_l
        sib3 = start(across, across, sib)
        for copy in (first_sib, sib1, sib2, sib3):
            yield copy

    def z_first():
        def block(dy, dz):
            return wg.at[yy(dy), zz(dz), pl.ds(0, 16)]

        spread = []

        def available(dz):
            spread.append(
                (dz, start(block(0, dz), block(0, dz), yu), start(block(0, dz), block(0, dz), yd))
            )

        up = start(block(0, 0), block(0, 0), zu)
        down = start(block(0, 0), block(0, 0), zd)
        available(0)
        for s in range(1, 4):
            yield up
            up = start(block(0, -s), block(0, -s), zu)
            available(-s)
            yield down
            if s < 3:
                down = start(block(0, s), block(0, s), zd)
            available(s)
        yield up
        available(4)
        last = []
        for dz, to_u, to_d in spread:
            yield to_u
            yield to_d
            if dz in (0, 1, 2, 3):
                last.append(start(block(-1, dz), block(-1, dz), yu))
            else:
                last.append(start(block(1, dz), block(1, dz), yd))
        for copy in last:
            yield copy

    def y_first():
        def block(dy):
            return wg.at[yy(dy), z, pl.ds(16, 16)]

        def bundle(dz, first=0, count=NY):
            return wg.at[pl.ds(first, count), zz(dz), pl.ds(16, 16)]

        to_u = start(block(0), block(0), yu)
        to_d = start(block(0), block(0), yd)
        yield to_u
        relay = start(block(-1), block(-1), yu)
        yield to_d
        yield relay
        up = start(bundle(0), bundle(0), zu)
        down = start(bundle(0), bundle(0), zd)
        for s in range(1, 4):
            yield up
            if s < 3:
                up = start(bundle(-s), bundle(-s), zu)
            else:
                up = start(bundle(-s, 0, 2), bundle(-s, 0, 2), zu)
            yield down
            if s < 3:
                down = start(bundle(s), bundle(s), zd)
            else:
                down = start(bundle(s, 2, 2), bundle(s, 2, 2), zd)
        yield up
        yield down

    def swap():
        one = start(wup.at[1 - c], up2.at[c], sib)
        two = start(wdn.at[1 - c], dn2.at[c], sib)
        yield from ()
        swaps.extend((one, two))

    swaps = []
    run_tasks([y_first(), z_first(), x_chain(), swap()])
    for copy in swaps:
        copy.wait_recv()
    for copy in locals_[4:]:
        copy.wait()
    sends.finish()


def gather_all(xc, w_qkv, w_out, w_up, w_down):
    return pl.pallas_call(
        gather_kernel,
        out_shape=(
            jax.ShapeDtypeStruct((8, XROWS, D), BF),
            jax.ShapeDtypeStruct((NY, NZ, 32, WCOLS), BF),
            jax.ShapeDtypeStruct(w_up.shape, BF),
            jax.ShapeDtypeStruct(w_down.shape, BF),
        ),
        in_specs=[ANY] * 5,
        out_specs=[ANY] * 4,
        scratch_shapes=[
            pltpu.SemaphoreType.DMA((GATHER_SENDS,)),
            pltpu.SemaphoreType.DMA((GATHER_SENDS,)),
            pltpu.SemaphoreType.DMA((8,)),
        ],
        compiler_params=pltpu.CompilerParams(collective_id=0, has_side_effects=True),
        name="gather",
    )(xc, w_qkv, w_out, w_up, w_down)


def attention_kernel(x_ref, w_ref, out_ref):
    block = x_ref[0]
    qkv = jnp.dot(block[:ROWS], w_ref[...], preferred_element_type=F32).astype(BF)
    marks = block[ROWS : ROWS + 4, :ROWS].astype(F32)
    same = lax.dot_general(marks, marks, (((0,), (0,)), ((), ())), preferred_element_type=F32)
    allowed = same > 0.5
    for h in range(2):
        q = qkv[:, h * 64 : h * 64 + 64]
        k = qkv[:, 128 + h * 64 : 128 + h * 64 + 64]
        v = qkv[:, 256 + h * 64 : 256 + h * 64 + 64]
        scores = lax.dot_general(q, k, (((1,), (1,)), ((), ())), preferred_element_type=F32)
        scores = jnp.where(allowed, scores * HEAD_DIM ** (-0.5), -1e30)
        highest = jnp.max(scores, axis=-1, keepdims=True)
        expo = jnp.exp(scores - highest)
        probs = (expo / jnp.sum(expo, axis=-1, keepdims=True)).astype(BF)
        mixed = jnp.dot(probs, v, preferred_element_type=F32).astype(BF)
        out_ref[0, :, h * 64 : h * 64 + 64] = mixed


def attention(xg, wg):
    return pl.pallas_call(
        attention_kernel,
        grid=(8,),
        out_shape=jax.ShapeDtypeStruct((8, ROWS, 128), BF),
        in_specs=[
            pl.BlockSpec((1, XROWS, D), lambda i: (i, 0, 0)),
            pl.BlockSpec((D, QCOLS), lambda i: (0, 0)),
        ],
        out_specs=pl.BlockSpec((1, ROWS, 128), lambda i: (i, 0, 0)),
        compiler_params=pltpu.CompilerParams(vmem_limit_bytes=24 << 20),
        name="attention",
    )(xg, wg.reshape(D, WCOLS))


def heads_kernel(mixed, wg, out, wo, send_sem, recv_sem, local_sem):
    me = Place()
    dp, c = me.dp, me.c
    peers = [((dp + o) % 8, me.ex) for o in range(1, 8)]
    sib = me.at(other=True)
    half = pl.ds(pl.multiple_of(c * OCOLS, 128), OCOLS)
    mine = wg.at[:, :, :, pl.ds(QCOLS, OCOLS)]
    keep = pltpu.make_async_copy(mixed.at[dp], out.at[dp], local_sem.at[0])
    keep.start()
    keep_w = pltpu.make_async_copy(mine, wo.at[:, :, :, half], local_sem.at[1])
    keep_w.start()
    greet(peers)
    sends = Sends(send_sem, recv_sem)
    for o in range(1, 8):
        sends.start(mixed.at[(dp + o) % 8], out.at[dp], peers[o - 1])
    sends.start(mine, wo.at[:, :, :, half], sib)
    for copy in sends.copies:
        copy.wait_recv()
    keep.wait()
    keep_w.wait()
    sends.finish()


def heads_back(mixed, wg):
    return pl.pallas_call(
        heads_kernel,
        out_shape=(
            jax.ShapeDtypeStruct((8, ROWS, 128), BF),
            jax.ShapeDtypeStruct((NY, NZ, 32, D), BF),
        ),
        in_specs=[ANY] * 2,
        out_specs=[ANY] * 2,
        scratch_shapes=[
            pltpu.SemaphoreType.DMA((8,)),
            pltpu.SemaphoreType.DMA((8,)),
            pltpu.SemaphoreType.DMA((2,)),
        ],
        compiler_params=pltpu.CompilerParams(collective_id=1, has_side_effects=True),
        name="heads_back",
    )(mixed, wg)


PLANE = [(dy, dz) for dz in range(NZ) for dy in range(NY) if (dy, dz) != (0, 0)]


def plane_peers(me):
    return [me.at(dy=dy, dz=dz) for dy, dz in PLANE]


def dispatch_kernel(cells, out, send_sem, recv_sem, local_sem):
    me = Place()
    x, y, z = me.x, me.y, me.z
    xr, xl = me.at(dx=1), me.at(dx=-1)
    keep = pltpu.make_async_copy(cells.at[y, z], out.at[x, z, y], local_sem.at[0])
    keep.start()
    greet(plane_peers(me) + [xr, xl])
    sends = Sends(send_sem, recv_sem)
    start = sends.start
    order = (0, 1, 7, 2, 6, 3, 5, 4)
    direct = {}
    for dz in order:
        for dy in range(NY):
            if (dy, dz) != (0, 0):
                src = cells.at[(y + dy) % NY, (z + dz) % NZ]
                direct[dy, dz] = start(src, out.at[x, z, y], me.at(dy=dy, dz=dz))
    keep.wait()
    right, left = (x + 1) % NX, (x + NX - 1) % NX
    sideways, last = [], []

    def relay(i):
        group = (z - order[i] + NZ) % NZ
        to_r, to_l = sideways[i]
        to_r.wait_recv()
        low = out.at[left, group, pl.ds(0, 2)]
        last.append(start(low, low, xr))
        to_l.wait_recv()
        high = out.at[right, group, pl.ds(2, 2)]
        last.append(start(high, high, xl))

    for i, dz in enumerate(order):
        for dy in range(NY):
            if (dy, dz) != (0, 0):
                direct[dy, dz].wait_recv()
        block = out.at[x, (z - dz + NZ) % NZ]
        sideways.append((start(block, block, xr), start(block, block, xl)))
        if i >= 1:
            relay(i - 1)
    relay(NZ - 1)
    for copy in last:
        copy.wait_recv()
    sends.finish()


def dispatch(cells):
    count = 31 + 4 * NZ
    return pl.pallas_call(
        dispatch_kernel,
        out_shape=jax.ShapeDtypeStruct((NX, NZ, NY, SUB, 128), BF),
        in_specs=[ANY],
        out_specs=ANY,
        scratch_shapes=[
            pltpu.SemaphoreType.DMA((count,)),
            pltpu.SemaphoreType.DMA((count,)),
            pltpu.SemaphoreType.DMA((1,)),
        ],
        compiler_params=pltpu.CompilerParams(collective_id=2, has_side_effects=True),
        name="dispatch",
    )(cells)


def combine_kernel(
    part, out, rel_r, rel_l, in_l, in_r, sum_r, sum_l, total, send_sem, recv_sem, local_sem
):
    me = Place()
    x, y, z = me.x, me.y, me.z
    xr, xl = me.at(dx=1), me.at(dx=-1)
    right, left, across = (x + 1) % NX, (x + NX - 1) % NX, (x + 2) % NX
    greet(plane_peers(me) + [xr, xl])
    sends = Sends(send_sem, recv_sem)
    start = sends.start
    order = (4, 3, 5, 2, 6, 1, 7, 0)
    low, high = pl.ds(0, 2), pl.ds(2, 2)
    begun, second, final = [], [], []

    def begin(i):
        g = (z + order[i]) % NZ
        begun.append(
            (
                start(part.at[across, g, low], rel_r.at[g], xr),
                start(part.at[across, g, high], rel_l.at[g], xl),
                start(part.at[right, g, high], in_l.at[g, high], xr),
                start(part.at[left, g, low], in_r.at[g, low], xl),
            )
        )

    def add(i):
        g = (z + order[i]) % NZ
        begun[i][0].wait_recv()
        sum_r[g] = (part[right, g, low].astype(F32) + rel_r[g].astype(F32)).astype(BF)
        one = start(sum_r.at[g], in_l.at[g, low], xr)
        begun[i][1].wait_recv()
        sum_l[g] = (part[left, g, high].astype(F32) + rel_l[g].astype(F32)).astype(BF)
        two = start(sum_l.at[g], in_r.at[g, high], xl)
        second.append((one, two))

    def close(i):
        g = (z + order[i]) % NZ
        begun[i][2].wait_recv()
        begun[i][3].wait_recv()
        second[i][0].wait_recv()
        second[i][1].wait_recv()
        total[g] = (
            part[x, g].astype(F32) + in_l[g].astype(F32) + in_r[g].astype(F32)
        ).astype(BF)
        for dy in range(NY):
            src = total.at[g, (y + dy) % NY]
            if (dy, order[i]) == (0, 0):
                keep = pltpu.make_async_copy(src, out.at[z, y], local_sem.at[0])
                keep.start()
                final.append(keep)
            else:
                start(src, out.at[z, y], me.at(dy=dy, dz=order[i]))
                final.append(sends.copies[-1])

    ahead = 3
    for i in range(ahead):
        begin(i)
    for i in range(NZ):
        if i + ahead < NZ:
            begin(i + ahead)
        add(i)
        if i >= 1:
            close(i - 1)
    close(NZ - 1)
    for copy in final[:-NY]:
        copy.wait_recv()
    final[-NY].wait()
    for copy in final[-NY + 1 :]:
        copy.wait_recv()
    sends.finish()


def combine(part):
    count = 31 + 6 * NZ
    cell = (SUB, 128)
    return pl.pallas_call(
        combine_kernel,
        out_shape=jax.ShapeDtypeStruct((NZ, NY) + cell, BF),
        in_specs=[VMEM],
        out_specs=ANY,
        scratch_shapes=[
            pltpu.VMEM((NZ, 2) + cell, BF),
            pltpu.VMEM((NZ, 2) + cell, BF),
            pltpu.VMEM((NZ, NY) + cell, BF),
            pltpu.VMEM((NZ, NY) + cell, BF),
            pltpu.VMEM((NZ, 2) + cell, BF),
            pltpu.VMEM((NZ, 2) + cell, BF),
            pltpu.VMEM((NZ, NY) + cell, BF),
            pltpu.SemaphoreType.DMA((count,)),
            pltpu.SemaphoreType.DMA((count,)),
            pltpu.SemaphoreType.DMA((1,)),
        ],
        compiler_params=pltpu.CompilerParams(
            collective_id=3, has_side_effects=True, vmem_limit_bytes=24 << 20
        ),
        name="combine",
    )(part)


def depthwise(normed, kernel, segments):
    half_width = (kernel.shape[0] - 1) // 2
    count_rows = normed.shape[0]
    padded = jnp.pad(normed, ((half_width, half_width), (0, 0)))
    seg_padded = jnp.pad(segments, (half_width, half_width), constant_values=-1)
    total = jnp.zeros_like(normed)
    for offset in range(kernel.shape[0]):
        window = padded[offset : offset + count_rows]
        same = (seg_padded[offset : offset + count_rows] == segments).astype(normed.dtype)
        total = total + kernel[offset][None, :] * window * same[:, None]
    return total


def swap_cores(values):
    return lax.ppermute(values, "dp", [(d, d ^ 1) for d in range(8)])


def local(frames, lengths, w_qkv, w_out, conv_w, w_router, expert_ids, w_up, w_down):
    core = lax.axis_index("dp") % 2
    offsets = jnp.arange(ROWS, dtype=jnp.int32)
    steps = jnp.arange(4, dtype=jnp.int32)
    ends = jnp.sum(jnp.where(steps[:, None] <= steps[None, :], lengths[0][:, None], 0), axis=0)
    segments = jnp.sum((offsets[:, None] >= ends[None, :]).astype(jnp.int32), axis=1)
    marks = (steps[:, None] == segments[None, :]).astype(BF)
    notes = jnp.concatenate([marks, expert_ids.T.astype(BF)], axis=0)
    notes = jnp.pad(notes, ((0, 16 - 6), (0, D - ROWS)))
    normed_in = normalize(frames.astype(F32)).astype(BF)
    xc = jnp.concatenate([normed_in, notes], axis=0)

    xg, wg, up2, dn2 = gather_all(xc, w_qkv, w_out, w_up, w_down)
    mixed, wo = heads_back(attention(xg, wg), wg)
    mixed = mixed.transpose(1, 0, 2).reshape(ROWS, D)

    first = (
        frames.astype(F32) + jnp.dot(mixed, wo.reshape(D, D), preferred_element_type=F32)
    ).astype(BF)
    conv_in = normalize(first.astype(F32))
    conv_out = depthwise(conv_in, conv_w, segments)
    second = (first.astype(F32) + jax.nn.silu(conv_out)).astype(BF)
    hidden = normalize(second.astype(F32)).astype(BF)

    theirs = swap_cores(hidden)
    both = jnp.stack([jnp.where(core == 0, hidden, theirs), jnp.where(core == 0, theirs, hidden)])
    both = both.reshape(2 * ROWS, D)
    pair = lax.dynamic_slice_in_dim(xg, lax.axis_index("dp") // 2 * 2, 2, axis=0)
    ids = pair[:, ROWS + 4 : ROWS + 6, :ROWS].astype(jnp.int32)
    logits = jnp.dot(both, w_router, preferred_element_type=F32).reshape(2, ROWS, -1)
    experts = jnp.arange(2 * EXPERT_DEVS, dtype=jnp.int32)
    chosen = ids[..., None] == experts
    gates = jax.nn.sigmoid(jnp.sum(jnp.where(chosen, logits[:, None], 0.0), axis=-1))
    flat = chosen.reshape(2, TOP * ROWS, -1).astype(BF)
    order = jnp.arange(TOP * ROWS, dtype=jnp.int32)
    before = (order[None, :] < order[:, None]).astype(BF)
    counts = jnp.einsum("ij,sje->sie", before, flat, preferred_element_type=F32)
    ranks = jnp.sum(counts * flat.astype(F32), axis=-1).astype(jnp.int32)
    ranks = ranks.reshape(2, TOP, ROWS)
    source = jnp.arange(2, dtype=jnp.int32)[:, None, None]
    slots = jnp.where(ids % 2 == core, ids // 2 * CELL + source * CAP + ranks, -1)
    slots = slots.transpose(1, 0, 2).reshape(TOP, 2 * ROWS)
    places = jnp.arange(EXPERT_DEVS * CELL, dtype=jnp.int32)
    hits = slots[:, :, None] == places
    pick = (hits[0] | hits[1]).astype(BF)
    cells = lax.dot_general(
        pick, both, (((0,), (0,)), ((), ())), preferred_element_type=F32
    ).astype(BF)

    routed = dispatch(cells.reshape(NY, NZ, SUB, 128)).reshape(-1, D)
    result = jnp.zeros((routed.shape[0], D), F32)
    for piece in range(2):
        upward = jnp.dot(routed, up2[piece], preferred_element_type=F32)
        activated = jax.nn.silu(upward).astype(BF)
        result = result + jnp.dot(activated, dn2[piece], preferred_element_type=F32)
    part = result.astype(BF).reshape(NX, NZ, NY, SUB, 128)
    returned = combine(part).reshape(NZ, NY, CELL, D).transpose(1, 0, 2, 3).reshape(-1, D)

    given = jnp.zeros((2 * ROWS, D), F32)
    for k in range(TOP):
        picked = jnp.dot(hits[k].astype(BF), returned, preferred_element_type=F32)
        given = given + gates[:, k].reshape(-1, 1) * picked
    given = given.reshape(2, ROWS, D)
    mine = jnp.where(core == 0, given[0], given[1])
    yours = jnp.where(core == 0, given[1], given[0])
    other = swap_cores(yours.astype(BF))
    return (second.astype(F32) + (mine + other.astype(F32))).astype(BF)


def solution(mesh):
    in_specs = (
        P(("dp", "expert"), None),
        P(("dp", "expert"), None),
        P("expert", None),
        P("expert", None),
        P(),
        P(),
        P(("dp", "expert"), None),
        P("expert", None, "dp"),
        P("expert", "dp", None),
    )
    out_specs = P(("dp", "expert"), None)
    return jax.shard_map(local, mesh=mesh, in_specs=in_specs, out_specs=out_specs, check_vma=False)
```

```python
import jax
import jax.numpy as jnp
from jax import lax
from jax.experimental import pallas as pl
from jax.experimental.pallas import tpu as pltpu
from jax.sharding import PartitionSpec as P

HEADS = 16
HEAD_DIM = 64
ROWS = 128
D = 1024
TOP = 2
NX, NY, NZ = 4, 4, 8
EXPERT_DEVS = NY * NZ
CAP = 5
CELL = 2 * CAP
SUB = CELL * D // 128
QCOLS = 384
OCOLS = 512
WCOLS = QCOLS + OCOLS
NOTES = 16
PLACES = EXPERT_DEVS * CELL
MESH = pl.DeviceIdType.MESH
ANY = pl.BlockSpec(memory_space=pl.ANY)
VMEM = pl.BlockSpec(memory_space=pltpu.VMEM)
SMEM = pl.BlockSpec(memory_space=pltpu.SMEM)
BF = jnp.bfloat16
F32 = jnp.float32


def normalize(values):
    mean_value = jnp.mean(values, axis=-1, keepdims=True)
    centred = values - mean_value
    variance = jnp.mean(centred * centred, axis=-1, keepdims=True)
    return centred * lax.rsqrt(variance + 1e-05)


class Place:
    def __init__(self):
        dp, ex = lax.axis_index("dp"), lax.axis_index("expert")
        self.dp, self.ex = dp, ex
        self.x, self.c = dp // 2, dp % 2
        self.y, self.z = ex // NZ, ex % NZ

    def at(self, dx=0, dy=0, dz=0, other=False):
        x, y, z = (self.x + dx + NX) % NX, (self.y + dy + NY) % NY, (self.z + dz + NZ) % NZ
        c = 1 - self.c if other else self.c
        return (x * 2 + c, y * NZ + z)


class Sends:
    def __init__(self, send_sem, recv_sem):
        self.send_sem, self.recv_sem, self.copies = send_sem, recv_sem, []

    def start(self, src, dst, device):
        at = len(self.copies)
        copy = pltpu.make_async_remote_copy(
            src_ref=src,
            dst_ref=dst,
            send_sem=self.send_sem.at[at],
            recv_sem=self.recv_sem.at[at],
            device_id=device,
            device_id_type=MESH,
        )
        copy.start()
        self.copies.append(copy)
        return copy

    def finish(self):
        for copy in self.copies:
            copy.wait_send()


def greet(devices):
    barrier = pltpu.get_barrier_semaphore()
    for device in devices:
        pl.semaphore_signal(barrier, inc=1, device_id=device, device_id_type=MESH)
    pl.semaphore_wait(barrier, len(devices))


def run_tasks(tasks):
    waiting = [(task, next(task, None)) for task in tasks]
    while waiting:
        later = []
        for task, copy in waiting:
            if copy is None:
                continue
            copy.wait_recv()
            later.append((task, next(task, None)))
        waiting = later


GATHER_SENDS = 80


def write_notes(lengths, ids, notes):
    rows = lax.broadcasted_iota(jnp.int32, (8, ROWS), 0)
    lanes = lax.broadcasted_iota(jnp.int32, (8, ROWS), 1)
    marks = jnp.zeros((8, ROWS), F32)
    begin = jnp.int32(0)
    for u in range(4):
        end = begin + lengths[0, u]
        inside = (rows == u) & (lanes >= begin) & (lanes < end)
        marks = jnp.where(inside, 1.0, marks)
        begin = end
    square = (ROWS, ROWS)
    eye = (
        lax.broadcasted_iota(jnp.int32, square, 0) == lax.broadcasted_iota(jnp.int32, square, 1)
    ).astype(BF)
    wide = jnp.zeros((ROWS, 8), jnp.int32)
    column = lax.broadcasted_iota(jnp.int32, (ROWS, 8), 1)
    for k in range(TOP):
        wide = jnp.where(column == 4 + k, ids[:, k : k + 1], wide)
    turned = lax.dot_general(
        wide.astype(F32).astype(BF), eye, (((0,), (0,)), ((), ())), preferred_element_type=F32
    )
    full = jnp.concatenate([marks + turned, jnp.zeros((NOTES - 8, ROWS), F32)], axis=0)
    notes[...] = full.astype(BF)


def gather_kernel(
    frames,
    lengths,
    ids,
    wqkv,
    wout,
    wup,
    wdn,
    xg,
    ng,
    wg,
    up_sib,
    dn_sib,
    xc,
    notes,
    send_sem,
    recv_sem,
    local_sem,
):
    me = Place()
    x, c, y, z, dp = me.x, me.c, me.y, me.z, me.dp
    sib = me.at(other=True)
    xr, xl = me.at(dx=1), me.at(dx=-1)
    yu, yd = me.at(dy=1), me.at(dy=-1)
    zu, zd = me.at(dz=1), me.at(dz=-1)
    locals_ = []

    def local(src, dst):
        copy = pltpu.make_async_copy(src, dst, local_sem.at[len(locals_)])
        copy.start()
        locals_.append(copy)

    for part in range(3):
        columns = pl.ds(pl.multiple_of(part * D + dp * 128, 128), 128)
        local(wqkv.at[:, columns], wg.at[y, z, :, pl.ds(part * 128, 128)])
    local(
        wout.at[:, pl.ds(pl.multiple_of(c * OCOLS, 128), OCOLS)],
        wg.at[y, z, :, pl.ds(QCOLS, OCOLS)],
    )
    others = [((dp + o) % 8, me.ex) for o in range(1, 8)]
    greet(others + [yu, yd, zu, zd])
    sends = Sends(send_sem, recv_sem)
    start = sends.start
    for copy in locals_:
        copy.wait()

    def yy(d):
        return (y + d + NY) % NY

    def zz(d):
        return (z + d + NZ) % NZ

    def x_chain():
        xc[...] = normalize(frames[...].astype(F32)).astype(BF)
        xg[dp] = xc[...]
        first_sib = start(xc, xg.at[dp], sib)
        to_r = start(xc, xg.at[dp], xr)
        to_l = start(xc, xg.at[dp], xl)
        write_notes(lengths, ids, notes)
        ng[dp] = notes[...]
        for device in others:
            noted.append(start(notes, ng.at[dp], device))
        left = xg.at[((x + NX - 1) % NX) * 2 + c]
        right = xg.at[((x + 1) % NX) * 2 + c]
        across = xg.at[((x + 2) % NX) * 2 + c]
        yield to_r
        low = left.at[pl.ds(0, 64)]
        relay_r = start(low, low, xr)
        sib1 = start(left, left, sib)
        yield to_l
        high = right.at[pl.ds(64, 64)]
        relay_l = start(high, high, xl)
        sib2 = start(right, right, sib)
        yield relay_r
        yield relay_l
        sib3 = start(across, across, sib)
        for copy in (first_sib, sib1, sib2, sib3):
            yield copy

    def z_first():
        def block(dy, dz):
            return wg.at[yy(dy), zz(dz), pl.ds(0, 16)]

        spread = []

        def available(dz):
            spread.append(
                (dz, start(block(0, dz), block(0, dz), yu), start(block(0, dz), block(0, dz), yd))
            )

        up = start(block(0, 0), block(0, 0), zu)
        down = start(block(0, 0), block(0, 0), zd)
        available(0)
        for s in range(1, 4):
            yield up
            up = start(block(0, -s), block(0, -s), zu)
            available(-s)
            yield down
            if s < 3:
                down = start(block(0, s), block(0, s), zd)
            available(s)
        yield up
        available(4)
        last = []
        for dz, to_u, to_d in spread:
            yield to_u
            yield to_d
            if dz in (0, 1, 2, 3):
                last.append(start(block(-1, dz), block(-1, dz), yu))
            else:
                last.append(start(block(1, dz), block(1, dz), yd))
        for copy in last:
            yield copy

    def y_first():
        def block(dy):
            return wg.at[yy(dy), z, pl.ds(16, 16)]

        def bundle(dz, first=0, count=NY):
            return wg.at[pl.ds(first, count), zz(dz), pl.ds(16, 16)]

        to_u = start(block(0), block(0), yu)
        to_d = start(block(0), block(0), yd)
        yield to_u
        relay = start(block(-1), block(-1), yu)
        yield to_d
        yield relay
        up = start(bundle(0), bundle(0), zu)
        down = start(bundle(0), bundle(0), zd)
        for s in range(1, 4):
            yield up
            if s < 3:
                up = start(bundle(-s), bundle(-s), zu)
            else:
                up = start(bundle(-s, 0, 2), bundle(-s, 0, 2), zu)
            yield down
            if s < 3:
                down = start(bundle(s), bundle(s), zd)
            else:
                down = start(bundle(s, 2, 2), bundle(s, 2, 2), zd)
        yield up
        yield down

    def swap():
        one = start(wup.at[1 - c], up_sib, sib)
        two = start(wdn.at[1 - c], dn_sib, sib)
        yield from ()
        swaps.extend((one, two))

    swaps, noted = [], []
    run_tasks([y_first(), z_first(), x_chain(), swap()])
    for copy in swaps + noted:
        copy.wait_recv()
    sends.finish()


def gather_all(frames, lengths, ids, w_qkv, w_out, w_up, w_down):
    return pl.pallas_call(
        gather_kernel,
        out_shape=(
            jax.ShapeDtypeStruct((8, ROWS, D), BF),
            jax.ShapeDtypeStruct((8, NOTES, ROWS), BF),
            jax.ShapeDtypeStruct((NY, NZ, 32, WCOLS), BF),
            jax.ShapeDtypeStruct(w_up.shape[1:], BF),
            jax.ShapeDtypeStruct(w_down.shape[1:], BF),
        ),
        in_specs=[VMEM, SMEM, VMEM] + [ANY] * 4,
        out_specs=[VMEM, VMEM, VMEM, ANY, ANY],
        scratch_shapes=[
            pltpu.VMEM((ROWS, D), BF),
            pltpu.VMEM((NOTES, ROWS), BF),
            pltpu.SemaphoreType.DMA((GATHER_SENDS,)),
            pltpu.SemaphoreType.DMA((GATHER_SENDS,)),
            pltpu.SemaphoreType.DMA((8,)),
        ],
        compiler_params=pltpu.CompilerParams(
            collective_id=0, has_side_effects=True, vmem_limit_bytes=24 << 20
        ),
        name="gather",
    )(frames, lengths, ids, w_qkv, w_out, w_up, w_down)


def attention_kernel(x_ref, notes_ref, w_ref, out_ref, qkv_ref):
    w = w_ref[...]
    for half in range(2):
        rows = x_ref[pl.ds(4 * half, 4)].reshape(4 * ROWS, D)
        qkv = jnp.dot(rows, w, preferred_element_type=F32).astype(BF)
        qkv_ref[pl.ds(4 * half, 4)] = qkv.reshape(4, ROWS, QCOLS)
    first_head = lax.broadcasted_iota(jnp.int32, (ROWS, 128), 1) < HEAD_DIM
    for b in range(8):
        marks = notes_ref[b, :4, :].astype(F32)
        same = lax.dot_general(marks, marks, (((0,), (0,)), ((), ())), preferred_element_type=F32)
        allowed = same > 0.5
        q, k, v = (qkv_ref[b, :, pl.ds(128 * i, 128)] for i in range(3))
        mixed = []
        for h in range(2):
            mine = jnp.where(first_head == (h == 0), q, jnp.zeros_like(q))
            scores = lax.dot_general(mine, k, (((1,), (1,)), ((), ())), preferred_element_type=F32)
            scores = jnp.where(allowed, scores * HEAD_DIM ** (-0.5), -1e30)
            highest = jnp.max(scores, axis=-1, keepdims=True)
            expo = jnp.exp(scores - highest)
            probs = (expo / jnp.sum(expo, axis=-1, keepdims=True)).astype(BF)
            mixed.append(jnp.dot(probs, v, preferred_element_type=F32))
        out_ref[b] = jnp.where(first_head, mixed[0], mixed[1]).astype(BF)


def attention(xg, ng, wg):
    return pl.pallas_call(
        attention_kernel,
        grid=(1,),
        out_shape=jax.ShapeDtypeStruct((8, ROWS, 128), BF),
        in_specs=[
            pl.BlockSpec((8, ROWS, D), lambda i: (0, 0, 0)),
            pl.BlockSpec((8, NOTES, ROWS), lambda i: (0, 0, 0)),
            pl.BlockSpec((D, QCOLS), lambda i: (0, 0)),
        ],
        out_specs=pl.BlockSpec((8, ROWS, 128), lambda i: (0, 0, 0)),
        scratch_shapes=[pltpu.VMEM((8, ROWS, QCOLS), BF)],
        compiler_params=pltpu.CompilerParams(vmem_limit_bytes=32 << 20),
        name="attention",
    )(xg, ng, wg.reshape(D, WCOLS))


def heads_kernel(mixed, wg, out, wo, send_sem, recv_sem, local_sem):
    me = Place()
    dp, c = me.dp, me.c
    peers = [((dp + o) % 8, me.ex) for o in range(1, 8)]
    sib = me.at(other=True)
    half = pl.ds(pl.multiple_of(c * OCOLS, 128), OCOLS)
    mine = wg.at[:, :, :, pl.ds(QCOLS, OCOLS)]
    keep = pltpu.make_async_copy(mixed.at[dp], out.at[dp], local_sem.at[0])
    keep.start()
    keep_w = pltpu.make_async_copy(mine, wo.at[:, :, :, half], local_sem.at[1])
    keep_w.start()
    greet(peers)
    sends = Sends(send_sem, recv_sem)
    for o in range(1, 8):
        sends.start(mixed.at[(dp + o) % 8], out.at[dp], peers[o - 1])
    sends.start(mine, wo.at[:, :, :, half], sib)
    for copy in sends.copies:
        copy.wait_recv()
    keep.wait()
    keep_w.wait()
    sends.finish()


def heads_back(mixed, wg):
    return pl.pallas_call(
        heads_kernel,
        out_shape=(
            jax.ShapeDtypeStruct((8, ROWS, 128), BF),
            jax.ShapeDtypeStruct((NY, NZ, 32, D), BF),
        ),
        in_specs=[ANY] * 2,
        out_specs=[VMEM] * 2,
        scratch_shapes=[
            pltpu.SemaphoreType.DMA((8,)),
            pltpu.SemaphoreType.DMA((8,)),
            pltpu.SemaphoreType.DMA((2,)),
        ],
        compiler_params=pltpu.CompilerParams(
            collective_id=1, has_side_effects=True, vmem_limit_bytes=16 << 20
        ),
        name="heads_back",
    )(mixed, wg)


def middle_kernel(
    frames, mixed, wo, notes, conv_w, w_router, ids, second, hidden, gates, hits, shifted, masks
):
    dp = lax.axis_index("dp")
    core = dp % 2
    rows = jnp.concatenate([mixed[b] for b in range(8)], axis=1)
    added = jnp.dot(rows, wo[...], preferred_element_type=F32)
    first = (frames[...].astype(F32) + added).astype(BF).astype(F32)
    conv_in = normalize(first)

    square = (ROWS, ROWS)
    at_row = lax.broadcasted_iota(jnp.int32, square, 0)
    at_lane = lax.broadcasted_iota(jnp.int32, square, 1)
    marks = notes[dp, :4, :].astype(F32)
    same = lax.dot_general(marks, marks, (((0,), (0,)), ((), ())), preferred_element_type=F32)
    begin = jnp.min(jnp.where(same > 0.5, at_lane, ROWS), axis=1, keepdims=True)
    end = jnp.max(jnp.where(same > 0.5, at_lane + 1, 0), axis=1, keepdims=True)
    low = jnp.broadcast_to(begin, square) - at_row + 15
    high = jnp.broadcast_to(end, square) - at_row + 15
    for j in range(31):
        masks[j] = jnp.where((low <= j) & (j < high), 1.0, 0.0)

    edge = jnp.zeros((16, D), F32)
    padded = jnp.concatenate([edge, conv_in, edge], axis=0)
    for s in range(8):
        shifted[s] = padded[s : s + 152]

    def columns(i, carry):
        lanes = pl.ds(pl.multiple_of(i * 128, 128), 128)
        total = jnp.zeros((ROWS, 128), F32)
        for j in range(31):
            window = shifted[(j + 1) % 8, pl.ds((j + 1) // 8 * 8, ROWS), lanes]
            total = total + (conv_w[pl.ds(j, 1), lanes] * window) * masks[j]
        shifted[0, pl.ds(0, ROWS), lanes] = total
        return carry

    lax.fori_loop(0, D // 128, columns, 0)
    conv_out = shifted[0, pl.ds(0, ROWS), :]
    after = (first + conv_out / (1.0 + jnp.exp(-conv_out))).astype(BF)
    second[...] = after
    normed = normalize(after.astype(F32)).astype(BF)
    hidden[...] = normed

    logits = jnp.dot(normed, w_router[...], preferred_element_type=F32)
    expert = lax.broadcasted_iota(jnp.int32, logits.shape, 1)
    for k in range(TOP):
        chosen = jnp.where(ids[:, k : k + 1] == expert, logits, 0.0)
        logit = jnp.sum(chosen, axis=1, keepdims=True)
        gates[:, k : k + 1] = 1.0 / (1.0 + jnp.exp(-logit))

    before = (at_row < at_lane).astype(BF)
    place = lax.broadcasted_iota(jnp.int32, (PLACES, ROWS), 0)
    each = lax.broadcasted_iota(jnp.int32, (2 * EXPERT_DEVS, ROWS), 0)
    for s in range(2):
        names = notes[dp // 2 * 2 + s, 4:8, :].astype(F32).astype(jnp.int32)
        held = jnp.zeros((2 * EXPERT_DEVS, 1), F32)
        for k in range(TOP):
            name = names[k : k + 1]
            one = name == each
            ones = jnp.where(one, 1.0, 0.0)
            earlier = jnp.dot(ones.astype(BF), before, preferred_element_type=F32) + held
            rank = jnp.sum(ones * earlier, axis=0, keepdims=True).astype(jnp.int32)
            held = held + jnp.sum(ones, axis=1, keepdims=True)
            slot = name // 2 * CELL + s * CAP + rank
            slot = jnp.where(name % 2 == core, slot, -1)
            hits[k, :, pl.ds(s * ROWS, ROWS)] = jnp.where(place == slot, 1.0, 0.0).astype(BF)


def middle(frames, mixed, wo, notes, conv_w, w_router, ids):
    return pl.pallas_call(
        middle_kernel,
        out_shape=(
            jax.ShapeDtypeStruct((ROWS, D), BF),
            jax.ShapeDtypeStruct((ROWS, D), BF),
            jax.ShapeDtypeStruct((ROWS, TOP), F32),
            jax.ShapeDtypeStruct((TOP, PLACES, 2 * ROWS), BF),
        ),
        in_specs=[VMEM] * 7,
        out_specs=[VMEM] * 4,
        scratch_shapes=[
            pltpu.VMEM((8, 152, D), F32),
            pltpu.VMEM((31, ROWS, ROWS), F32),
        ],
        compiler_params=pltpu.CompilerParams(vmem_limit_bytes=32 << 20),
        name="middle",
    )(frames, mixed, wo, notes, conv_w, w_router, ids)


PLANE = [(dy, dz) for dz in range(NZ) for dy in range(NY) if (dy, dz) != (0, 0)]


def plane_peers(me):
    return [me.at(dy=dy, dz=dz) for dy, dz in PLANE]


def dispatch_kernel(hidden, hits, out, both, cells, send_sem, recv_sem, local_sem):
    me = Place()
    x, y, z = me.x, me.y, me.z
    xr, xl, sib = me.at(dx=1), me.at(dx=-1), me.at(other=True)
    greet(plane_peers(me) + [xr, xl, sib])
    sends = Sends(send_sem, recv_sem)
    start = sends.start
    theirs = start(hidden, both.at[me.c], sib)
    both[me.c] = hidden[...]
    pick = hits[0] + hits[1]
    theirs.wait_recv()
    rows = jnp.dot(pick, both[...].reshape(2 * ROWS, D), preferred_element_type=F32)
    cells[...] = rows.astype(BF).reshape(PLACES, 8, 128).reshape(NY, NZ, SUB, 128)
    keep = pltpu.make_async_copy(cells.at[y, z], out.at[x, z, y], local_sem.at[0])
    keep.start()
    order = (0, 1, 7, 2, 6, 3, 5, 4)
    direct = {}

    def issue(dz):
        for dy in range(NY):
            if (dy, dz) != (0, 0):
                src = cells.at[(y + dy) % NY, (z + dz) % NZ]
                direct[dy, dz] = start(src, out.at[x, z, y], me.at(dy=dy, dz=dz))

    ahead = 2
    for dz in order[:ahead]:
        issue(dz)
    keep.wait()
    right, left = (x + 1) % NX, (x + NX - 1) % NX
    sideways, last = [], []

    def relay(i):
        group = (z - order[i] + NZ) % NZ
        to_r, to_l = sideways[i]
        to_r.wait_recv()
        low = out.at[left, group, pl.ds(0, 2)]
        last.append(start(low, low, xr))
        to_l.wait_recv()
        high = out.at[right, group, pl.ds(2, 2)]
        last.append(start(high, high, xl))

    for i, dz in enumerate(order):
        if i + ahead < NZ:
            issue(order[i + ahead])
        for dy in range(NY):
            if (dy, dz) != (0, 0):
                direct[dy, dz].wait_recv()
        block = out.at[x, (z - dz + NZ) % NZ]
        sideways.append((start(block, block, xr), start(block, block, xl)))
        if i >= 1:
            relay(i - 1)
    relay(NZ - 1)
    for copy in last:
        copy.wait_recv()
    sends.finish()


def dispatch(hidden, hits):
    count = 32 + 4 * NZ
    return pl.pallas_call(
        dispatch_kernel,
        out_shape=jax.ShapeDtypeStruct((NX, NZ, NY, SUB, 128), BF),
        in_specs=[VMEM, VMEM],
        out_specs=ANY,
        scratch_shapes=[
            pltpu.VMEM((2, ROWS, D), BF),
            pltpu.VMEM((NY, NZ, SUB, 128), BF),
            pltpu.SemaphoreType.DMA((count,)),
            pltpu.SemaphoreType.DMA((count,)),
            pltpu.SemaphoreType.DMA((1,)),
        ],
        compiler_params=pltpu.CompilerParams(
            collective_id=2, has_side_effects=True, vmem_limit_bytes=24 << 20
        ),
        name="dispatch",
    )(hidden, hits)


def expert_kernel(core_ref, x_ref, up_own, dn_own, up_sib, dn_sib, out_ref):
    rows = x_ref[0].reshape(PLACES, 8, 128).reshape(PLACES, D)
    result = None
    for up, down in ((up_own.at[0], dn_own.at[0]), (up_sib, dn_sib)):
        upward = jnp.dot(rows, up[...], preferred_element_type=F32)
        activated = (upward / (1.0 + jnp.exp(-upward))).astype(BF)
        term = jnp.dot(activated, down[...], preferred_element_type=F32)
        result = term if result is None else result + term
    out_ref[0] = result.astype(BF).reshape(PLACES, 8, 128).reshape(PLACES * 8, 128)


def expert(core, routed, w_up, w_down, up_sib, dn_sib):
    block = pl.BlockSpec((1, PLACES * 8, 128), lambda i, c: (i, 0, 0))
    return pl.pallas_call(
        expert_kernel,
        out_shape=jax.ShapeDtypeStruct(routed.shape, BF),
        grid_spec=pltpu.PrefetchScalarGridSpec(
            num_scalar_prefetch=1,
            grid=(NX,),
            in_specs=[
                block,
                pl.BlockSpec((1,) + w_up.shape[1:], lambda i, c: (c[0], 0, 0)),
                pl.BlockSpec((1,) + w_down.shape[1:], lambda i, c: (c[0], 0, 0)),
                pl.BlockSpec(up_sib.shape, lambda i, c: (0, 0)),
                pl.BlockSpec(dn_sib.shape, lambda i, c: (0, 0)),
            ],
            out_specs=block,
        ),
        compiler_params=pltpu.CompilerParams(vmem_limit_bytes=40 << 20),
        name="expert",
    )(core, routed, w_up, w_down, up_sib, dn_sib)


def combine_kernel(
    part,
    hits,
    gates,
    second,
    block_out,
    out,
    rel_r,
    rel_l,
    in_l,
    in_r,
    sum_r,
    sum_l,
    total,
    picked,
    inbox,
    send_sem,
    recv_sem,
    local_sem,
):
    me = Place()
    x, y, z = me.x, me.y, me.z
    xr, xl = me.at(dx=1), me.at(dx=-1)
    right, left, across = (x + 1) % NX, (x + NX - 1) % NX, (x + 2) % NX
    sib = me.at(other=True)
    greet(plane_peers(me) + [xr, xl, sib])
    sends = Sends(send_sem, recv_sem)
    start = sends.start
    order = (4, 3, 5, 2, 6, 1, 7, 0)
    low, high = pl.ds(0, 2), pl.ds(2, 2)
    begun, summed, final = [], [], []

    def begin(i):
        g = (z + order[i]) % NZ
        begun.append(
            (
                start(part.at[across, g, low], rel_r.at[g], xr),
                start(part.at[across, g, high], rel_l.at[g], xl),
                start(part.at[right, g, high], in_l.at[g, high], xr),
                start(part.at[left, g, low], in_r.at[g, low], xl),
            )
        )

    def add(i):
        g = (z + order[i]) % NZ
        begun[i][0].wait_recv()
        sum_r[g] = (part[right, g, low].astype(F32) + rel_r[g].astype(F32)).astype(BF)
        one = start(sum_r.at[g], in_l.at[g, low], xr)
        begun[i][1].wait_recv()
        sum_l[g] = (part[left, g, high].astype(F32) + rel_l[g].astype(F32)).astype(BF)
        two = start(sum_l.at[g], in_r.at[g, high], xl)
        summed.append((one, two))

    def close(i):
        g = (z + order[i]) % NZ
        begun[i][2].wait_recv()
        begun[i][3].wait_recv()
        summed[i][0].wait_recv()
        summed[i][1].wait_recv()
        total[g] = (
            part[x, g].astype(F32) + in_l[g].astype(F32) + in_r[g].astype(F32)
        ).astype(BF)
        for dy in range(NY):
            src = total.at[g, (y + dy) % NY]
            if (dy, order[i]) == (0, 0):
                keep = pltpu.make_async_copy(src, out.at[y, z], local_sem.at[0])
                keep.start()
                final.append(keep)
            else:
                start(src, out.at[y, z], me.at(dy=dy, dz=order[i]))
                final.append(sends.copies[-1])

    ahead = 3
    for i in range(ahead):
        begin(i)
    for i in range(NZ):
        if i + ahead < NZ:
            begin(i + ahead)
        add(i)
        if i >= 1:
            close(i - 1)
    close(NZ - 1)
    for copy in final[:-NY]:
        copy.wait_recv()
    final[-NY].wait()
    for copy in final[-NY + 1 :]:
        copy.wait_recv()

    rows = out[...].reshape(PLACES * 8, 128).reshape(PLACES, 8, 128).reshape(PLACES, D)
    given = []
    for k in range(TOP):
        taken = lax.dot_general(
            hits[k], rows, (((0,), (0,)), ((), ())), preferred_element_type=F32
        )
        picked[k] = taken.astype(BF).reshape(2, ROWS, D)
        given.append(start(picked.at[k, 1 - me.c], inbox.at[k], sib))
    result = second[...].astype(F32)
    for k in range(TOP):
        given[k].wait_recv()
        value = picked[k, me.c].astype(F32) + inbox[k].astype(F32)
        result = result + gates[:, k : k + 1] * value
    block_out[...] = result.astype(BF)
    sends.finish()


def combine(part, hits, gates, second):
    count = 31 + 6 * NZ + TOP
    cell = (SUB, 128)
    return pl.pallas_call(
        combine_kernel,
        out_shape=jax.ShapeDtypeStruct(second.shape, BF),
        in_specs=[VMEM] * 4,
        out_specs=VMEM,
        scratch_shapes=[
            pltpu.VMEM((NY, NZ) + cell, BF),
            pltpu.VMEM((NZ, 2) + cell, BF),
            pltpu.VMEM((NZ, 2) + cell, BF),
            pltpu.VMEM((NZ, NY) + cell, BF),
            pltpu.VMEM((NZ, NY) + cell, BF),
            pltpu.VMEM((NZ, 2) + cell, BF),
            pltpu.VMEM((NZ, 2) + cell, BF),
            pltpu.VMEM((NZ, NY) + cell, BF),
            pltpu.VMEM((TOP, 2, ROWS, D), BF),
            pltpu.VMEM((TOP, ROWS, D), BF),
            pltpu.SemaphoreType.DMA((count,)),
            pltpu.SemaphoreType.DMA((count,)),
            pltpu.SemaphoreType.DMA((1,)),
        ],
        compiler_params=pltpu.CompilerParams(
            collective_id=3, has_side_effects=True, vmem_limit_bytes=32 << 20
        ),
        name="combine",
    )(part, hits, gates, second)


def local(frames, lengths, w_qkv, w_out, conv_w, w_router, expert_ids, w_up, w_down):
    xg, ng, wg, up_sib, dn_sib = gather_all(
        frames, lengths, expert_ids, w_qkv, w_out, w_up, w_down
    )
    mixed, wo = heads_back(attention(xg, ng, wg), wg)
    second, hidden, gates, hits = middle(
        frames, mixed, wo.reshape(D, D), ng, conv_w, w_router, expert_ids
    )
    routed = dispatch(hidden, hits)
    core = (lax.axis_index("dp") % 2).reshape(1)
    part = expert(core, routed.reshape(NX, -1, 128), w_up, w_down, up_sib, dn_sib)
    return combine(part.reshape(routed.shape), hits, gates, second)


def solution(mesh):
    in_specs = (
        P(("dp", "expert"), None),
        P(("dp", "expert"), None),
        P("expert", None),
        P("expert", None),
        P(),
        P(),
        P(("dp", "expert"), None),
        P("expert", None, "dp"),
        P("expert", "dp", None),
    )
    out_specs = P(("dp", "expert"), None)
    return jax.shard_map(local, mesh=mesh, in_specs=in_specs, out_specs=out_specs, check_vma=False)
```

```python
import jax
import jax.numpy as jnp
from jax import lax
from jax.experimental import pallas as pl
from jax.experimental.pallas import tpu as pltpu
from jax.sharding import PartitionSpec as P

HEADS = 16
HEAD_DIM = 64
ROWS = 128
D = 1024
TOP = 2
NX, NY, NZ = 4, 4, 8
EXPERT_DEVS = NY * NZ
CAP = 5
CELL = 2 * CAP
SUB = CELL * D // 128
QCOLS = 384
OCOLS = 512
WCOLS = QCOLS + OCOLS
NOTES = 16
PLACES = EXPERT_DEVS * CELL
MESH = pl.DeviceIdType.MESH
ANY = pl.BlockSpec(memory_space=pltpu.HBM)
VMEM = pl.BlockSpec(memory_space=pltpu.VMEM)
SMEM = pl.BlockSpec(memory_space=pltpu.SMEM)
BF = jnp.bfloat16
F32 = jnp.float32


def normalize(values):
    mean_value = jnp.mean(values, axis=-1, keepdims=True)
    centred = values - mean_value
    variance = jnp.mean(centred * centred, axis=-1, keepdims=True)
    return centred * lax.rsqrt(variance + 1e-05)


class Place:
    def __init__(self):
        dp, ex = lax.axis_index("dp"), lax.axis_index("expert")
        self.dp, self.ex = dp, ex
        self.x, self.c = dp // 2, dp % 2
        self.y, self.z = ex // NZ, ex % NZ

    def at(self, dx=0, dy=0, dz=0, other=False):
        x, y, z = (self.x + dx + NX) % NX, (self.y + dy + NY) % NY, (self.z + dz + NZ) % NZ
        c = 1 - self.c if other else self.c
        return (x * 2 + c, y * NZ + z)


class Sends:
    def __init__(self, send_sem, recv_sem):
        self.send_sem, self.recv_sem, self.copies = send_sem, recv_sem, []

    def start(self, src, dst, device):
        at = len(self.copies)
        copy = pltpu.make_async_remote_copy(
            src_ref=src,
            dst_ref=dst,
            send_sem=self.send_sem.at[at],
            recv_sem=self.recv_sem.at[at],
            device_id=device,
            device_id_type=MESH,
        )
        copy.start()
        self.copies.append(copy)
        return copy

    def finish(self):
        for copy in self.copies:
            copy.wait_send()


def greet(devices):
    barrier = pltpu.get_barrier_semaphore()
    for device in devices:
        pl.semaphore_signal(barrier, inc=1, device_id=device, device_id_type=MESH)
    pl.semaphore_wait(barrier, len(devices))


def run_tasks(tasks):
    waiting = [(task, next(task, None)) for task in tasks]
    while waiting:
        later = []
        for task, copy in waiting:
            if copy is None:
                continue
            copy.wait_recv()
            later.append((task, next(task, None)))
        waiting = later


GATHER_SENDS = 80


def write_notes(lengths, ids, notes):
    rows = lax.broadcasted_iota(jnp.int32, (8, ROWS), 0)
    lanes = lax.broadcasted_iota(jnp.int32, (8, ROWS), 1)
    marks = jnp.zeros((8, ROWS), F32)
    begin = jnp.int32(0)
    for u in range(4):
        end = begin + lengths[0, u]
        inside = (rows == u) & (lanes >= begin) & (lanes < end)
        marks = jnp.where(inside, 1.0, marks)
        begin = end
    square = (ROWS, ROWS)
    eye = (
        lax.broadcasted_iota(jnp.int32, square, 0) == lax.broadcasted_iota(jnp.int32, square, 1)
    ).astype(BF)
    wide = jnp.zeros((ROWS, 8), jnp.int32)
    column = lax.broadcasted_iota(jnp.int32, (ROWS, 8), 1)
    for k in range(TOP):
        wide = jnp.where(column == 4 + k, ids[:, k : k + 1], wide)
    turned = lax.dot_general(
        wide.astype(F32).astype(BF), eye, (((0,), (0,)), ((), ())), preferred_element_type=F32
    )
    full = jnp.concatenate([marks + turned, jnp.zeros((NOTES - 8, ROWS), F32)], axis=0)
    notes[...] = full.astype(BF)


def gather_kernel(
    frames,
    lengths,
    ids,
    wqkv,
    wout,
    wup,
    wdn,
    xg,
    ng,
    wg,
    up_sib,
    dn_sib,
    xc,
    notes,
    send_sem,
    recv_sem,
    local_sem,
):
    me = Place()
    x, c, y, z, dp = me.x, me.c, me.y, me.z, me.dp
    sib = me.at(other=True)
    xr, xl = me.at(dx=1), me.at(dx=-1)
    yu, yd = me.at(dy=1), me.at(dy=-1)
    zu, zd = me.at(dz=1), me.at(dz=-1)
    locals_ = []

    def local(src, dst):
        copy = pltpu.make_async_copy(src, dst, local_sem.at[len(locals_)])
        copy.start()
        locals_.append(copy)

    for part in range(3):
        columns = pl.ds(pl.multiple_of(part * D + dp * 128, 128), 128)
        local(wqkv.at[:, columns], wg.at[y, z, :, pl.ds(part * 128, 128)])
    local(
        wout.at[:, pl.ds(pl.multiple_of(c * OCOLS, 128), OCOLS)],
        wg.at[y, z, :, pl.ds(QCOLS, OCOLS)],
    )
    others = [((dp + o) % 8, me.ex) for o in range(1, 8)]
    greet(others + [yu, yd, zu, zd])
    sends = Sends(send_sem, recv_sem)
    start = sends.start
    for copy in locals_:
        copy.wait()

    def yy(d):
        return (y + d + NY) % NY

    def zz(d):
        return (z + d + NZ) % NZ

    def x_chain():
        xc[...] = normalize(frames[...].astype(F32)).astype(BF)
        xg[dp] = xc[...]
        first_sib = start(xc, xg.at[dp], sib)
        to_r = start(xc, xg.at[dp], xr)
        to_l = start(xc, xg.at[dp], xl)
        write_notes(lengths, ids, notes)
        ng[dp] = notes[...]
        for device in others:
            noted.append(start(notes, ng.at[dp], device))
        left = xg.at[((x + NX - 1) % NX) * 2 + c]
        right = xg.at[((x + 1) % NX) * 2 + c]
        across = xg.at[((x + 2) % NX) * 2 + c]
        yield to_r
        low = left.at[pl.ds(0, 64)]
        relay_r = start(low, low, xr)
        sib1 = start(left, left, sib)
        yield to_l
        high = right.at[pl.ds(64, 64)]
        relay_l = start(high, high, xl)
        sib2 = start(right, right, sib)
        yield relay_r
        yield relay_l
        sib3 = start(across, across, sib)
        for copy in (first_sib, sib1, sib2, sib3):
            yield copy

    def z_first():
        def block(dy, dz):
            return wg.at[yy(dy), zz(dz), pl.ds(0, 16)]

        spread = []

        def available(dz):
            spread.append(
                (dz, start(block(0, dz), block(0, dz), yu), start(block(0, dz), block(0, dz), yd))
            )

        up = start(block(0, 0), block(0, 0), zu)
        down = start(block(0, 0), block(0, 0), zd)
        available(0)
        for s in range(1, 4):
            yield up
            up = start(block(0, -s), block(0, -s), zu)
            available(-s)
            yield down
            if s < 3:
                down = start(block(0, s), block(0, s), zd)
            available(s)
        yield up
        available(4)
        last = []
        for dz, to_u, to_d in spread:
            yield to_u
            yield to_d
            if dz in (0, 1, 2, 3):
                last.append(start(block(-1, dz), block(-1, dz), yu))
            else:
                last.append(start(block(1, dz), block(1, dz), yd))
        for copy in last:
            yield copy

    def y_first():
        def block(dy):
            return wg.at[yy(dy), z, pl.ds(16, 16)]

        def bundle(dz, first=0, count=NY):
            return wg.at[pl.ds(first, count), zz(dz), pl.ds(16, 16)]

        to_u = start(block(0), block(0), yu)
        to_d = start(block(0), block(0), yd)
        yield to_u
        relay = start(block(-1), block(-1), yu)
        yield to_d
        yield relay
        up = start(bundle(0), bundle(0), zu)
        down = start(bundle(0), bundle(0), zd)
        for s in range(1, 4):
            yield up
            if s < 3:
                up = start(bundle(-s), bundle(-s), zu)
            else:
                up = start(bundle(-s, 0, 2), bundle(-s, 0, 2), zu)
            yield down
            if s < 3:
                down = start(bundle(s), bundle(s), zd)
            else:
                down = start(bundle(s, 2, 2), bundle(s, 2, 2), zd)
        yield up
        yield down

    def swap():
        one = start(wup.at[1 - c], up_sib, sib)
        two = start(wdn.at[1 - c], dn_sib, sib)
        yield from ()
        swaps.extend((one, two))

    swaps, noted = [], []
    run_tasks([y_first(), z_first(), x_chain(), swap()])
    for copy in swaps + noted:
        copy.wait_recv()
    sends.finish()


def gather_all(frames, lengths, ids, w_qkv, w_out, w_up, w_down):
    return pl.pallas_call(
        gather_kernel,
        out_shape=(
            jax.ShapeDtypeStruct((8, ROWS, D), BF),
            jax.ShapeDtypeStruct((8, NOTES, ROWS), BF),
            jax.ShapeDtypeStruct((NY, NZ, 32, WCOLS), BF),
            jax.ShapeDtypeStruct(w_up.shape[1:], BF),
            jax.ShapeDtypeStruct(w_down.shape[1:], BF),
        ),
        in_specs=[VMEM, SMEM, VMEM] + [ANY] * 4,
        out_specs=[VMEM, VMEM, VMEM, ANY, ANY],
        scratch_shapes=[
            pltpu.VMEM((ROWS, D), BF),
            pltpu.VMEM((NOTES, ROWS), BF),
            pltpu.SemaphoreType.DMA((GATHER_SENDS,)),
            pltpu.SemaphoreType.DMA((GATHER_SENDS,)),
            pltpu.SemaphoreType.DMA((8,)),
        ],
        compiler_params=pltpu.CompilerParams(
            collective_id=0, has_side_effects=True, vmem_limit_bytes=24 << 20
        ),
        name="gather",
    )(frames, lengths, ids, w_qkv, w_out, w_up, w_down)


def attention_kernel(x_ref, notes_ref, w_ref, out_ref, qkv_ref):
    w = w_ref[...]
    for half in range(2):
        rows = x_ref[pl.ds(4 * half, 4)].reshape(4 * ROWS, D)
        qkv = jnp.dot(rows, w, preferred_element_type=F32).astype(BF)
        qkv_ref[pl.ds(4 * half, 4)] = qkv.reshape(4, ROWS, QCOLS)
    first_head = lax.broadcasted_iota(jnp.int32, (ROWS, 128), 1) < HEAD_DIM
    for b in range(8):
        marks = notes_ref[b, :4, :].astype(F32)
        same = lax.dot_general(marks, marks, (((0,), (0,)), ((), ())), preferred_element_type=F32)
        allowed = same > 0.5
        q, k, v = (qkv_ref[b, :, pl.ds(128 * i, 128)] for i in range(3))
        mixed = []
        for h in range(2):
            mine = jnp.where(first_head == (h == 0), q, jnp.zeros_like(q))
            scores = lax.dot_general(mine, k, (((1,), (1,)), ((), ())), preferred_element_type=F32)
            scores = jnp.where(allowed, scores * HEAD_DIM ** (-0.5), -1e30)
            highest = jnp.max(scores, axis=-1, keepdims=True)
            expo = jnp.exp(scores - highest)
            probs = (expo / jnp.sum(expo, axis=-1, keepdims=True)).astype(BF)
            mixed.append(jnp.dot(probs, v, preferred_element_type=F32))
        out_ref[b] = jnp.where(first_head, mixed[0], mixed[1]).astype(BF)


def attention(xg, ng, wg):
    return pl.pallas_call(
        attention_kernel,
        grid=(1,),
        out_shape=jax.ShapeDtypeStruct((8, ROWS, 128), BF),
        in_specs=[
            pl.BlockSpec((8, ROWS, D), lambda i: (0, 0, 0)),
            pl.BlockSpec((8, NOTES, ROWS), lambda i: (0, 0, 0)),
            pl.BlockSpec((D, QCOLS), lambda i: (0, 0)),
        ],
        out_specs=pl.BlockSpec((8, ROWS, 128), lambda i: (0, 0, 0)),
        scratch_shapes=[pltpu.VMEM((8, ROWS, QCOLS), BF)],
        compiler_params=pltpu.CompilerParams(vmem_limit_bytes=32 << 20),
        name="attention",
    )(xg, ng, wg.reshape(D, WCOLS))


def heads_kernel(mixed, wg, out, wo, send_sem, recv_sem, local_sem):
    me = Place()
    dp, c = me.dp, me.c
    peers = [((dp + o) % 8, me.ex) for o in range(1, 8)]
    sib = me.at(other=True)
    half = pl.ds(pl.multiple_of(c * OCOLS, 128), OCOLS)
    mine = wg.at[:, :, :, pl.ds(QCOLS, OCOLS)]
    keep = pltpu.make_async_copy(mixed.at[dp], out.at[dp], local_sem.at[0])
    keep.start()
    keep_w = pltpu.make_async_copy(mine, wo.at[:, :, :, half], local_sem.at[1])
    keep_w.start()
    greet(peers)
    sends = Sends(send_sem, recv_sem)
    for o in range(1, 8):
        sends.start(mixed.at[(dp + o) % 8], out.at[dp], peers[o - 1])
    sends.start(mine, wo.at[:, :, :, half], sib)
    for copy in sends.copies:
        copy.wait_recv()
    keep.wait()
    keep_w.wait()
    sends.finish()


def heads_back(mixed, wg):
    return pl.pallas_call(
        heads_kernel,
        out_shape=(
            jax.ShapeDtypeStruct((8, ROWS, 128), BF),
            jax.ShapeDtypeStruct((NY, NZ, 32, D), BF),
        ),
        in_specs=[ANY] * 2,
        out_specs=[VMEM] * 2,
        scratch_shapes=[
            pltpu.SemaphoreType.DMA((8,)),
            pltpu.SemaphoreType.DMA((8,)),
            pltpu.SemaphoreType.DMA((2,)),
        ],
        compiler_params=pltpu.CompilerParams(
            collective_id=1, has_side_effects=True, vmem_limit_bytes=16 << 20
        ),
        name="heads_back",
    )(mixed, wg)


def middle_kernel(
    frames, mixed, wo, notes, conv_w, w_router, ids, second, hidden, gates, hits, shifted, masks
):
    dp = lax.axis_index("dp")
    core = dp % 2
    rows = jnp.concatenate([mixed[b] for b in range(8)], axis=1)
    added = jnp.dot(rows, wo[...], preferred_element_type=F32)
    first = (frames[...].astype(F32) + added).astype(BF).astype(F32)
    conv_in = normalize(first)

    square = (ROWS, ROWS)
    at_row = lax.broadcasted_iota(jnp.int32, square, 0)
    at_lane = lax.broadcasted_iota(jnp.int32, square, 1)
    marks = notes[dp, :4, :].astype(F32)
    same = lax.dot_general(marks, marks, (((0,), (0,)), ((), ())), preferred_element_type=F32)
    begin = jnp.min(jnp.where(same > 0.5, at_lane, ROWS), axis=1, keepdims=True)
    end = jnp.max(jnp.where(same > 0.5, at_lane + 1, 0), axis=1, keepdims=True)
    low = jnp.broadcast_to(begin, square) - at_row + 15
    high = jnp.broadcast_to(end, square) - at_row + 15
    for j in range(31):
        masks[j] = jnp.where((low <= j) & (j < high), 1.0, 0.0)

    edge = jnp.zeros((16, D), F32)
    padded = jnp.concatenate([edge, conv_in, edge], axis=0)
    for s in range(8):
        shifted[s] = padded[s : s + 152]

    def columns(i, carry):
        lanes = pl.ds(pl.multiple_of(i * 128, 128), 128)
        total = jnp.zeros((ROWS, 128), F32)
        for j in range(31):
            window = shifted[(j + 1) % 8, pl.ds((j + 1) // 8 * 8, ROWS), lanes]
            total = total + (conv_w[pl.ds(j, 1), lanes] * window) * masks[j]
        shifted[0, pl.ds(0, ROWS), lanes] = total
        return carry

    lax.fori_loop(0, D // 128, columns, 0)
    conv_out = shifted[0, pl.ds(0, ROWS), :]
    after = (first + conv_out / (1.0 + jnp.exp(-conv_out))).astype(BF)
    second[...] = after
    normed = normalize(after.astype(F32)).astype(BF)
    hidden[...] = normed

    logits = jnp.dot(normed, w_router[...], preferred_element_type=F32)
    expert = lax.broadcasted_iota(jnp.int32, logits.shape, 1)
    for k in range(TOP):
        chosen = jnp.where(ids[:, k : k + 1] == expert, logits, 0.0)
        logit = jnp.sum(chosen, axis=1, keepdims=True)
        gates[:, k : k + 1] = 1.0 / (1.0 + jnp.exp(-logit))

    before = (at_row < at_lane).astype(BF)
    place = lax.broadcasted_iota(jnp.int32, (PLACES, ROWS), 0)
    each = lax.broadcasted_iota(jnp.int32, (2 * EXPERT_DEVS, ROWS), 0)
    for s in range(2):
        names = notes[dp // 2 * 2 + s, 4:8, :].astype(F32).astype(jnp.int32)
        held = jnp.zeros((2 * EXPERT_DEVS, 1), F32)
        for k in range(TOP):
            name = names[k : k + 1]
            one = name == each
            ones = jnp.where(one, 1.0, 0.0)
            earlier = jnp.dot(ones.astype(BF), before, preferred_element_type=F32) + held
            rank = jnp.sum(ones * earlier, axis=0, keepdims=True).astype(jnp.int32)
            held = held + jnp.sum(ones, axis=1, keepdims=True)
            slot = name // 2 * CELL + s * CAP + rank
            slot = jnp.where(name % 2 == core, slot, -1)
            hits[k, :, pl.ds(s * ROWS, ROWS)] = jnp.where(place == slot, 1.0, 0.0).astype(BF)


def middle(frames, mixed, wo, notes, conv_w, w_router, ids):
    return pl.pallas_call(
        middle_kernel,
        out_shape=(
            jax.ShapeDtypeStruct((ROWS, D), BF),
            jax.ShapeDtypeStruct((ROWS, D), BF),
            jax.ShapeDtypeStruct((ROWS, TOP), F32),
            jax.ShapeDtypeStruct((TOP, PLACES, 2 * ROWS), BF),
        ),
        in_specs=[VMEM] * 7,
        out_specs=[VMEM] * 4,
        scratch_shapes=[
            pltpu.VMEM((8, 152, D), F32),
            pltpu.VMEM((31, ROWS, ROWS), F32),
        ],
        compiler_params=pltpu.CompilerParams(vmem_limit_bytes=32 << 20),
        name="middle",
    )(frames, mixed, wo, notes, conv_w, w_router, ids)


PLANE = [(dy, dz) for dz in range(NZ) for dy in range(NY) if (dy, dz) != (0, 0)]


def plane_peers(me):
    return [me.at(dy=dy, dz=dz) for dy, dz in PLANE]


ORDER = (0, 1, 7, 2, 6, 3, 5, 4)


def experts_kernel(
    hidden,
    hits,
    gates,
    second,
    wup,
    wdn,
    up_sib,
    dn_sib,
    block_out,
    both,
    cells,
    routed,
    part,
    up_own,
    dn_own,
    back,
    rel_r,
    rel_l,
    in_l,
    in_r,
    sum_r,
    sum_l,
    total,
    picked,
    inbox,
    send_sem,
    recv_sem,
    local_sem,
):
    me = Place()
    x, y, z, c = me.x, me.y, me.z, me.c
    xr, xl, sib = me.at(dx=1), me.at(dx=-1), me.at(other=True)
    right, left, across = (x + 1) % NX, (x + NX - 1) % NX, (x + 2) % NX
    low, high = pl.ds(0, 2), pl.ds(2, 2)
    load_up = pltpu.make_async_copy(wup.at[c], up_own, local_sem.at[0])
    load_up.start()
    load_dn = pltpu.make_async_copy(wdn.at[c], dn_own, local_sem.at[1])
    load_dn.start()
    greet(plane_peers(me) + [xr, xl, sib])
    sends = Sends(send_sem, recv_sem)
    start = sends.start

    theirs = start(hidden, both.at[c], sib)
    both[c] = hidden[...]
    pick = hits[0] + hits[1]
    theirs.wait_recv()
    rows = jnp.dot(pick, both[...].reshape(2 * ROWS, D), preferred_element_type=F32)
    cells[...] = rows.astype(BF).reshape(PLACES, 8, 128).reshape(NY, NZ, SUB, 128)
    keep = pltpu.make_async_copy(cells.at[y, z], routed.at[z, x, y], local_sem.at[2])
    keep.start()

    direct, sideways, relays, begun, summed, final = {}, [], [], [], [], []

    def group(i):
        return (z - ORDER[i] + NZ) % NZ

    def issue(i):
        dz = ORDER[i]
        for dy in range(NY):
            if (dy, dz) != (0, 0):
                src = cells.at[(y + dy) % NY, (z + dz) % NZ]
                direct[dy, dz] = start(src, routed.at[z, x, y], me.at(dy=dy, dz=dz))

    def spread(i):
        for dy in range(NY):
            if (dy, ORDER[i]) == (0, 0):
                keep.wait()
            else:
                direct[dy, ORDER[i]].wait_recv()
        block = routed.at[group(i), x]
        sideways.append((start(block, block, xr), start(block, block, xl)))

    def relay(i):
        g = group(i)
        sideways[i][0].wait_recv()
        one = routed.at[g, left, low]
        to_r = start(one, one, xr)
        sideways[i][1].wait_recv()
        two = routed.at[g, right, high]
        relays.append((to_r, start(two, two, xl)))

    def compute(i):
        g = group(i)
        relays[i][0].wait_recv()
        relays[i][1].wait_recv()
        count = NX * NY * CELL
        rows = routed[g].reshape(count * 8, 128).reshape(count, 8, 128).reshape(count, D)
        result = None
        for up, down in ((up_own, dn_own), (up_sib, dn_sib)):
            upward = jnp.dot(rows, up[...], preferred_element_type=F32)
            activated = (upward / (1.0 + jnp.exp(-upward))).astype(BF)
            term = jnp.dot(activated, down[...], preferred_element_type=F32)
            result = term if result is None else result + term
        part[g] = result.astype(BF).reshape(count, 8, 128).reshape(NX, NY, SUB, 128)
        begun.append(
            (
                start(part.at[g, across, low], rel_r.at[g], xr),
                start(part.at[g, across, high], rel_l.at[g], xl),
                start(part.at[g, right, high], in_l.at[g, high], xr),
                start(part.at[g, left, low], in_r.at[g, low], xl),
            )
        )

    def add(i):
        g = group(i)
        begun[i][0].wait_recv()
        sum_r[g] = (part[g, right, low].astype(F32) + rel_r[g].astype(F32)).astype(BF)
        one = start(sum_r.at[g], in_l.at[g, low], xr)
        begun[i][1].wait_recv()
        sum_l[g] = (part[g, left, high].astype(F32) + rel_l[g].astype(F32)).astype(BF)
        summed.append((one, start(sum_l.at[g], in_r.at[g, high], xl)))

    def close(i):
        g = group(i)
        begun[i][2].wait_recv()
        begun[i][3].wait_recv()
        summed[i][0].wait_recv()
        summed[i][1].wait_recv()
        total[g] = (
            part[g, x].astype(F32) + in_l[g].astype(F32) + in_r[g].astype(F32)
        ).astype(BF)
        for dy in range(NY):
            src = total.at[g, (y + dy) % NY]
            if (dy, ORDER[i]) == (0, 0):
                home = pltpu.make_async_copy(src, back.at[y, z], local_sem.at[3])
                home.start()
                final.append(home.wait)
            else:
                copy = start(src, back.at[y, z], me.at(dy=dy, dz=-ORDER[i]))
                final.append(copy.wait_recv)

    ahead = 2
    for i in range(ahead):
        issue(i)
    for t in range(NZ + 4):
        if t + ahead < NZ:
            issue(t + ahead)
        if t < NZ:
            spread(t)
        if 1 <= t <= NZ:
            relay(t - 1)
        if t == 2:
            load_up.wait()
            load_dn.wait()
        if 2 <= t <= NZ + 1:
            compute(t - 2)
        if 3 <= t <= NZ + 2:
            add(t - 3)
        if 4 <= t:
            close(t - 4)
    for wait in final:
        wait()

    rows = back[...].reshape(PLACES * 8, 128).reshape(PLACES, 8, 128).reshape(PLACES, D)
    given = []
    for k in range(TOP):
        taken = lax.dot_general(
            hits[k], rows, (((0,), (0,)), ((), ())), preferred_element_type=F32
        )
        picked[k] = taken.astype(BF).reshape(2, ROWS, D)
        given.append(start(picked.at[k, 1 - c], inbox.at[k], sib))
    result = second[...].astype(F32)
    for k in range(TOP):
        given[k].wait_recv()
        value = picked[k, c].astype(F32) + inbox[k].astype(F32)
        result = result + gates[:, k : k + 1] * value
    block_out[...] = result.astype(BF)
    sends.finish()


def experts(hidden, hits, gates, second, w_up, w_down, up_sib, dn_sib):
    count = 1 + 31 + 4 * NZ + 6 * NZ + 31 + TOP
    cell = (SUB, 128)
    return pl.pallas_call(
        experts_kernel,
        out_shape=jax.ShapeDtypeStruct(second.shape, BF),
        in_specs=[VMEM] * 4 + [ANY] * 2 + [VMEM] * 2,
        out_specs=VMEM,
        scratch_shapes=[
            pltpu.VMEM((2, ROWS, D), BF),
            pltpu.VMEM((NY, NZ) + cell, BF),
            pltpu.VMEM((NZ, NX, NY) + cell, BF),
            pltpu.VMEM((NZ, NX, NY) + cell, BF),
            pltpu.VMEM(up_sib.shape, BF),
            pltpu.VMEM(dn_sib.shape, BF),
            pltpu.VMEM((NY, NZ) + cell, BF),
            pltpu.VMEM((NZ, 2) + cell, BF),
            pltpu.VMEM((NZ, 2) + cell, BF),
            pltpu.VMEM((NZ, NY) + cell, BF),
            pltpu.VMEM((NZ, NY) + cell, BF),
            pltpu.VMEM((NZ, 2) + cell, BF),
            pltpu.VMEM((NZ, 2) + cell, BF),
            pltpu.VMEM((NZ, NY) + cell, BF),
            pltpu.VMEM((TOP, 2, ROWS, D), BF),
            pltpu.VMEM((TOP, ROWS, D), BF),
            pltpu.SemaphoreType.DMA((count,)),
            pltpu.SemaphoreType.DMA((count,)),
            pltpu.SemaphoreType.DMA((4,)),
        ],
        compiler_params=pltpu.CompilerParams(
            collective_id=2, has_side_effects=True, vmem_limit_bytes=48 << 20
        ),
        name="experts",
    )(hidden, hits, gates, second, w_up, w_down, up_sib, dn_sib)


def local(frames, lengths, w_qkv, w_out, conv_w, w_router, expert_ids, w_up, w_down):
    xg, ng, wg, up_sib, dn_sib = gather_all(
        frames, lengths, expert_ids, w_qkv, w_out, w_up, w_down
    )
    mixed, wo = heads_back(attention(xg, ng, wg), wg)
    second, hidden, gates, hits = middle(
        frames, mixed, wo.reshape(D, D), ng, conv_w, w_router, expert_ids
    )
    return experts(hidden, hits, gates, second, w_up, w_down, up_sib, dn_sib)


def solution(mesh):
    in_specs = (
        P(("dp", "expert"), None),
        P(("dp", "expert"), None),
        P("expert", None),
        P("expert", None),
        P(),
        P(),
        P(("dp", "expert"), None),
        P("expert", None, "dp"),
        P("expert", "dp", None),
    )
    out_specs = P(("dp", "expert"), None)
    return jax.shard_map(local, mesh=mesh, in_specs=in_specs, out_specs=out_specs, check_vma=False)
```

```python
import types

import jax
import jax.numpy as jnp
from jax import lax
from jax.experimental import pallas as pl
from jax.experimental.pallas import tpu as pltpu
from jax.sharding import PartitionSpec as P

HEAD_DIM = 64
ROWS = 128
D = 1024
TOP = 2
NX, NY, NZ = 4, 4, 8
EXPERT_DEVS = NY * NZ
CAP = 5
CELL = 2 * CAP
SUB = CELL * D // 128
QCOLS = 384
OCOLS = 512
NOTES = 16
PLACES = EXPERT_DEVS * CELL
MESH = pl.DeviceIdType.MESH
HBM = pl.BlockSpec(memory_space=pltpu.HBM)
VMEM = pl.BlockSpec(memory_space=pltpu.VMEM)
SMEM = pl.BlockSpec(memory_space=pltpu.SMEM)
BF = jnp.bfloat16
F32 = jnp.float32


def normalize(values):
    mean_value = jnp.mean(values, axis=-1, keepdims=True)
    centred = values - mean_value
    variance = jnp.mean(centred * centred, axis=-1, keepdims=True)
    return centred * lax.rsqrt(variance + 1e-05)


class Place:
    def __init__(self):
        dp, ex = lax.axis_index("dp"), lax.axis_index("expert")
        self.dp, self.ex = dp, ex
        self.x, self.c = dp // 2, dp % 2
        self.y, self.z = ex // NZ, ex % NZ

    def at(self, dx=0, dy=0, dz=0, other=False):
        x, y, z = (self.x + dx + NX) % NX, (self.y + dy + NY) % NY, (self.z + dz + NZ) % NZ
        c = 1 - self.c if other else self.c
        return (x * 2 + c, y * NZ + z)


class Sends:
    def __init__(self, send_sem, recv_sem):
        self.send_sem, self.recv_sem, self.copies = send_sem, recv_sem, []

    def start(self, src, dst, device):
        at = len(self.copies)
        copy = pltpu.make_async_remote_copy(
            src_ref=src,
            dst_ref=dst,
            send_sem=self.send_sem.at[at],
            recv_sem=self.recv_sem.at[at],
            device_id=device,
            device_id_type=MESH,
        )
        copy.start()
        self.copies.append(copy)
        return copy

    def finish(self):
        for copy in self.copies:
            copy.wait_send()


def greet(devices):
    barrier = pltpu.get_barrier_semaphore()
    for device in devices:
        pl.semaphore_signal(barrier, inc=1, device_id=device, device_id_type=MESH)
    pl.semaphore_wait(barrier, len(devices))


def run_tasks(tasks):
    waiting = [(next(task, None), task) for task in tasks]
    waiting = [entry for entry in waiting if entry[0] is not None]
    while waiting:
        first = min(range(len(waiting)), key=lambda n: waiting[n][0][0])
        (_, copy), task = waiting.pop(first)
        if copy is not None:
            copy.wait_recv()
        following = next(task, None)
        if following is not None:
            waiting.append((following, task))


def write_notes(lengths, ids, notes):
    rows = lax.broadcasted_iota(jnp.int32, (8, ROWS), 0)
    lanes = lax.broadcasted_iota(jnp.int32, (8, ROWS), 1)
    marks = jnp.zeros((8, ROWS), F32)
    begin = jnp.int32(0)
    for u in range(4):
        end = begin + lengths[0, u]
        inside = (rows == u) & (lanes >= begin) & (lanes < end)
        marks = jnp.where(inside, 1.0, marks)
        begin = end
    for k in range(TOP):
        marks = jnp.where(rows == 4 + k, ids[k : k + 1, :].astype(F32), marks)
    full = jnp.concatenate([marks, jnp.zeros((NOTES - 8, ROWS), F32)], axis=0)
    notes[...] = full.astype(BF)


def attend(qkv, marks):
    first_head = lax.broadcasted_iota(jnp.int32, (ROWS, 128), 1) < HEAD_DIM
    same = lax.dot_general(marks, marks, (((0,), (0,)), ((), ())), preferred_element_type=F32)
    allowed = same > 0.5
    q, k, v = (qkv[:, 128 * i : 128 * i + 128] for i in range(3))
    mixed = []
    for h in range(2):
        mine = jnp.where(first_head == (h == 0), q, jnp.zeros_like(q))
        scores = lax.dot_general(mine, k, (((1,), (1,)), ((), ())), preferred_element_type=F32)
        scores = jnp.where(allowed, scores * HEAD_DIM ** (-0.5), -1e30)
        highest = jnp.max(scores, axis=-1, keepdims=True)
        expo = jnp.exp(scores - highest)
        probs = (expo / jnp.sum(expo, axis=-1, keepdims=True)).astype(BF)
        mixed.append(jnp.dot(probs, v, preferred_element_type=F32))
    return jnp.where(first_head, mixed[0], mixed[1]).astype(BF)


def middle(
    dp, frames, rows, wo, notes, conv_w, w_router, ids, second, hidden, gates, hits, shifted, masks
):
    core = dp % 2
    added = jnp.dot(rows, wo, preferred_element_type=F32)
    first = (frames[...].astype(F32) + added).astype(BF).astype(F32)
    conv_in = normalize(first)

    square = (ROWS, ROWS)
    at_row = lax.broadcasted_iota(jnp.int32, square, 0)
    at_lane = lax.broadcasted_iota(jnp.int32, square, 1)
    marks = notes[dp, :4, :].astype(F32)
    same = lax.dot_general(marks, marks, (((0,), (0,)), ((), ())), preferred_element_type=F32)
    begin = jnp.min(jnp.where(same > 0.5, at_lane, ROWS), axis=1, keepdims=True)
    end = jnp.max(jnp.where(same > 0.5, at_lane + 1, 0), axis=1, keepdims=True)
    low = jnp.broadcast_to(begin, square) - at_row + 15
    high = jnp.broadcast_to(end, square) - at_row + 15
    for j in range(31):
        masks[j] = jnp.where((low <= j) & (j < high), 1.0, 0.0)

    edge = jnp.zeros((16, D), F32)
    padded = jnp.concatenate([edge, conv_in, edge], axis=0)
    for s in range(8):
        shifted[s] = padded[s : s + 152]

    def columns(i, carry):
        lanes = pl.ds(pl.multiple_of(i * 128, 128), 128)
        total = jnp.zeros((ROWS, 128), F32)
        for j in range(31):
            window = shifted[(j + 1) % 8, pl.ds((j + 1) // 8 * 8, ROWS), lanes]
            total = total + (conv_w[pl.ds(j, 1), lanes] * window) * masks[j]
        shifted[0, pl.ds(0, ROWS), lanes] = total
        return carry

    lax.fori_loop(0, D // 128, columns, 0)
    conv_out = shifted[0, pl.ds(0, ROWS), :]
    after = (first + conv_out / (1.0 + jnp.exp(-conv_out))).astype(BF)
    second[...] = after
    normed = normalize(after.astype(F32)).astype(BF)
    hidden[...] = normed

    logits = lax.dot_general(
        w_router[...], normed, (((1,), (1,)), ((), ())), preferred_element_type=F32
    )
    each = lax.broadcasted_iota(jnp.int32, (2 * EXPERT_DEVS, ROWS), 0)
    for k in range(TOP):
        chosen = jnp.where(ids[k : k + 1, :] == each, logits, 0.0)
        gate = 1.0 / (1.0 + jnp.exp(-jnp.sum(chosen, axis=0, keepdims=True)))
        turned = jnp.where(at_row == at_lane, jnp.broadcast_to(gate, square), 0.0)
        gates[:, k : k + 1] = jnp.sum(turned, axis=1, keepdims=True)

    before = (at_row < at_lane).astype(BF)
    place = lax.broadcasted_iota(jnp.int32, (PLACES, ROWS), 0)
    for s in range(2):
        names = notes[dp // 2 * 2 + s, 4:8, :].astype(F32).astype(jnp.int32)
        held = jnp.zeros((2 * EXPERT_DEVS, 1), F32)
        for k in range(TOP):
            name = names[k : k + 1]
            ones = jnp.where(name == each, 1.0, 0.0)
            earlier = jnp.dot(ones.astype(BF), before, preferred_element_type=F32) + held
            rank = jnp.sum(ones * earlier, axis=0, keepdims=True).astype(jnp.int32)
            held = held + jnp.sum(ones, axis=1, keepdims=True)
            slot = name // 2 * CELL + s * CAP + rank
            slot = jnp.where(name % 2 == core, slot, -1)
            hits[k, :, pl.ds(s * ROWS, ROWS)] = jnp.where(place == slot, 1.0, 0.0).astype(BF)


SCRATCH = dict(
    second=((ROWS, D), BF),
    hidden=((ROWS, D), BF),
    gates=((ROWS, TOP), F32),
    hits=((TOP, PLACES, 2 * ROWS), BF),
    up_sib=((D, 512), BF),
    dn_sib=((512, D), BF),
    up_own=((D, 512), BF),
    dn_own=((512, D), BF),
    xc=((ROWS, D), BF),
    xg=((8, ROWS, D), BF),
    notes=((NOTES, ROWS), BF),
    ng=((8, NOTES, ROWS), BF),
    wq=((NY, NZ, 32, QCOLS), BF),
    wo=((NY, NZ, 32, D), BF),
    mixed=((8, ROWS, 128), BF),
    heads=((8, ROWS, 128), BF),
    shifted=((8, 152, D), F32),
    masks=((31, ROWS, ROWS), F32),
    both=((2, ROWS, D), BF),
    cells=((NY, NZ, SUB, 128), BF),
    routed=((NZ, NX, NY, SUB, 128), BF),
    part=((NZ, NX, NY, SUB, 128), BF),
    back=((NY, NZ, SUB, 128), BF),
    rel_r=((NZ, 2, SUB, 128), BF),
    rel_l=((NZ, 2, SUB, 128), BF),
    in_l=((NZ, NY, SUB, 128), BF),
    in_r=((NZ, NY, SUB, 128), BF),
    sum_r=((NZ, 2, SUB, 128), BF),
    sum_l=((NZ, 2, SUB, 128), BF),
    total=((NZ, NY, SUB, 128), BF),
    picked=((TOP, 2, ROWS, D), BF),
    inbox=((TOP, ROWS, D), BF),
)
COPIES = 256


def block_kernel(
    frames, lengths, ids, conv_w, w_router, wqkv, wout, wup, wdn, block_out, *scratch
):
    send_sem, recv_sem, local_sem = scratch[len(SCRATCH) :]
    ref = types.SimpleNamespace(**dict(zip(SCRATCH, scratch)))
    me = Place()
    sib = me.at(other=True)
    others = [((me.dp + o) % 8, me.ex) for o in range(1, 8)]
    half = pl.ds(pl.multiple_of(me.c * OCOLS, 128), OCOLS)
    loads = [
        (wout.at[:, half], ref.wo.at[me.y, me.z, :, half]),
        (wup.at[me.c], ref.up_own),
        (wdn.at[me.c], ref.dn_own),
    ]
    for part in range(3):
        columns = pl.ds(pl.multiple_of(part * D + me.dp * 128, 128), 128)
        loads.append((wqkv.at[:, columns], ref.wq.at[me.y, me.z, :, pl.ds(part * 128, 128)]))
    loads = [
        pltpu.make_async_copy(src, dst, local_sem.at[n]) for n, (src, dst) in enumerate(loads)
    ]
    for copy in loads:
        copy.start()
    greet(plane_peers(me) + others)
    sends = Sends(send_sem, recv_sem)
    for copy in loads:
        copy.wait()
    front(me, sends, others, frames, lengths, ids, conv_w, w_router, wup, wdn, ref)
    experts(me, sends, block_out, ref, local_sem)
    sends.finish()


def front(me, sends, others, frames, lengths, ids, conv_w, w_router, wup, wdn, ref):
    start = sends.start
    xc, xg, notes, ng, wq, wo = ref.xc, ref.xg, ref.notes, ref.ng, ref.wq, ref.wo
    mixed, heads = ref.mixed, ref.heads
    x, c, y, z, dp = me.x, me.c, me.y, me.z, me.dp
    sib = me.at(other=True)
    xr, xl = me.at(dx=1), me.at(dx=-1)
    yu, yd = me.at(dy=1), me.at(dy=-1)
    zu, zd = me.at(dz=1), me.at(dz=-1)
    half = pl.ds(pl.multiple_of(c * OCOLS, 128), OCOLS)

    def yy(d):
        return (y + d + NY) % NY

    def zz(d):
        return (z + d + NZ) % NZ

    swaps, noted, given, ready = [], [], [], set()

    def out_weights():
        def block(dy):
            return wo.at[yy(dy), z, :, half]

        def bundle(dz, first=0, count=NY):
            return wo.at[pl.ds(first, count), zz(dz), :, half]

        def share(dz):
            given.append(start(bundle(dz), bundle(dz), sib))

        to_u = start(block(0), block(0), yu)
        to_d = start(block(0), block(0), yd)
        yield 1.5, to_u
        over = start(block(-1), block(-1), yu)
        yield 1.5, to_d
        yield 3.0, over
        up = start(bundle(0), bundle(0), zu)
        down = start(bundle(0), bundle(0), zd)
        share(0)
        for s in range(1, 4):
            yield 3.0 + 3.4 * s, up
            if s < 3:
                up = start(bundle(-s), bundle(-s), zu)
            else:
                up = start(bundle(-s, 0, 2), bundle(-s, 0, 2), zu)
            share(-s)
            yield 3.0 + 3.4 * s, down
            if s < 3:
                down = start(bundle(s), bundle(s), zd)
            else:
                down = start(bundle(s, 2, 2), bundle(s, 2, 2), zd)
            share(s)
        yield 15.0, up
        yield 15.0, down
        share(4)

    def qkv_weights():
        def block(dy, dz):
            return wq.at[yy(dy), zz(dz)]

        def available(dz):
            one = block(0, dz)
            spread.append((dz, start(one, one, yu), start(one, one, yd)))

        def pass_on(n, time):
            dz, to_u, to_d = spread[n]
            yield time, to_u
            yield time, to_d
            one = block(-1, dz) if dz in (0, 1, 2, 3) else block(1, dz)
            last.append(start(one, one, yu if dz in (0, 1, 2, 3) else yd))

        spread, last = [], []
        up = start(block(0, 0), block(0, 0), zu)
        down = start(block(0, 0), block(0, 0), zd)
        available(0)
        for s in range(1, 4):
            yield 1.2 * s, up
            up = start(block(0, -s), block(0, -s), zu)
            available(-s)
            yield 1.2 * s, down
            if s < 3:
                down = start(block(0, s), block(0, s), zd)
            available(s)
            yield from pass_on(2 * s - 2, 1.2 * s + 0.1)
            if s > 1:
                yield from pass_on(2 * s - 3, 1.2 * s + 0.1)
        yield 4.8, up
        available(4)
        for n in (5, 6, 7):
            yield from pass_on(n, 5.0 + 0.4 * n)
        for copy in last:
            yield 8.4, copy
        ready.add("w")

    def row_blocks():
        xc[...] = normalize(frames[...].astype(F32)).astype(BF)
        xg[dp] = xc[...]
        low, high = pl.ds(0, 64), pl.ds(64, 64)
        left = xg.at[((x + NX - 1) % NX) * 2 + c]
        right = xg.at[((x + 1) % NX) * 2 + c]
        across = xg.at[((x + 2) % NX) * 2 + c]
        r_low = start(xc.at[low], xg.at[dp, low], xr)
        l_high = start(xc.at[high], xg.at[dp, high], xl)
        to_sib = start(xc, xg.at[dp], sib)
        r_high = start(xc.at[high], xg.at[dp, high], xr)
        l_low = start(xc.at[low], xg.at[dp, low], xl)
        write_notes(lengths, ids, notes)
        ng[dp] = notes[...]
        for device in others:
            noted.append(start(notes, ng.at[dp], device))
        swaps.append(start(wup.at[1 - c], ref.up_sib, sib))
        swaps.append(start(wdn.at[1 - c], ref.dn_sib, sib))
        yield 4.5, r_low
        over_r = start(left.at[low], left.at[low], xr)
        yield 4.5, l_high
        over_l = start(right.at[high], right.at[high], xl)
        yield 8.0, r_high
        left_sib = start(left, left, sib)
        yield 8.0, l_low
        right_sib = start(right, right, sib)
        yield 8.45, to_sib
        for copy in noted:
            yield 8.45, copy
        ready.add(0)
        ready.add(1)
        yield 9.5, over_r
        yield 9.5, over_l
        across_sib = start(across, across, sib)
        yield 10.5, left_sib
        yield 10.5, right_sib
        ready.add(2)
        yield 11.5, across_sib
        ready.add(3)

    def attention():
        pairs = (
            (dp, x * 2 + 1 - c),
            ((x + NX - 1) % NX * 2 + c, (x + 1) % NX * 2 + c),
            ((x + NX - 1) % NX * 2 + 1 - c, (x + 1) % NX * 2 + 1 - c),
            ((x + 2) % NX * 2 + c, (x + 2) % NX * 2 + 1 - c),
        )
        for n, pair in enumerate(pairs):
            yield 8.6 + n, None
            assert "w" in ready and n in ready
            rows = jnp.concatenate([xg[b] for b in pair], axis=0)
            qkv = jnp.dot(rows, wq[...].reshape(D, QCOLS), preferred_element_type=F32).astype(BF)
            for m, b in enumerate(pair):
                marks = ng[b, :4, :].astype(F32)
                result = attend(qkv[m * ROWS : (m + 1) * ROWS], marks)
                if (n, m) == (0, 0):
                    heads[dp] = result
                else:
                    mixed[b] = result
                    back.append(start(mixed.at[b], heads.at[dp], (b, me.ex)))

    back = []
    run_tasks([qkv_weights(), out_weights(), row_blocks(), attention()])
    for copy in given + back + swaps:
        copy.wait_recv()
    rows = jnp.concatenate([heads[b] for b in range(8)], axis=1)
    middle(
        dp,
        frames,
        rows,
        wo[...].reshape(D, D),
        ng,
        conv_w,
        w_router,
        ids,
        ref.second,
        ref.hidden,
        ref.gates,
        ref.hits,
        ref.shifted,
        ref.masks,
    )


PLANE = [(dy, dz) for dz in range(NZ) for dy in range(NY) if (dy, dz) != (0, 0)]


def plane_peers(me):
    return [me.at(dy=dy, dz=dz) for dy, dz in PLANE]


ORDER = (0, 1, 7, 2, 6, 3, 5, 4)


def experts(me, sends, block_out, ref, local_sem):
    start = sends.start
    hidden, hits, gates, second = ref.hidden, ref.hits, ref.gates, ref.second
    both, cells, routed, part, back = ref.both, ref.cells, ref.routed, ref.part, ref.back
    rel_r, rel_l, in_l, in_r = ref.rel_r, ref.rel_l, ref.in_l, ref.in_r
    sum_r, sum_l, total, picked, inbox = ref.sum_r, ref.sum_l, ref.total, ref.picked, ref.inbox
    x, y, z, c = me.x, me.y, me.z, me.c
    xr, xl, sib = me.at(dx=1), me.at(dx=-1), me.at(other=True)
    right, left, across = (x + 1) % NX, (x + NX - 1) % NX, (x + 2) % NX
    low, high = pl.ds(0, 2), pl.ds(2, 2)

    theirs = start(hidden, both.at[c], sib)
    both[c] = hidden[...]
    pick = hits[0] + hits[1]
    theirs.wait_recv()
    rows = jnp.dot(pick, both[...].reshape(2 * ROWS, D), preferred_element_type=F32)
    cells[...] = rows.astype(BF).reshape(PLACES, 8, 128).reshape(NY, NZ, SUB, 128)
    keep = pltpu.make_async_copy(cells.at[y, z], routed.at[z, x, y], local_sem.at[6])
    keep.start()

    direct, sideways, relays, begun, summed, final = {}, [], [], [], [], []

    def group(i):
        return (z - ORDER[i] + NZ) % NZ

    def issue(i):
        dz = ORDER[i]
        for dy in range(NY):
            if (dy, dz) != (0, 0):
                src = cells.at[(y + dy) % NY, (z + dz) % NZ]
                direct[dy, dz] = start(src, routed.at[z, x, y], me.at(dy=dy, dz=dz))

    def spread(i):
        for dy in range(NY):
            if (dy, ORDER[i]) == (0, 0):
                keep.wait()
            else:
                direct[dy, ORDER[i]].wait_recv()
        block = routed.at[group(i), x]
        sideways.append((start(block, block, xr), start(block, block, xl)))

    def relay(i):
        g = group(i)
        sideways[i][0].wait_recv()
        one = routed.at[g, left, low]
        to_r = start(one, one, xr)
        sideways[i][1].wait_recv()
        two = routed.at[g, right, high]
        relays.append((to_r, start(two, two, xl)))

    def compute(i):
        g = group(i)
        relays[i][0].wait_recv()
        relays[i][1].wait_recv()
        count = NX * NY * CELL
        rows = routed[g].reshape(count * 8, 128).reshape(count, 8, 128).reshape(count, D)
        result = None
        for up, down in ((ref.up_own, ref.dn_own), (ref.up_sib, ref.dn_sib)):
            upward = jnp.dot(rows, up[...], preferred_element_type=F32)
            activated = (upward / (1.0 + jnp.exp(-upward))).astype(BF)
            term = jnp.dot(activated, down[...], preferred_element_type=F32)
            result = term if result is None else result + term
        part[g] = result.astype(BF).reshape(count, 8, 128).reshape(NX, NY, SUB, 128)
        begun.append(
            (
                start(part.at[g, across, low], rel_r.at[g], xr),
                start(part.at[g, across, high], rel_l.at[g], xl),
                start(part.at[g, right, high], in_l.at[g, high], xr),
                start(part.at[g, left, low], in_r.at[g, low], xl),
            )
        )

    def add(i):
        g = group(i)
        begun[i][0].wait_recv()
        sum_r[g] = (part[g, right, low].astype(F32) + rel_r[g].astype(F32)).astype(BF)
        one = start(sum_r.at[g], in_l.at[g, low], xr)
        begun[i][1].wait_recv()
        sum_l[g] = (part[g, left, high].astype(F32) + rel_l[g].astype(F32)).astype(BF)
        summed.append((one, start(sum_l.at[g], in_r.at[g, high], xl)))

    def close(i):
        g = group(i)
        begun[i][2].wait_recv()
        begun[i][3].wait_recv()
        summed[i][0].wait_recv()
        summed[i][1].wait_recv()
        total[g] = (
            part[g, x].astype(F32) + in_l[g].astype(F32) + in_r[g].astype(F32)
        ).astype(BF)
        for dy in range(NY):
            src = total.at[g, (y + dy) % NY]
            if (dy, ORDER[i]) == (0, 0):
                home = pltpu.make_async_copy(src, back.at[y, z], local_sem.at[7])
                home.start()
                final.append(home.wait)
            else:
                copy = start(src, back.at[y, z], me.at(dy=dy, dz=-ORDER[i]))
                final.append(copy.wait_recv)

    ahead = 2
    for i in range(ahead):
        issue(i)
    for t in range(NZ + 4):
        if t + ahead < NZ:
            issue(t + ahead)
        if t < NZ:
            spread(t)
        if 1 <= t <= NZ:
            relay(t - 1)
        if 2 <= t <= NZ + 1:
            compute(t - 2)
        if 3 <= t <= NZ + 2:
            add(t - 3)
        if 4 <= t:
            close(t - 4)
    for wait in final:
        wait()

    rows = back[...].reshape(PLACES * 8, 128).reshape(PLACES, 8, 128).reshape(PLACES, D)
    given = []
    for k in range(TOP):
        taken = lax.dot_general(
            hits[k], rows, (((0,), (0,)), ((), ())), preferred_element_type=F32
        )
        picked[k] = taken.astype(BF).reshape(2, ROWS, D)
        given.append(start(picked.at[k, 1 - c], inbox.at[k], sib))
    result = second[...].astype(F32)
    for k in range(TOP):
        given[k].wait_recv()
        value = picked[k, c].astype(F32) + inbox[k].astype(F32)
        result = result + gates[:, k : k + 1] * value
    block_out[...] = result


def local(frames, lengths, w_qkv, w_out, conv_w, w_router, expert_ids, w_up, w_down):
    result = pl.pallas_call(
        block_kernel,
        out_shape=jax.ShapeDtypeStruct((ROWS, D), F32),
        in_specs=[VMEM, SMEM, VMEM, VMEM, VMEM] + [HBM] * 4,
        out_specs=VMEM,
        scratch_shapes=[pltpu.VMEM(*shape) for shape in SCRATCH.values()]
        + [
            pltpu.SemaphoreType.DMA((COPIES,)),
            pltpu.SemaphoreType.DMA((COPIES,)),
            pltpu.SemaphoreType.DMA((8,)),
        ],
        compiler_params=pltpu.CompilerParams(
            collective_id=0, has_side_effects=True, vmem_limit_bytes=60 << 20
        ),
        name="block",
    )(frames, lengths, expert_ids.T, conv_w, w_router.T, w_qkv, w_out, w_up, w_down)
    return result.astype(BF)


def solution(mesh):
    in_specs = (
        P(("dp", "expert"), None),
        P(("dp", "expert"), None),
        P("expert", None),
        P("expert", None),
        P(),
        P(),
        P(("dp", "expert"), None),
        P("expert", None, "dp"),
        P("expert", "dp", None),
    )
    out_specs = P(("dp", "expert"), None)
    return jax.shard_map(local, mesh=mesh, in_specs=in_specs, out_specs=out_specs, check_vma=False)
```

```python
import math
import types

import jax
import jax.numpy as jnp
from jax import lax
from jax.experimental import pallas as pl
from jax.experimental.pallas import tpu as pltpu
from jax.sharding import PartitionSpec as P

HEAD_DIM = 64
ROWS = 128
D = 1024
TOP = 2
NX, NY, NZ = 4, 4, 8
EXPERT_DEVS = NY * NZ
CAP = 5
CELL = 2 * CAP
SUB = CELL * D // 128
QCOLS = 384
OCOLS = 512
NOTES = 16
PLACES = EXPERT_DEVS * CELL
MESH = pl.DeviceIdType.MESH
HBM = pl.BlockSpec(memory_space=pltpu.HBM)
VMEM = pl.BlockSpec(memory_space=pltpu.VMEM)
SMEM = pl.BlockSpec(memory_space=pltpu.SMEM)
BF = jnp.bfloat16
F32 = jnp.float32


def normalize(values):
    mean_value = jnp.mean(values, axis=-1, keepdims=True)
    centred = values - mean_value
    variance = jnp.mean(centred * centred, axis=-1, keepdims=True)
    return centred * lax.rsqrt(variance + 1e-05)


class Place:
    def __init__(self):
        dp, ex = lax.axis_index("dp"), lax.axis_index("expert")
        self.dp, self.ex = dp, ex
        self.x, self.c = dp // 2, dp % 2
        self.y, self.z = ex // NZ, ex % NZ

    def at(self, dx=0, dy=0, dz=0, other=False):
        x, y, z = (self.x + dx + NX) % NX, (self.y + dy + NY) % NY, (self.z + dz + NZ) % NZ
        c = 1 - self.c if other else self.c
        return (x * 2 + c, y * NZ + z)


class Sends:
    def __init__(self, send_sem, recv_sem, ruler):
        self.send_sem, self.recv_sem, self.ruler = send_sem, recv_sem, ruler
        self.slots, self.sent = 0, [0]

    def slot(self):
        self.slots += 1
        assert self.slots <= self.recv_sem.shape[0]
        return self.slots - 1

    def start(self, src, dst, device, slot=None):
        slot = self.slot() if slot is None else slot
        length = math.prod(src.shape) // 128
        if self.sent[-1] + length > self.ruler.shape[0]:
            self.sent.append(0)
        self.sent[-1] += length
        copy = pltpu.make_async_remote_copy(
            src_ref=src,
            dst_ref=dst,
            send_sem=self.send_sem.at[len(self.sent) - 1],
            recv_sem=self.recv_sem.at[slot],
            device_id=device,
            device_id_type=MESH,
        )
        copy.start()
        return copy

    def measure(self, length, sem):
        piece = self.ruler.at[pl.ds(0, length)]
        pltpu.make_async_copy(piece, piece, sem).wait()

    def arrive(self, slot, length):
        self.measure(length, self.recv_sem.at[slot])

    def finish(self):
        for n, length in enumerate(self.sent):
            self.measure(length, self.send_sem.at[n])


def greet(devices):
    barrier = pltpu.get_barrier_semaphore()
    for device in devices:
        pl.semaphore_signal(barrier, inc=1, device_id=device, device_id_type=MESH)
    pl.semaphore_wait(barrier, len(devices))


def run_tasks(tasks):
    waiting = [(next(task, None), task) for task in tasks]
    waiting = [entry for entry in waiting if entry[0] is not None]
    while waiting:
        first = min(range(len(waiting)), key=lambda n: waiting[n][0][0])
        (_, copy), task = waiting.pop(first)
        if copy is not None:
            copy.wait_recv()
        following = next(task, None)
        if following is not None:
            waiting.append((following, task))


def write_notes(lengths, ids, notes):
    rows = lax.broadcasted_iota(jnp.int32, (8, ROWS), 0)
    lanes = lax.broadcasted_iota(jnp.int32, (8, ROWS), 1)
    marks = jnp.zeros((8, ROWS), F32)
    begin = jnp.int32(0)
    for u in range(4):
        end = begin + lengths[0, u]
        inside = (rows == u) & (lanes >= begin) & (lanes < end)
        marks = jnp.where(inside, 1.0, marks)
        begin = end
    for k in range(TOP):
        marks = jnp.where(rows == 4 + k, ids[k : k + 1, :].astype(F32), marks)
    full = jnp.concatenate([marks, jnp.zeros((NOTES - 8, ROWS), F32)], axis=0)
    notes[...] = full.astype(BF)


def attend(qkv, marks):
    first_head = lax.broadcasted_iota(jnp.int32, (ROWS, 128), 1) < HEAD_DIM
    same = lax.dot_general(marks, marks, (((0,), (0,)), ((), ())), preferred_element_type=F32)
    allowed = same > 0.5
    q, k, v = (qkv[:, 128 * i : 128 * i + 128] for i in range(3))
    mixed = []
    for h in range(2):
        mine = jnp.where(first_head == (h == 0), q, jnp.zeros_like(q))
        scores = lax.dot_general(mine, k, (((1,), (1,)), ((), ())), preferred_element_type=F32)
        scores = jnp.where(allowed, scores * HEAD_DIM ** (-0.5), -1e30)
        highest = jnp.max(scores, axis=-1, keepdims=True)
        expo = jnp.exp(scores - highest)
        probs = (expo / jnp.sum(expo, axis=-1, keepdims=True)).astype(BF)
        mixed.append(jnp.dot(probs, v, preferred_element_type=F32))
    return jnp.where(first_head, mixed[0], mixed[1]).astype(BF)


def plan(dp, notes, hits, masks):
    core = dp % 2
    each = lax.broadcasted_iota(jnp.int32, (2 * EXPERT_DEVS, ROWS), 0)
    square = (ROWS, ROWS)
    at_row = lax.broadcasted_iota(jnp.int32, square, 0)
    at_lane = lax.broadcasted_iota(jnp.int32, square, 1)
    marks = notes[dp, :4, :].astype(F32)
    same = lax.dot_general(marks, marks, (((0,), (0,)), ((), ())), preferred_element_type=F32)
    begin = jnp.min(jnp.where(same > 0.5, at_lane, ROWS), axis=1, keepdims=True)
    end = jnp.max(jnp.where(same > 0.5, at_lane + 1, 0), axis=1, keepdims=True)
    low = jnp.broadcast_to(begin, square) - at_row + 15
    high = jnp.broadcast_to(end, square) - at_row + 15
    for j in range(31):
        masks[j] = jnp.where((low <= j) & (j < high), 1.0, 0.0)

    before = (at_row < at_lane).astype(BF)
    place = lax.broadcasted_iota(jnp.int32, (PLACES, ROWS), 0)
    for s in range(2):
        names = notes[dp // 2 * 2 + s, 4:8, :].astype(F32).astype(jnp.int32)
        held = jnp.zeros((2 * EXPERT_DEVS, 1), F32)
        for k in range(TOP):
            name = names[k : k + 1]
            ones = jnp.where(name == each, 1.0, 0.0)
            earlier = jnp.dot(ones.astype(BF), before, preferred_element_type=F32) + held
            rank = jnp.sum(ones * earlier, axis=0, keepdims=True).astype(jnp.int32)
            held = held + jnp.sum(ones, axis=1, keepdims=True)
            slot = name // 2 * CELL + s * CAP + rank
            slot = jnp.where(name % 2 == core, slot, -1)
            hits[k, :, pl.ds(s * ROWS, ROWS)] = jnp.where(place == slot, 1.0, 0.0).astype(BF)


def middle(
    frames, rows, wo, conv_w, w_router, ids, second, hidden, gates, shifted, masks
):
    square = (ROWS, ROWS)
    at_row = lax.broadcasted_iota(jnp.int32, square, 0)
    at_lane = lax.broadcasted_iota(jnp.int32, square, 1)
    halves = [
        jnp.dot(rows, wo[n].reshape(D, OCOLS), preferred_element_type=F32) for n in range(2)
    ]
    added = jnp.concatenate(halves, axis=1)
    first = (frames[...].astype(F32) + added).astype(BF).astype(F32)
    conv_in = normalize(first)

    edge = jnp.zeros((16, D), F32)
    padded = jnp.concatenate([edge, conv_in, edge], axis=0)
    for s in range(8):
        shifted[s] = padded[s : s + 152]

    def columns(i, carry):
        lanes = pl.ds(pl.multiple_of(i * 128, 128), 128)
        total = jnp.zeros((ROWS, 128), F32)
        for j in range(31):
            window = shifted[(j + 1) % 8, pl.ds((j + 1) // 8 * 8, ROWS), lanes]
            total = total + (conv_w[pl.ds(j, 1), lanes] * window) * masks[j]
        shifted[0, pl.ds(0, ROWS), lanes] = total
        return carry

    lax.fori_loop(0, D // 128, columns, 0)
    conv_out = shifted[0, pl.ds(0, ROWS), :]
    after = (first + conv_out / (1.0 + jnp.exp(-conv_out))).astype(BF)
    second[...] = after
    normed = normalize(after.astype(F32)).astype(BF)
    hidden[...] = normed

    logits = lax.dot_general(
        w_router[...], normed, (((1,), (1,)), ((), ())), preferred_element_type=F32
    )
    each = lax.broadcasted_iota(jnp.int32, (2 * EXPERT_DEVS, ROWS), 0)
    for k in range(TOP):
        chosen = jnp.where(ids[k : k + 1, :] == each, logits, 0.0)
        gate = 1.0 / (1.0 + jnp.exp(-jnp.sum(chosen, axis=0, keepdims=True)))
        turned = jnp.where(at_row == at_lane, jnp.broadcast_to(gate, square), 0.0)
        gates[:, k : k + 1] = jnp.sum(turned, axis=1, keepdims=True)


SCRATCH = dict(
    second=((ROWS, D), BF),
    hidden=((ROWS, D), BF),
    gates=((ROWS, TOP), F32),
    hits=((TOP, PLACES, 2 * ROWS), BF),
    up_sib=((D, 512), BF),
    dn_sib=((512, D), BF),
    up_own=((D, 512), BF),
    dn_own=((512, D), BF),
    xc=((ROWS, D), BF),
    xg=((8, ROWS, D), BF),
    notes=((NOTES, ROWS), BF),
    ng=((8, NOTES, ROWS), BF),
    wq=((NY, NZ, 32, QCOLS), BF),
    wo=((2, NY, NZ, 32, OCOLS), BF),
    mixed=((8, ROWS, 128), BF),
    heads=((8, ROWS, 128), BF),
    shifted=((8, 152, D), F32),
    masks=((31, ROWS, ROWS), F32),
    both=((2, ROWS, D), BF),
    cells=((NY, NZ, SUB, 128), BF),
    routed=((NZ, NX, NY, SUB, 128), BF),
    part=((NZ, NX, NY, SUB, 128), BF),
    back=((NY, NZ, SUB, 128), BF),
    rel_r=((NZ, 2, SUB, 128), BF),
    rel_l=((NZ, 2, SUB, 128), BF),
    in_l=((NZ, NY, SUB, 128), BF),
    in_r=((NZ, NY, SUB, 128), BF),
    sum_r=((NZ, 2, SUB, 128), BF),
    sum_l=((NZ, 2, SUB, 128), BF),
    total=((NZ, NY, SUB, 128), BF),
    picked=((TOP, 2, ROWS, D), BF),
    inbox=((TOP, ROWS, D), BF),
    ruler=((20480, 128), BF),
)
SEND_SLOTS, RECV_SLOTS = 3, 121


def block_kernel(
    frames, lengths, ids, conv_w, w_router, wqkv, wout, wup, wdn, block_out, *scratch
):
    send_sem, recv_sem, local_sem = scratch[len(SCRATCH) :]
    ref = types.SimpleNamespace(**dict(zip(SCRATCH, scratch)))
    me = Place()
    sib = me.at(other=True)
    others = [((me.dp + o) % 8, me.ex) for o in range(1, 8)]
    half = pl.ds(pl.multiple_of(me.c * OCOLS, 128), OCOLS)
    loads = [
        (wout.at[:, half], ref.wo.at[me.c, me.y, me.z]),
        (wup.at[me.c], ref.up_own),
        (wdn.at[me.c], ref.dn_own),
    ]
    for part in range(3):
        columns = pl.ds(pl.multiple_of(part * D + me.dp * 128, 128), 128)
        loads.append((wqkv.at[:, columns], ref.wq.at[me.y, me.z, :, pl.ds(part * 128, 128)]))
    loads = [
        pltpu.make_async_copy(src, dst, local_sem.at[n]) for n, (src, dst) in enumerate(loads)
    ]
    for copy in loads:
        copy.start()
    greet(plane_peers(me) + others)
    sends = Sends(send_sem, recv_sem, ref.ruler)
    for copy in loads[:1] + loads[3:]:
        copy.wait()
    front(me, sends, others, frames, lengths, ids, conv_w, w_router, wup, wdn, ref)
    for copy in loads[1:3]:
        copy.wait()
    experts(me, sends, block_out, ref, local_sem)
    sends.finish()


def front(me, sends, others, frames, lengths, ids, conv_w, w_router, wup, wdn, ref):
    start = sends.start
    xc, xg, notes, ng, wq, wo = ref.xc, ref.xg, ref.notes, ref.ng, ref.wq, ref.wo
    mixed, heads = ref.mixed, ref.heads
    x, c, y, z, dp = me.x, me.c, me.y, me.z, me.dp
    sib = me.at(other=True)
    xr, xl = me.at(dx=1), me.at(dx=-1)
    yu, yd = me.at(dy=1), me.at(dy=-1)
    zu, zd = me.at(dz=1), me.at(dz=-1)
    def yy(d):
        return (y + d + NY) % NY

    def zz(d):
        return (z + d + NZ) % NZ

    swaps, noted, given, heard, ready = *(sends.slot() for _ in range(4)), set()

    def out_weights():
        def block(dy, dz):
            return wo.at[c, yy(dy), zz(dz)]

        def share(dy, dz):
            start(block(dy, dz), block(dy, dz), sib, given)

        def along_z(dy, time):
            up = start(block(dy, 0), block(dy, 0), zu)
            down = start(block(dy, 0), block(dy, 0), zd)
            share(dy, 0)
            for s in range(1, 4):
                yield time + 2.6 * s, up
                if s < 3 or dy in (0, 2):
                    up = start(block(dy, -s), block(dy, -s), zu)
                share(dy, -s)
                yield time + 2.6 * s + 0.1, down
                if s < 3 or dy in (1, -1):
                    down = start(block(dy, s), block(dy, s), zd)
                share(dy, s)
            yield time + 10.4, up if dy in (0, 2) else down
            share(dy, 4)

        def from_above():
            yield 1.9, to_d
            yield from along_z(1, 2.0)

        def from_across():
            yield 2.0, None
            yield 4.1, overs[0]
            yield from along_z(2, 4.2)

        to_u = start(block(0, 0), block(0, 0), yu)
        to_d = start(block(0, 0), block(0, 0), yd)
        overs = []

        def from_below():
            yield 1.9, to_u
            overs.append(start(block(-1, 0), block(-1, 0), yu))
            yield from along_z(-1, 2.0)

        return [along_z(0, 0.0), from_below(), from_above(), from_across()]

    def qkv_weights():
        def block(dy, dz):
            return wq.at[yy(dy), zz(dz)]

        def available(dz):
            one, slot = block(0, dz), sends.slot()
            start(one, one, yu, slot)
            start(one, one, yd, slot)
            spread.append((dz, slot))

        def pass_on(n, time):
            dz, slot = spread[n]
            yield time, None
            sends.arrive(slot, 2 * 32 * QCOLS // 128)
            one = block(-1, dz) if dz in (0, 1, 2, -3) else block(1, dz)
            start(one, one, yu if dz in (0, 1, 2, -3) else yd, last)

        spread, last = [], sends.slot()
        order = (1, -1, 2, -2, 3, -3, 4)
        direct = [
            start(block(0, 0), block(0, 0), me.at(dz=dz)) for dz in order
        ]
        available(0)
        for n, dz in enumerate(order):
            yield 2.0 + 0.5 * n, direct[n]
            available(-dz)
            if n >= 3:
                yield from pass_on(n - 3, 2.1 + 0.5 * n)
        for n in range(4, 8):
            yield from pass_on(n, 4.2 + 0.6 * n)
        yield 10.2, None
        sends.arrive(last, NZ * 32 * QCOLS // 128)
        ready.add("w")

    def row_blocks():
        xc[...] = normalize(frames[...].astype(F32)).astype(BF)
        xg[dp] = xc[...]
        low, high = pl.ds(0, 64), pl.ds(64, 64)
        left = xg.at[((x + NX - 1) % NX) * 2 + c]
        right = xg.at[((x + 1) % NX) * 2 + c]
        across = xg.at[((x + 2) % NX) * 2 + c]
        r_low = start(xc.at[low], xg.at[dp, low], xr)
        l_high = start(xc.at[high], xg.at[dp, high], xl)
        to_sib = start(xc, xg.at[dp], sib)
        r_high = start(xc.at[high], xg.at[dp, high], xr)
        l_low = start(xc.at[low], xg.at[dp, low], xl)
        write_notes(lengths, ids, notes)
        ng[dp] = notes[...]
        for device in others:
            start(notes, ng.at[dp], device, noted)
        start(wup.at[1 - c], ref.up_sib, sib, swaps)
        start(wdn.at[1 - c], ref.dn_sib, sib, swaps)
        yield 5.5, r_low
        over_r = start(left.at[low], left.at[low], xr)
        yield 5.5, l_high
        over_l = start(right.at[high], right.at[high], xl)
        yield 8.5, r_high
        left_sib = start(left, left, sib)
        yield 8.5, l_low
        right_sib = start(right, right, sib)
        yield 8.6, to_sib
        yield 8.6, None
        sends.arrive(noted, 7 * NOTES)
        ready.add(0)
        ready.add(1)
        plan(dp, ng, ref.hits, ref.masks)
        yield 10.0, over_r
        yield 10.0, over_l
        across_sib = start(across, across, sib)
        yield 10.5, left_sib
        yield 10.5, right_sib
        ready.add(2)
        yield 12.0, across_sib
        ready.add(3)

    def attention():
        pairs = (
            (dp, x * 2 + 1 - c),
            ((x + NX - 1) % NX * 2 + c, (x + 1) % NX * 2 + c),
            ((x + NX - 1) % NX * 2 + 1 - c, (x + 1) % NX * 2 + 1 - c),
            ((x + 2) % NX * 2 + c, (x + 2) % NX * 2 + 1 - c),
        )
        for n, pair in enumerate(pairs):
            yield 10.3 + n, None
            assert "w" in ready and n in ready
            rows = jnp.concatenate([xg[b] for b in pair], axis=0)
            qkv = jnp.dot(rows, wq[...].reshape(D, QCOLS), preferred_element_type=F32).astype(BF)
            for m, b in enumerate(pair):
                marks = ng[b, :4, :].astype(F32)
                result = attend(qkv[m * ROWS : (m + 1) * ROWS], marks)
                if (n, m) == (0, 0):
                    heads[dp] = result
                else:
                    mixed[b] = result
                    start(mixed.at[b], heads.at[dp], (b, me.ex), heard)

    run_tasks([qkv_weights(), *out_weights(), row_blocks(), attention()])
    sends.arrive(given, D * OCOLS // 128)
    sends.arrive(heard, 7 * ROWS)
    sends.arrive(swaps, 2 * D * 512 // 128)
    rows = jnp.concatenate([heads[b] for b in range(8)], axis=1)
    middle(
        frames,
        rows,
        wo,
        conv_w,
        w_router,
        ids,
        ref.second,
        ref.hidden,
        ref.gates,
        ref.shifted,
        ref.masks,
    )


PLANE = [(dy, dz) for dz in range(NZ) for dy in range(NY) if (dy, dz) != (0, 0)]


def plane_peers(me):
    return [me.at(dy=dy, dz=dz) for dy, dz in PLANE]


ORDER = (0, 2, 6, 4, 3, 5, 1, 7)


def experts(me, sends, block_out, ref, local_sem):
    start = sends.start
    hidden, hits, gates, second = ref.hidden, ref.hits, ref.gates, ref.second
    both, cells, routed, part, back = ref.both, ref.cells, ref.routed, ref.part, ref.back
    rel_r, rel_l, in_l, in_r = ref.rel_r, ref.rel_l, ref.in_l, ref.in_r
    sum_r, sum_l, total, picked, inbox = ref.sum_r, ref.sum_l, ref.total, ref.picked, ref.inbox
    x, y, z, c = me.x, me.y, me.z, me.c
    xr, xl, sib = me.at(dx=1), me.at(dx=-1), me.at(other=True)
    right, left, across = (x + 1) % NX, (x + NX - 1) % NX, (x + 2) % NX
    low, high = pl.ds(0, 2), pl.ds(2, 2)

    theirs = start(hidden, both.at[c], sib)
    both[c] = hidden[...]
    pick = hits[0] + hits[1]
    theirs.wait_recv()
    rows = jnp.dot(pick, both[...].reshape(2 * ROWS, D), preferred_element_type=F32)
    cells[...] = rows.astype(BF).reshape(PLACES, 8, 128).reshape(NY, NZ, SUB, 128)
    keep = pltpu.make_async_copy(cells.at[y, z], routed.at[z, x, y], local_sem.at[6])
    keep.start()

    direct, sideways, relays, begun, closing = [], [], [], [], []
    returned = sends.slot()

    def group(i):
        return (z - ORDER[i] + NZ) % NZ

    def issue(i):
        dz = ORDER[i]
        direct.append(sends.slot())
        for dy in range(NY):
            if (dy, dz) != (0, 0):
                src = cells.at[(y + dy) % NY, (z + dz) % NZ]
                start(src, routed.at[z, x, y], me.at(dy=dy, dz=dz), direct[i])

    def spread(i):
        if ORDER[i] == 0:
            keep.wait()
        sends.arrive(direct[i], (NY - (ORDER[i] == 0)) * SUB)
        block = routed.at[group(i), x]
        sideways.append((start(block, block, xr), start(block, block, xl)))

    def relay(i):
        g = group(i)
        relays.append(sends.slot())
        sideways[i][0].wait_recv()
        one = routed.at[g, left, low]
        start(one, one, xr, relays[i])
        sideways[i][1].wait_recv()
        two = routed.at[g, right, high]
        start(two, two, xl, relays[i])

    def compute(i):
        g = group(i)
        sends.arrive(relays[i], NY * SUB)
        count = NX * NY * CELL
        rows = routed[g].reshape(count * 8, 128).reshape(count, 8, 128).reshape(count, D)
        result = None
        for up, down in ((ref.up_own, ref.dn_own), (ref.up_sib, ref.dn_sib)):
            upward = jnp.dot(rows, up[...], preferred_element_type=F32)
            activated = (upward / (1.0 + jnp.exp(-upward))).astype(BF)
            term = jnp.dot(activated, down[...], preferred_element_type=F32)
            result = term if result is None else result + term
        part[g] = result.astype(BF).reshape(count, 8, 128).reshape(NX, NY, SUB, 128)
        begun.append(
            (
                start(part.at[g, across, low], rel_r.at[g], xr),
                start(part.at[g, across, high], rel_l.at[g], xl),
            )
        )
        closing.append(sends.slot())
        start(part.at[g, right, high], in_l.at[g, high], xr, closing[i])
        start(part.at[g, left, low], in_r.at[g, low], xl, closing[i])

    def add(i):
        g = group(i)
        begun[i][0].wait_recv()
        sum_r[g] = (part[g, right, low].astype(F32) + rel_r[g].astype(F32)).astype(BF)
        start(sum_r.at[g], in_l.at[g, low], xr, closing[i])
        begun[i][1].wait_recv()
        sum_l[g] = (part[g, left, high].astype(F32) + rel_l[g].astype(F32)).astype(BF)
        start(sum_l.at[g], in_r.at[g, high], xl, closing[i])

    def close(i):
        g = group(i)
        sends.arrive(closing[i], 2 * NY * SUB)
        total[g] = (
            part[g, x].astype(F32) + in_l[g].astype(F32) + in_r[g].astype(F32)
        ).astype(BF)
        for dy in range(NY):
            src = total.at[g, (y + dy) % NY]
            if (dy, ORDER[i]) == (0, 0):
                back[y, z] = total[g, y]
            else:
                start(src, back.at[y, z], me.at(dy=dy, dz=-ORDER[i]), returned)

    ahead = 2
    for i in range(ahead):
        issue(i)
    for t in range(NZ + 4):
        if t + ahead < NZ:
            issue(t + ahead)
        if t < NZ:
            spread(t)
        if 1 <= t <= NZ:
            relay(t - 1)
        if 2 <= t <= NZ + 1:
            compute(t - 2)
        if 3 <= t <= NZ + 2:
            add(t - 3)
        if 4 <= t:
            close(t - 4)
    sends.arrive(returned, (NY * NZ - 1) * SUB)

    rows = back[...].reshape(PLACES * 8, 128).reshape(PLACES, 8, 128).reshape(PLACES, D)
    given = []
    for k in range(TOP):
        taken = lax.dot_general(
            hits[k], rows, (((0,), (0,)), ((), ())), preferred_element_type=F32
        )
        picked[k] = taken.astype(BF).reshape(2, ROWS, D)
        given.append(start(picked.at[k, 1 - c], inbox.at[k], sib))
    result = second[...].astype(F32)
    for k in range(TOP):
        given[k].wait_recv()
        value = picked[k, c].astype(F32) + inbox[k].astype(F32)
        result = result + gates[:, k : k + 1] * value
    block_out[...] = result


def local(frames, lengths, w_qkv, w_out, conv_w, w_router, expert_ids, w_up, w_down):
    result = pl.pallas_call(
        block_kernel,
        out_shape=jax.ShapeDtypeStruct((ROWS, D), F32),
        in_specs=[VMEM, SMEM, VMEM, VMEM, VMEM] + [HBM] * 4,
        out_specs=VMEM,
        scratch_shapes=[pltpu.VMEM(*shape) for shape in SCRATCH.values()]
        + [
            pltpu.SemaphoreType.DMA((SEND_SLOTS,)),
            pltpu.SemaphoreType.DMA((RECV_SLOTS,)),
            pltpu.SemaphoreType.DMA((8,)),
        ],
        compiler_params=pltpu.CompilerParams(
            collective_id=0, has_side_effects=True, vmem_limit_bytes=60 << 20
        ),
        name="block",
    )(frames, lengths, expert_ids.T, conv_w, w_router.T, w_qkv, w_out, w_up, w_down)
    return result.astype(BF)


def solution(mesh):
    in_specs = (
        P(("dp", "expert"), None),
        P(("dp", "expert"), None),
        P("expert", None),
        P("expert", None),
        P(),
        P(),
        P(("dp", "expert"), None),
        P("expert", None, "dp"),
        P("expert", "dp", None),
    )
    out_specs = P(("dp", "expert"), None)
    return jax.shard_map(local, mesh=mesh, in_specs=in_specs, out_specs=out_specs, check_vma=False)
```

```python
import math
import types

import jax
import jax.numpy as jnp
from jax import lax
from jax.experimental import pallas as pl
from jax.experimental.pallas import tpu as pltpu
from jax.sharding import PartitionSpec as P

HEAD_DIM = 64
ROWS = 128
D = 1024
TOP = 2
NX, NY, NZ = 4, 4, 8
EXPERT_DEVS = NY * NZ
CAP = 5
CELL = 2 * CAP
SUB = CELL * D // 128
QCOLS = 384
OCOLS = 512
NOTES = 16
PLACES = EXPERT_DEVS * CELL
MESH = pl.DeviceIdType.MESH
HBM = pl.BlockSpec(memory_space=pltpu.HBM)
VMEM = pl.BlockSpec(memory_space=pltpu.VMEM)
SMEM = pl.BlockSpec(memory_space=pltpu.SMEM)
BF = jnp.bfloat16
F32 = jnp.float32


def normalize(values):
    mean_value = jnp.mean(values, axis=-1, keepdims=True)
    centred = values - mean_value
    variance = jnp.mean(centred * centred, axis=-1, keepdims=True)
    return centred * lax.rsqrt(variance + 1e-05)


class Place:
    def __init__(self):
        dp, ex = lax.axis_index("dp"), lax.axis_index("expert")
        self.dp, self.ex = dp, ex
        self.x, self.c = dp // 2, dp % 2
        self.y, self.z = ex // NZ, ex % NZ

    def at(self, dx=0, dy=0, dz=0, other=False):
        x, y, z = (self.x + dx + NX) % NX, (self.y + dy + NY) % NY, (self.z + dz + NZ) % NZ
        c = 1 - self.c if other else self.c
        return (x * 2 + c, y * NZ + z)


class Sends:
    def __init__(self, send_sem, recv_sem, ruler):
        self.send_sem, self.recv_sem, self.ruler = send_sem, recv_sem, ruler
        self.slots, self.sent = 0, [0]

    def slot(self):
        self.slots += 1
        assert self.slots <= self.recv_sem.shape[0]
        return self.slots - 1

    def start(self, src, dst, device, slot=None):
        slot = self.slot() if slot is None else slot
        length = math.prod(src.shape) // 128
        if self.sent[-1] + length > self.ruler.shape[0]:
            self.sent.append(0)
        self.sent[-1] += length
        copy = pltpu.make_async_remote_copy(
            src_ref=src,
            dst_ref=dst,
            send_sem=self.send_sem.at[len(self.sent) - 1],
            recv_sem=self.recv_sem.at[slot],
            device_id=device,
            device_id_type=MESH,
        )
        copy.start()
        return copy

    def measure(self, length, sem):
        piece = self.ruler.at[pl.ds(0, length)]
        pltpu.make_async_copy(piece, piece, sem).wait()

    def arrive(self, slot, length):
        self.measure(length, self.recv_sem.at[slot])

    def finish(self):
        for n, length in enumerate(self.sent):
            self.measure(length, self.send_sem.at[n])


def greet(devices):
    barrier = pltpu.get_barrier_semaphore()
    for device in devices:
        pl.semaphore_signal(barrier, inc=1, device_id=device, device_id_type=MESH)
    pl.semaphore_wait(barrier, len(devices))


def run_tasks(tasks):
    waiting = [(next(task, None), task) for task in tasks]
    waiting = [entry for entry in waiting if entry[0] is not None]
    while waiting:
        first = min(range(len(waiting)), key=lambda n: waiting[n][0][0])
        (_, copy), task = waiting.pop(first)
        if copy is not None:
            copy.wait_recv()
        following = next(task, None)
        if following is not None:
            waiting.append((following, task))


def write_notes(lengths, ids, notes):
    rows = lax.broadcasted_iota(jnp.int32, (8, ROWS), 0)
    lanes = lax.broadcasted_iota(jnp.int32, (8, ROWS), 1)
    marks = jnp.zeros((8, ROWS), F32)
    begin = jnp.int32(0)
    for u in range(4):
        end = begin + lengths[0, u]
        inside = (rows == u) & (lanes >= begin) & (lanes < end)
        marks = jnp.where(inside, 1.0, marks)
        begin = end
    for k in range(TOP):
        marks = jnp.where(rows == 4 + k, ids[k : k + 1, :].astype(F32), marks)
    full = jnp.concatenate([marks, jnp.zeros((NOTES - 8, ROWS), F32)], axis=0)
    notes[...] = full.astype(BF)


def attend(qkv, marks):
    first_head = lax.broadcasted_iota(jnp.int32, (ROWS, 128), 1) < HEAD_DIM
    same = lax.dot_general(marks, marks, (((0,), (0,)), ((), ())), preferred_element_type=F32)
    allowed = same > 0.5
    q, k, v = (qkv[:, 128 * i : 128 * i + 128] for i in range(3))
    q = q * jnp.asarray(HEAD_DIM ** (-0.5), BF)
    mixed = []
    for h in range(2):
        own = first_head == (h == 0)
        scores = lax.dot_general(
            jnp.where(own, q, jnp.zeros_like(q)),
            k,
            (((1,), (1,)), ((), ())),
            preferred_element_type=F32,
        )
        scores = jnp.where(allowed, scores, -1e30)
        expo = jnp.exp(scores - jnp.max(scores, axis=-1, keepdims=True)).astype(BF)
        mixed.append(
            jnp.dot(expo, jnp.where(own, v, jnp.ones_like(v)), preferred_element_type=F32)
        )
    sums = jnp.where(first_head, mixed[1], mixed[0])
    return (jnp.where(first_head, mixed[0], mixed[1]) / pltpu.roll(sums, 64, 1)).astype(BF)


def plan(dp, notes, hits, masks):
    core = dp % 2
    each = lax.broadcasted_iota(jnp.int32, (2 * EXPERT_DEVS, ROWS), 0)
    square = (ROWS, ROWS)
    at_row = lax.broadcasted_iota(jnp.int32, square, 0)
    at_lane = lax.broadcasted_iota(jnp.int32, square, 1)
    marks = notes[dp, :4, :].astype(F32)
    same = lax.dot_general(marks, marks, (((0,), (0,)), ((), ())), preferred_element_type=F32)
    begin = jnp.min(jnp.where(same > 0.5, at_lane, ROWS), axis=1, keepdims=True)
    end = jnp.max(jnp.where(same > 0.5, at_lane + 1, 0), axis=1, keepdims=True)
    low = jnp.broadcast_to(begin, square) - at_row + 15
    high = jnp.broadcast_to(end, square) - at_row + 15
    for j in range(31):
        masks[j] = jnp.where((low <= j) & (j < high), 1.0, 0.0)

    before = (at_row < at_lane).astype(BF)
    place = lax.broadcasted_iota(jnp.int32, (PLACES, ROWS), 0)
    for s in range(2):
        names = notes[dp // 2 * 2 + s, 4:8, :].astype(F32).astype(jnp.int32)
        held = jnp.zeros((2 * EXPERT_DEVS, 1), F32)
        for k in range(TOP):
            name = names[k : k + 1]
            ones = jnp.where(name == each, 1.0, 0.0)
            earlier = jnp.dot(ones.astype(BF), before, preferred_element_type=F32) + held
            rank = jnp.sum(ones * earlier, axis=0, keepdims=True).astype(jnp.int32)
            held = held + jnp.sum(ones, axis=1, keepdims=True)
            slot = name // 2 * CELL + s * CAP + rank
            slot = jnp.where(name % 2 == core, slot, -1)
            hits[k, :, pl.ds(s * ROWS, ROWS)] = jnp.where(place == slot, 1.0, 0.0).astype(BF)


def middle(
    frames, rows, wo, conv_w, w_router, ids, second, hidden, gates, shifted, masks
):
    square = (ROWS, ROWS)
    at_row = lax.broadcasted_iota(jnp.int32, square, 0)
    at_lane = lax.broadcasted_iota(jnp.int32, square, 1)
    halves = [
        jnp.dot(rows, wo[n].reshape(D, OCOLS), preferred_element_type=F32) for n in range(2)
    ]
    added = jnp.concatenate(halves, axis=1)
    first = (frames[...].astype(F32) + added).astype(BF).astype(F32)
    conv_in = normalize(first)

    edge = jnp.zeros((16, D), F32)
    padded = jnp.concatenate([edge, conv_in, edge], axis=0)
    for s in range(8):
        shifted[s] = padded[s : s + 152]

    def columns(i, carry):
        lanes = pl.ds(pl.multiple_of(i * 128, 128), 128)
        total = jnp.zeros((ROWS, 128), F32)
        for j in range(31):
            window = shifted[(j + 1) % 8, pl.ds((j + 1) // 8 * 8, ROWS), lanes]
            total = total + (conv_w[pl.ds(j, 1), lanes] * window) * masks[j]
        shifted[0, pl.ds(0, ROWS), lanes] = total
        return carry

    lax.fori_loop(0, D // 128, columns, 0)
    conv_out = shifted[0, pl.ds(0, ROWS), :]
    after = (first + conv_out / (1.0 + jnp.exp(-conv_out))).astype(BF)
    second[...] = after
    normed = normalize(after.astype(F32)).astype(BF)
    hidden[...] = normed

    logits = lax.dot_general(
        w_router[...], normed, (((1,), (1,)), ((), ())), preferred_element_type=F32
    )
    each = lax.broadcasted_iota(jnp.int32, (2 * EXPERT_DEVS, ROWS), 0)
    for k in range(TOP):
        chosen = jnp.where(ids[k : k + 1, :] == each, logits, 0.0)
        gate = 1.0 / (1.0 + jnp.exp(-jnp.sum(chosen, axis=0, keepdims=True)))
        turned = jnp.where(at_row == at_lane, jnp.broadcast_to(gate, square), 0.0)
        gates[:, k : k + 1] = jnp.sum(turned, axis=1, keepdims=True)


SCRATCH = dict(
    frames=((ROWS, D), BF),
    conv_w=((31, D), F32),
    w_router=((2 * EXPERT_DEVS, D), BF),
    second=((ROWS, D), BF),
    hidden=((ROWS, D), BF),
    gates=((ROWS, TOP), F32),
    hits=((TOP, PLACES, 2 * ROWS), BF),
    up_sib=((D, 512), BF),
    dn_sib=((512, D), BF),
    up_own=((D, 512), BF),
    dn_own=((512, D), BF),
    xc=((ROWS, D), BF),
    xg=((8, ROWS, D), BF),
    notes=((NOTES, ROWS), BF),
    ng=((8, NOTES, ROWS), BF),
    wq=((NY, NZ, 32, QCOLS), BF),
    wo=((2, NY, NZ, 32, OCOLS), BF),
    mixed=((8, ROWS, 128), BF),
    heads=((8, ROWS, 128), BF),
    shifted=((8, 152, D), F32),
    masks=((31, ROWS, ROWS), F32),
    both=((2, ROWS, D), BF),
    cells=((NY, NZ, SUB, 128), BF),
    routed=((NZ, NX, NY, SUB, 128), BF),
    part=((NZ, NX, NY, SUB, 128), BF),
    back=((NY, NZ, SUB, 128), BF),
    rel_r=((NZ, 2, SUB, 128), BF),
    rel_l=((NZ, 2, SUB, 128), BF),
    in_l=((NZ, NY, SUB, 128), BF),
    in_r=((NZ, NY, SUB, 128), BF),
    sum_r=((NZ, 2, SUB, 128), BF),
    sum_l=((NZ, 2, SUB, 128), BF),
    total=((NZ, NY, SUB, 128), BF),
    picked=((TOP, 2, ROWS, D), BF),
    inbox=((TOP, ROWS, D), BF),
    ruler=((20480, 128), BF),
)
SEND_SLOTS, RECV_SLOTS = 3, 119


def block_kernel(
    lengths, ids, frames, conv_w, w_router, wqkv, wout, wup, wdn, block_out, *scratch
):
    send_sem, recv_sem, local_sem = scratch[len(SCRATCH) :]
    ref = types.SimpleNamespace(**dict(zip(SCRATCH, scratch)))
    me = Place()
    sib = me.at(other=True)
    others = [((me.dp + o) % 8, me.ex) for o in range(1, 8)]
    half = pl.ds(pl.multiple_of(me.c * OCOLS, 128), OCOLS)
    loads = [
        (frames, ref.frames),
        (wout.at[:, half], ref.wo.at[me.c, me.y, me.z]),
        (wup.at[me.c], ref.up_own),
        (wdn.at[me.c], ref.dn_own),
        (conv_w, ref.conv_w),
        (w_router, ref.w_router),
    ]
    for part in range(3):
        columns = pl.ds(pl.multiple_of(part * D + me.dp * 128, 128), 128)
        loads.append((wqkv.at[:, columns], ref.wq.at[me.y, me.z, :, pl.ds(part * 128, 128)]))
    loads = [
        pltpu.make_async_copy(src, dst, local_sem.at[n]) for n, (src, dst) in enumerate(loads)
    ]
    for copy in loads:
        copy.start()
    greet(plane_peers(me) + others)
    sends = Sends(send_sem, recv_sem, ref.ruler)
    for copy in loads[1:2] + loads[6:]:
        copy.wait()
    front(me, sends, others, loads, lengths, ids, wup, wdn, ref)
    for copy in loads[2:4]:
        copy.wait()
    experts(me, sends, block_out, ref, local_sem)
    sends.finish()


def front(me, sends, others, loads, lengths, ids, wup, wdn, ref):
    start = sends.start
    xc, xg, notes, ng, wq, wo = ref.xc, ref.xg, ref.notes, ref.ng, ref.wq, ref.wo
    mixed, heads = ref.mixed, ref.heads
    x, c, y, z, dp = me.x, me.c, me.y, me.z, me.dp
    sib = me.at(other=True)
    xr, xl = me.at(dx=1), me.at(dx=-1)
    yu, yd = me.at(dy=1), me.at(dy=-1)
    zu, zd = me.at(dz=1), me.at(dz=-1)
    def yy(d):
        return (y + d + NY) % NY

    def zz(d):
        return (z + d + NZ) % NZ

    swaps, noted, given, heard, ready = *(sends.slot() for _ in range(4)), set()

    def out_weights():
        def block(dy, dz):
            return wo.at[c, yy(dy), zz(dz)]

        def share(dy, dz):
            start(block(dy, dz), block(dy, dz), sib, given)

        def along_z(dy, time):
            up = start(block(dy, 0), block(dy, 0), zu)
            down = start(block(dy, 0), block(dy, 0), zd)
            share(dy, 0)
            for s in range(1, 4):
                yield time + 2.6 * s, up
                if s < 3 or dy in (0, 2):
                    up = start(block(dy, -s), block(dy, -s), zu)
                share(dy, -s)
                yield time + 2.6 * s + 0.1, down
                if s < 3 or dy in (1, -1):
                    down = start(block(dy, s), block(dy, s), zd)
                share(dy, s)
            yield time + 10.4, up if dy in (0, 2) else down
            share(dy, 4)

        def from_above():
            yield 1.9, to_d
            yield from along_z(1, 2.0)

        def from_across():
            yield 2.4, over
            yield from along_z(2, 2.5)

        to_u = start(block(0, 0), block(0, 0), yu)
        to_d = start(block(0, 0), block(0, 0), yd)
        over = start(block(0, 0), block(0, 0), me.at(dy=2))

        def from_below():
            yield 1.9, to_u
            yield from along_z(-1, 2.0)

        return [along_z(0, 0.0), from_below(), from_above(), from_across()]

    def qkv_weights():
        def block(dy, dz):
            return wq.at[yy(dy), zz(dz)]

        def available(dz):
            one, slot = block(0, dz), sends.slot()
            start(one, one, yu, slot)
            start(one, one, yd, slot)
            if len(spread) >= 5:
                start(one, one, me.at(dy=2), last)
            spread.append((dz, slot))

        def pass_on(n, time):
            dz, slot = spread[n]
            yield time, None
            sends.arrive(slot, 2 * 32 * QCOLS // 128)
            if n >= 5:
                return
            one = block(-1, dz) if dz in (0, 1, 2, -3) else block(1, dz)
            start(one, one, yu if dz in (0, 1, 2, -3) else yd, last)

        spread, last = [], sends.slot()
        order = (1, -1, 2, -2, 3, -3, 4)
        direct = [
            start(block(0, 0), block(0, 0), me.at(dz=dz)) for dz in order
        ]
        available(0)
        for n, dz in enumerate(order):
            yield 2.0 + 0.5 * n, direct[n]
            available(-dz)
            if n >= 3:
                yield from pass_on(n - 3, 2.1 + 0.5 * n)
        for n in range(4, 8):
            yield from pass_on(n, 4.6 + 0.5 * n)
        yield 8.8, None
        sends.arrive(last, NZ * 32 * QCOLS // 128)
        ready.add("w")

    def row_blocks():
        loads[0].wait()
        xc[...] = normalize(ref.frames[...].astype(F32)).astype(BF)
        xg[dp] = xc[...]
        low, high = pl.ds(0, 64), pl.ds(64, 64)
        left = xg.at[((x + NX - 1) % NX) * 2 + c]
        right = xg.at[((x + 1) % NX) * 2 + c]
        across = xg.at[((x + 2) % NX) * 2 + c]
        r_low = start(xc.at[low], xg.at[dp, low], xr)
        l_high = start(xc.at[high], xg.at[dp, high], xl)
        to_sib = start(xc, xg.at[dp], sib)
        r_high = start(xc.at[high], xg.at[dp, high], xr)
        l_low = start(xc.at[low], xg.at[dp, low], xl)
        write_notes(lengths, ids, notes)
        ng[dp] = notes[...]
        for device in others:
            start(notes, ng.at[dp], device, noted)
        start(wup.at[1 - c], ref.up_sib, sib, swaps)
        start(wdn.at[1 - c], ref.dn_sib, sib, swaps)
        yield 5.5, r_low
        over_r = start(left.at[low], left.at[low], xr)
        yield 5.5, l_high
        over_l = start(right.at[high], right.at[high], xl)
        yield 8.5, r_high
        left_sib = start(left, left, sib)
        yield 8.5, l_low
        right_sib = start(right, right, sib)
        yield 8.6, to_sib
        yield 8.6, None
        sends.arrive(noted, 7 * NOTES)
        ready.add(0)
        ready.add(1)
        plan(dp, ng, ref.hits, ref.masks)
        yield 10.0, over_r
        yield 10.0, over_l
        across_sib = start(across, across, sib)
        yield 10.5, left_sib
        yield 10.5, right_sib
        ready.add(2)
        yield 12.0, across_sib
        ready.add(3)

    def attention():
        pairs = (
            (dp, x * 2 + 1 - c),
            ((x + NX - 1) % NX * 2 + c, (x + 1) % NX * 2 + c),
            ((x + NX - 1) % NX * 2 + 1 - c, (x + 1) % NX * 2 + 1 - c),
            ((x + 2) % NX * 2 + c, (x + 2) % NX * 2 + 1 - c),
        )
        for n, pair in enumerate(pairs):
            yield (9.0, 9.6, 10.6, 12.1)[n], None
            assert "w" in ready and n in ready
            rows = jnp.concatenate([xg[b] for b in pair], axis=0)
            qkv = jnp.dot(rows, wq[...].reshape(D, QCOLS), preferred_element_type=F32).astype(BF)
            for m, b in enumerate(pair):
                marks = ng[b, :4, :].astype(F32)
                result = attend(qkv[m * ROWS : (m + 1) * ROWS], marks)
                if (n, m) == (0, 0):
                    heads[dp] = result
                else:
                    mixed[b] = result
                    start(mixed.at[b], heads.at[dp], (b, me.ex), heard)

    run_tasks([qkv_weights(), *out_weights(), row_blocks(), attention()])
    sends.arrive(given, D * OCOLS // 128)
    sends.arrive(heard, 7 * ROWS)
    sends.arrive(swaps, 2 * D * 512 // 128)
    rows = jnp.concatenate([heads[b] for b in range(8)], axis=1)
    loads[4].wait()
    loads[5].wait()
    middle(
        ref.frames,
        rows,
        wo,
        ref.conv_w,
        ref.w_router,
        ids,
        ref.second,
        ref.hidden,
        ref.gates,
        ref.shifted,
        ref.masks,
    )


PLANE = [(dy, dz) for dz in range(NZ) for dy in range(NY) if (dy, dz) != (0, 0)]


def plane_peers(me):
    return [me.at(dy=dy, dz=dz) for dy, dz in PLANE]


ORDER = (0, 2, 6, 4, 3, 5, 1, 7)
STRAIGHT = 7


def experts(me, sends, block_out, ref, local_sem):
    start = sends.start
    hidden, hits, gates, second = ref.hidden, ref.hits, ref.gates, ref.second
    both, cells, routed, part, back = ref.both, ref.cells, ref.routed, ref.part, ref.back
    rel_r, rel_l, in_l, in_r = ref.rel_r, ref.rel_l, ref.in_l, ref.in_r
    sum_r, sum_l, total, picked, inbox = ref.sum_r, ref.sum_l, ref.total, ref.picked, ref.inbox
    x, y, z, c = me.x, me.y, me.z, me.c
    xr, xl, sib = me.at(dx=1), me.at(dx=-1), me.at(other=True)
    right, left, across = (x + 1) % NX, (x + NX - 1) % NX, (x + 2) % NX
    low, high = pl.ds(0, 2), pl.ds(2, 2)

    theirs = start(hidden, both.at[c], sib)
    both[c] = hidden[...]
    pick = hits[0] + hits[1]
    theirs.wait_recv()
    rows = jnp.dot(pick, both[...].reshape(2 * ROWS, D), preferred_element_type=F32)
    cells[...] = rows.astype(BF).reshape(PLACES, 8, 128).reshape(NY, NZ, SUB, 128)
    keep = pltpu.make_async_copy(cells.at[y, z], routed.at[z, x, y], local_sem.at[9])
    keep.start()

    direct, sideways, relays, begun, closing = [], [], [], [], []
    returned = sends.slot()

    def group(i):
        return (z - ORDER[i] + NZ) % NZ

    def issue(i):
        dz = ORDER[i]
        direct.append(sends.slot())
        for dy in range(NY):
            if (dy, dz) != (0, 0):
                src = cells.at[(y + dy) % NY, (z + dz) % NZ]
                start(src, routed.at[z, x, y], me.at(dy=dy, dz=dz), direct[i])

    def spread(i):
        if ORDER[i] == 0:
            keep.wait()
        sends.arrive(direct[i], (NY - (ORDER[i] == 0)) * SUB)
        block = routed.at[group(i), x]
        sideways.append((start(block, block, xr), start(block, block, xl)))

    def relay(i):
        g = group(i)
        relays.append(sends.slot())
        sideways[i][0].wait_recv()
        one = routed.at[g, left, low]
        start(one, one, xr, relays[i])
        sideways[i][1].wait_recv()
        two = routed.at[g, right, high]
        start(two, two, xl, relays[i])

    def compute(i):
        g = group(i)
        sends.arrive(relays[i], NY * SUB)
        count = NX * NY * CELL
        rows = routed[g].reshape(count * 8, 128).reshape(count, 8, 128).reshape(count, D)
        result = None
        for up, down in ((ref.up_own, ref.dn_own), (ref.up_sib, ref.dn_sib)):
            upward = jnp.dot(rows, up[...], preferred_element_type=F32)
            activated = (upward / (1.0 + jnp.exp(-upward))).astype(BF)
            term = jnp.dot(activated, down[...], preferred_element_type=F32)
            result = term if result is None else result + term
        part[g] = result.astype(BF).reshape(count, 8, 128).reshape(NX, NY, SUB, 128)
        closing.append(sends.slot())
        if i >= STRAIGHT:
            start(part.at[g, across, low], rel_r.at[g], me.at(dx=2), closing[i])
            start(part.at[g, across, high], rel_l.at[g], me.at(dx=2), closing[i])
            start(part.at[g, right], in_l.at[g], xr, closing[i])
            start(part.at[g, left], in_r.at[g], xl, closing[i])
            return
        begun.append(
            (
                start(part.at[g, across, low], rel_r.at[g], xr),
                start(part.at[g, across, high], rel_l.at[g], xl),
            )
        )
        start(part.at[g, right, high], in_l.at[g, high], xr, closing[i])
        start(part.at[g, left, low], in_r.at[g, low], xl, closing[i])

    def add(i):
        g = group(i)
        if i >= STRAIGHT:
            return
        begun[i][0].wait_recv()
        sum_r[g] = (part[g, right, low].astype(F32) + rel_r[g].astype(F32)).astype(BF)
        start(sum_r.at[g], in_l.at[g, low], xr, closing[i])
        begun[i][1].wait_recv()
        sum_l[g] = (part[g, left, high].astype(F32) + rel_l[g].astype(F32)).astype(BF)
        start(sum_l.at[g], in_r.at[g, high], xl, closing[i])

    def close(i):
        g = group(i)
        sends.arrive(closing[i], (2 + (i >= STRAIGHT)) * NY * SUB)
        added = part[g, x].astype(F32) + in_l[g].astype(F32) + in_r[g].astype(F32)
        if i >= STRAIGHT:
            added = added + jnp.concatenate([rel_r[g], rel_l[g]], axis=0).astype(F32)
        total[g] = added.astype(BF)
        for dy in range(NY):
            src = total.at[g, (y + dy) % NY]
            if (dy, ORDER[i]) == (0, 0):
                back[y, z] = total[g, y]
            else:
                start(src, back.at[y, z], me.at(dy=dy, dz=-ORDER[i]), returned)

    ahead = 2
    for i in range(ahead):
        issue(i)
    for t in range(NZ + 3):
        if t + ahead < NZ:
            issue(t + ahead)
        if t < NZ:
            spread(t)
        if 1 <= t <= NZ:
            relay(t - 1)
        if 2 <= t <= NZ + 1:
            compute(t - 2)
        if 3 <= t <= NZ + 2:
            add(t - 3)
        if 4 <= t:
            close(t - 4)
    close(NZ - 1)
    sends.arrive(returned, (NY * NZ - 1) * SUB)

    rows = back[...].reshape(PLACES * 8, 128).reshape(PLACES, 8, 128).reshape(PLACES, D)
    given = []
    for k in range(TOP):
        taken = lax.dot_general(
            hits[k], rows, (((0,), (0,)), ((), ())), preferred_element_type=F32
        )
        picked[k] = taken.astype(BF).reshape(2, ROWS, D)
        given.append(start(picked.at[k, 1 - c], inbox.at[k], sib))
    result = second[...].astype(F32)
    for k in range(TOP):
        given[k].wait_recv()
        value = picked[k, c].astype(F32) + inbox[k].astype(F32)
        result = result + gates[:, k : k + 1] * value
    block_out[...] = result.astype(BF)


def local(frames, lengths, w_qkv, w_out, conv_w, w_router, expert_ids, w_up, w_down):
    result = pl.pallas_call(
        block_kernel,
        out_shape=jax.ShapeDtypeStruct((ROWS, D), BF),
        in_specs=[SMEM, VMEM] + [HBM] * 7,
        out_specs=VMEM,
        scratch_shapes=[pltpu.VMEM(*shape) for shape in SCRATCH.values()]
        + [
            pltpu.SemaphoreType.DMA((SEND_SLOTS,)),
            pltpu.SemaphoreType.DMA((RECV_SLOTS,)),
            pltpu.SemaphoreType.DMA((10,)),
        ],
        compiler_params=pltpu.CompilerParams(
            collective_id=0, has_side_effects=True, vmem_limit_bytes=60 << 20
        ),
        name="block",
    )(lengths, expert_ids.T, frames, conv_w, w_router.T, w_qkv, w_out, w_up, w_down)
    return jnp.maximum(result, jnp.finfo(BF).min)


def solution(mesh):
    in_specs = (
        P(("dp", "expert"), None),
        P(("dp", "expert"), None),
        P("expert", None),
        P("expert", None),
        P(),
        P(),
        P(("dp", "expert"), None),
        P("expert", None, "dp"),
        P("expert", "dp", None),
    )
    out_specs = P(("dp", "expert"), None)
    return jax.shard_map(local, mesh=mesh, in_specs=in_specs, out_specs=out_specs, check_vma=False)
```

```python
import math
import types

import jax
import jax.numpy as jnp
from jax import lax
from jax.experimental import pallas as pl
from jax.experimental.pallas import tpu as pltpu
from jax.sharding import PartitionSpec as P

HEAD_DIM = 64
ROWS = 128
D = 1024
TOP = 2
NX, NY, NZ = 4, 4, 8
EXPERT_DEVS = NY * NZ
CAP = 5
CELL = 2 * CAP
SUB = CELL * D // 128
QCOLS = 384
OCOLS = 512
NOTES = 16
PLACES = EXPERT_DEVS * CELL
MESH = pl.DeviceIdType.MESH
HBM = pl.BlockSpec(memory_space=pltpu.HBM)
VMEM = pl.BlockSpec(memory_space=pltpu.VMEM)
SMEM = pl.BlockSpec(memory_space=pltpu.SMEM)
BF = jnp.bfloat16
F32 = jnp.float32


def normalize(values):
    mean_value = jnp.mean(values, axis=-1, keepdims=True)
    centred = values - mean_value
    variance = jnp.mean(centred * centred, axis=-1, keepdims=True)
    return centred * lax.rsqrt(variance + 1e-05)


class Place:
    def __init__(self):
        dp, ex = lax.axis_index("dp"), lax.axis_index("expert")
        self.dp, self.ex = dp, ex
        self.x, self.c = dp // 2, dp % 2
        self.y, self.z = ex // NZ, ex % NZ

    def at(self, dx=0, dy=0, dz=0, other=False):
        x, y, z = (self.x + dx + NX) % NX, (self.y + dy + NY) % NY, (self.z + dz + NZ) % NZ
        c = 1 - self.c if other else self.c
        return (x * 2 + c, y * NZ + z)


class Sends:
    def __init__(self, send_sem, recv_sem, ruler):
        self.send_sem, self.recv_sem, self.ruler = send_sem, recv_sem, ruler
        self.slots, self.sent = 0, [0]

    def slot(self):
        self.slots += 1
        assert self.slots <= self.recv_sem.shape[0]
        return self.slots - 1

    def start(self, src, dst, device, slot=None):
        slot = self.slot() if slot is None else slot
        length = math.prod(src.shape) // 128
        if self.sent[-1] + length > self.ruler.shape[0]:
            self.sent.append(0)
        self.sent[-1] += length
        copy = pltpu.make_async_remote_copy(
            src_ref=src,
            dst_ref=dst,
            send_sem=self.send_sem.at[len(self.sent) - 1],
            recv_sem=self.recv_sem.at[slot],
            device_id=device,
            device_id_type=MESH,
        )
        copy.start()
        return copy

    def measure(self, length, sem):
        piece = self.ruler.at[pl.ds(0, length)]
        pltpu.make_async_copy(piece, piece, sem).wait()

    def arrive(self, slot, length):
        self.measure(length, self.recv_sem.at[slot])

    def finish(self):
        for n, length in enumerate(self.sent):
            self.measure(length, self.send_sem.at[n])


def greet(devices):
    barrier = pltpu.get_barrier_semaphore()
    for device in devices:
        pl.semaphore_signal(barrier, inc=1, device_id=device, device_id_type=MESH)
    pl.semaphore_wait(barrier, len(devices))


def run_tasks(tasks):
    waiting = [(next(task, None), task) for task in tasks]
    waiting = [entry for entry in waiting if entry[0] is not None]
    while waiting:
        first = min(range(len(waiting)), key=lambda n: waiting[n][0][0])
        (_, copy), task = waiting.pop(first)
        if copy is not None:
            copy.wait_recv()
        following = next(task, None)
        if following is not None:
            waiting.append((following, task))


def write_notes(lengths, ids, notes):
    rows = lax.broadcasted_iota(jnp.int32, (8, ROWS), 0)
    lanes = lax.broadcasted_iota(jnp.int32, (8, ROWS), 1)
    marks = jnp.zeros((8, ROWS), F32)
    begin = jnp.int32(0)
    for u in range(4):
        end = begin + lengths[0, u]
        inside = (rows == u) & (lanes >= begin) & (lanes < end)
        marks = jnp.where(inside, 1.0, marks)
        begin = end
    for k in range(TOP):
        marks = jnp.where(rows == 4 + k, ids[k : k + 1, :].astype(F32), marks)
    full = jnp.concatenate([marks, jnp.zeros((NOTES - 8, ROWS), F32)], axis=0)
    notes[...] = full.astype(BF)


def attend(qkv, marks):
    first_head = lax.broadcasted_iota(jnp.int32, (ROWS, 128), 1) < HEAD_DIM
    same = lax.dot_general(marks, marks, (((0,), (0,)), ((), ())), preferred_element_type=F32)
    allowed = same > 0.5
    q, k, v = (qkv[:, 128 * i : 128 * i + 128] for i in range(3))
    q = q * jnp.asarray(HEAD_DIM ** (-0.5), BF)
    mixed = []
    for h in range(2):
        own = first_head == (h == 0)
        scores = lax.dot_general(
            jnp.where(own, q, jnp.zeros_like(q)),
            k,
            (((1,), (1,)), ((), ())),
            preferred_element_type=F32,
        )
        scores = jnp.where(allowed, scores, -1e30)
        expo = jnp.exp(scores - jnp.max(scores, axis=-1, keepdims=True)).astype(BF)
        mixed.append(
            jnp.dot(expo, jnp.where(own, v, jnp.ones_like(v)), preferred_element_type=F32)
        )
    sums = jnp.where(first_head, mixed[1], mixed[0])
    return (jnp.where(first_head, mixed[0], mixed[1]) / pltpu.roll(sums, 64, 1)).astype(BF)


def plan(dp, notes, hits, masks):
    core = dp % 2
    each = lax.broadcasted_iota(jnp.int32, (2 * EXPERT_DEVS, ROWS), 0)
    square = (ROWS, ROWS)
    at_row = lax.broadcasted_iota(jnp.int32, square, 0)
    at_lane = lax.broadcasted_iota(jnp.int32, square, 1)
    marks = notes[dp, :4, :].astype(F32)
    same = lax.dot_general(marks, marks, (((0,), (0,)), ((), ())), preferred_element_type=F32)
    begin = jnp.min(jnp.where(same > 0.5, at_lane, ROWS), axis=1, keepdims=True)
    end = jnp.max(jnp.where(same > 0.5, at_lane + 1, 0), axis=1, keepdims=True)
    low = jnp.broadcast_to(begin, square) - at_row + 15
    high = jnp.broadcast_to(end, square) - at_row + 15
    for j in range(31):
        masks[j] = jnp.where((low <= j) & (j < high), 1.0, 0.0)

    before = (at_row < at_lane).astype(BF)
    place = lax.broadcasted_iota(jnp.int32, (PLACES, ROWS), 0)
    for s in range(2):
        names = notes[dp // 2 * 2 + s, 4:8, :].astype(F32).astype(jnp.int32)
        held = jnp.zeros((2 * EXPERT_DEVS, 1), F32)
        for k in range(TOP):
            name = names[k : k + 1]
            ones = jnp.where(name == each, 1.0, 0.0)
            earlier = jnp.dot(ones.astype(BF), before, preferred_element_type=F32) + held
            rank = jnp.sum(ones * earlier, axis=0, keepdims=True).astype(jnp.int32)
            held = held + jnp.sum(ones, axis=1, keepdims=True)
            slot = name // 2 * CELL + s * CAP + rank
            slot = jnp.where(name % 2 == core, slot, -1)
            hits[k, :, pl.ds(s * ROWS, ROWS)] = jnp.where(place == slot, 1.0, 0.0).astype(BF)


def middle(
    frames, rows, wo, conv_w, w_router, ids, second, hidden, gates, shifted, masks, swap
):
    square = (ROWS, ROWS)
    at_row = lax.broadcasted_iota(jnp.int32, square, 0)
    at_lane = lax.broadcasted_iota(jnp.int32, square, 1)
    halves = [
        jnp.dot(rows, wo[n].reshape(D, OCOLS), preferred_element_type=F32) for n in range(2)
    ]
    added = jnp.concatenate(halves, axis=1)
    first = (frames[...].astype(F32) + added).astype(BF).astype(F32)
    conv_in = normalize(first)

    edge = jnp.zeros((16, D), F32)
    padded = jnp.concatenate([edge, conv_in, edge], axis=0)
    for s in range(8):
        shifted[s] = padded[s : s + 152]

    def columns(i, carry):
        lanes = pl.ds(pl.multiple_of(i * 128, 128), 128)
        total = jnp.zeros((ROWS, 128), F32)
        for j in range(31):
            window = shifted[(j + 1) % 8, pl.ds((j + 1) // 8 * 8, ROWS), lanes]
            total = total + (conv_w[pl.ds(j, 1), lanes] * window) * masks[j]
        shifted[0, pl.ds(0, ROWS), lanes] = total
        return carry

    lax.fori_loop(0, D // 128, columns, 0)
    conv_out = shifted[0, pl.ds(0, ROWS), :]
    after = (first + conv_out / (1.0 + jnp.exp(-conv_out))).astype(BF)
    second[...] = after
    normed = normalize(after.astype(F32)).astype(BF)
    hidden[...] = normed
    swap()

    logits = lax.dot_general(
        w_router[...], normed, (((1,), (1,)), ((), ())), preferred_element_type=F32
    )
    each = lax.broadcasted_iota(jnp.int32, (2 * EXPERT_DEVS, ROWS), 0)
    for k in range(TOP):
        chosen = jnp.where(ids[k : k + 1, :] == each, logits, 0.0)
        gate = 1.0 / (1.0 + jnp.exp(-jnp.sum(chosen, axis=0, keepdims=True)))
        turned = jnp.where(at_row == at_lane, jnp.broadcast_to(gate, square), 0.0)
        gates[:, k : k + 1] = jnp.sum(turned, axis=1, keepdims=True)


SCRATCH = dict(
    frames=((ROWS, D), BF),
    conv_w=((31, D), F32),
    w_router=((2 * EXPERT_DEVS, D), BF),
    second=((ROWS, D), BF),
    hidden=((ROWS, D), BF),
    gates=((ROWS, TOP), F32),
    hits=((TOP, PLACES, 2 * ROWS), BF),
    up_sib=((D, 512), BF),
    dn_sib=((512, D), BF),
    up_own=((D, 512), BF),
    dn_own=((512, D), BF),
    xc=((ROWS, D), BF),
    xg=((8, ROWS, D), BF),
    notes=((NOTES, ROWS), BF),
    ng=((8, NOTES, ROWS), BF),
    wq=((NY, NZ, 32, QCOLS), BF),
    wo=((2, NY, NZ, 32, OCOLS), BF),
    mixed=((8, ROWS, 128), BF),
    heads=((8, ROWS, 128), BF),
    shifted=((8, 152, D), F32),
    masks=((31, ROWS, ROWS), F32),
    both=((2, ROWS, D), BF),
    cells=((NY, NZ, SUB, 128), BF),
    routed=((NZ, NX, NY, SUB, 128), BF),
    part=((NZ, NX, NY, SUB, 128), BF),
    back=((NY, NZ, SUB, 128), BF),
    rel_r=((NZ, 2, SUB, 128), BF),
    rel_l=((NZ, 2, SUB, 128), BF),
    in_l=((NZ, NY, SUB, 128), BF),
    in_r=((NZ, NY, SUB, 128), BF),
    sum_r=((NZ, 2, SUB, 128), BF),
    sum_l=((NZ, 2, SUB, 128), BF),
    total=((NZ, NY, SUB, 128), BF),
    picked=((TOP, ROWS, D), BF),
    inbox=((TOP, ROWS, D), BF),
    ruler=((20480, 128), BF),
)
SEND_SLOTS, RECV_SLOTS = 3, 119


def block_kernel(
    lengths, ids, frames, conv_w, w_router, wqkv, wout, wup, wdn, block_out, *scratch
):
    send_sem, recv_sem, local_sem = scratch[len(SCRATCH) :]
    ref = types.SimpleNamespace(**dict(zip(SCRATCH, scratch)))
    me = Place()
    sib = me.at(other=True)
    others = [((me.dp + o) % 8, me.ex) for o in range(1, 8)]
    half = pl.ds(pl.multiple_of(me.c * OCOLS, 128), OCOLS)
    loads = [
        (frames, ref.frames),
        (wout.at[:, half], ref.wo.at[me.c, me.y, me.z]),
        (wup.at[me.c], ref.up_own),
        (wdn.at[me.c], ref.dn_own),
        (conv_w, ref.conv_w),
        (w_router, ref.w_router),
    ]
    for part in range(3):
        columns = pl.ds(pl.multiple_of(part * D + me.dp * 128, 128), 128)
        loads.append((wqkv.at[:, columns], ref.wq.at[me.y, me.z, :, pl.ds(part * 128, 128)]))
    loads = [
        pltpu.make_async_copy(src, dst, local_sem.at[n]) for n, (src, dst) in enumerate(loads)
    ]
    for copy in loads:
        copy.start()
    greet(plane_peers(me) + others)
    sends = Sends(send_sem, recv_sem, ref.ruler)
    for copy in loads[1:2] + loads[6:]:
        copy.wait()
    theirs = front(me, sends, others, loads, lengths, ids, wup, wdn, ref)
    for copy in loads[2:4]:
        copy.wait()
    experts(me, sends, theirs, block_out, ref)
    sends.finish()


def front(me, sends, others, loads, lengths, ids, wup, wdn, ref):
    start = sends.start
    xc, xg, notes, ng, wq, wo = ref.xc, ref.xg, ref.notes, ref.ng, ref.wq, ref.wo
    mixed, heads = ref.mixed, ref.heads
    x, c, y, z, dp = me.x, me.c, me.y, me.z, me.dp
    sib = me.at(other=True)
    xr, xl = me.at(dx=1), me.at(dx=-1)
    yu, yd = me.at(dy=1), me.at(dy=-1)
    zu, zd = me.at(dz=1), me.at(dz=-1)
    def yy(d):
        return (y + d + NY) % NY

    def zz(d):
        return (z + d + NZ) % NZ

    swaps, noted, given, heard, ready = *(sends.slot() for _ in range(4)), set()

    def out_weights():
        def block(dy, dz):
            return wo.at[c, yy(dy), zz(dz)]

        def share(dy, dz):
            start(block(dy, dz), block(dy, dz), sib, given)

        def along_z(dy, time):
            up = start(block(dy, 0), block(dy, 0), zu)
            down = start(block(dy, 0), block(dy, 0), zd)
            share(dy, 0)
            for s in range(1, 4):
                yield time + 3.6 * s, up
                if s < 3 or dy in (0, 2):
                    up = start(block(dy, -s), block(dy, -s), zu)
                share(dy, -s)
                yield time + 3.6 * s + 0.1, down
                if s < 3 or dy in (1, -1):
                    down = start(block(dy, s), block(dy, s), zd)
                share(dy, s)
            yield time + 14.4, up if dy in (0, 2) else down
            share(dy, 4)

        def from_above():
            yield 1.9, to_d
            yield from along_z(1, 2.0)

        def from_across():
            yield 2.4, over
            yield from along_z(2, 2.5)

        to_u = start(block(0, 0), block(0, 0), yu)
        to_d = start(block(0, 0), block(0, 0), yd)
        over = start(block(0, 0), block(0, 0), me.at(dy=2))

        def from_below():
            yield 1.9, to_u
            yield from along_z(-1, 2.0)

        return [along_z(0, 0.0), from_below(), from_above(), from_across()]

    def qkv_weights():
        def block(dy, dz):
            return wq.at[yy(dy), zz(dz)]

        def available(dz):
            one, slot = block(0, dz), sends.slot()
            start(one, one, yu, slot)
            start(one, one, yd, slot)
            if len(spread) >= 5:
                start(one, one, me.at(dy=2), last)
            spread.append((dz, slot))

        def pass_on(n, time):
            dz, slot = spread[n]
            yield time, None
            sends.arrive(slot, 2 * 32 * QCOLS // 128)
            if n >= 5:
                return
            one = block(-1, dz) if dz in (0, 1, 2, -3) else block(1, dz)
            start(one, one, yu if dz in (0, 1, 2, -3) else yd, last)

        spread, last = [], sends.slot()
        order = (1, -1, 2, -2, 3, -3, 4)
        direct = [
            start(block(0, 0), block(0, 0), me.at(dz=dz)) for dz in order
        ]
        available(0)
        for n, dz in enumerate(order):
            yield 2.0 + 0.5 * n, direct[n]
            available(-dz)
            if n >= 3:
                yield from pass_on(n - 3, 2.1 + 0.5 * n)
        for n in range(4, 8):
            yield from pass_on(n, 4.6 + 0.5 * n)
        yield 8.8, None
        sends.arrive(last, NZ * 32 * QCOLS // 128)
        ready.add("w")

    def row_blocks():
        loads[0].wait()
        xc[...] = normalize(ref.frames[...].astype(F32)).astype(BF)
        xg[dp] = xc[...]
        low, high = pl.ds(0, 64), pl.ds(64, 64)
        left = xg.at[((x + NX - 1) % NX) * 2 + c]
        right = xg.at[((x + 1) % NX) * 2 + c]
        across = xg.at[((x + 2) % NX) * 2 + c]
        r_low = start(xc.at[low], xg.at[dp, low], xr)
        l_high = start(xc.at[high], xg.at[dp, high], xl)
        to_sib = start(xc, xg.at[dp], sib)
        r_high = start(xc.at[high], xg.at[dp, high], xr)
        l_low = start(xc.at[low], xg.at[dp, low], xl)
        write_notes(lengths, ids, notes)
        ng[dp] = notes[...]
        for device in others:
            start(notes, ng.at[dp], device, noted)
        start(wup.at[1 - c], ref.up_sib, sib, swaps)
        start(wdn.at[1 - c], ref.dn_sib, sib, swaps)
        yield 5.5, r_low
        over_r = start(left.at[low], left.at[low], xr)
        yield 5.5, l_high
        over_l = start(right.at[high], right.at[high], xl)
        yield 8.5, r_high
        left_sib = start(left, left, sib)
        yield 8.5, l_low
        right_sib = start(right, right, sib)
        yield 8.6, to_sib
        yield 8.6, None
        sends.arrive(noted, 7 * NOTES)
        ready.add(0)
        ready.add(1)
        plan(dp, ng, ref.hits, ref.masks)
        yield 10.0, over_r
        yield 10.0, over_l
        across_sib = start(across, across, sib)
        yield 10.5, left_sib
        yield 10.5, right_sib
        ready.add(2)
        yield 12.0, across_sib
        ready.add(3)

    def attention():
        pairs = (
            (dp, x * 2 + 1 - c),
            ((x + NX - 1) % NX * 2 + c, (x + 1) % NX * 2 + c),
            ((x + NX - 1) % NX * 2 + 1 - c, (x + 1) % NX * 2 + 1 - c),
            ((x + 2) % NX * 2 + c, (x + 2) % NX * 2 + 1 - c),
        )
        for n, pair in enumerate(pairs):
            yield (9.0, 9.6, 10.6, 12.1)[n], None
            assert "w" in ready and n in ready
            rows = jnp.concatenate([xg[b] for b in pair], axis=0)
            qkv = jnp.dot(rows, wq[...].reshape(D, QCOLS), preferred_element_type=F32).astype(BF)
            for m, b in enumerate(pair):
                marks = ng[b, :4, :].astype(F32)
                result = attend(qkv[m * ROWS : (m + 1) * ROWS], marks)
                if (n, m) == (0, 0):
                    heads[dp] = result
                else:
                    mixed[b] = result
                    start(mixed.at[b], heads.at[dp], (b, me.ex), heard)

    run_tasks([qkv_weights(), *out_weights(), row_blocks(), attention()])
    sends.arrive(given, D * OCOLS // 128)
    sends.arrive(heard, 7 * ROWS)
    sends.arrive(swaps, 2 * D * 512 // 128)
    rows = jnp.concatenate([heads[b] for b in range(8)], axis=1)
    swapped = []
    loads[4].wait()
    loads[5].wait()
    middle(
        ref.frames,
        rows,
        wo,
        ref.conv_w,
        ref.w_router,
        ids,
        ref.second,
        ref.hidden,
        ref.gates,
        ref.shifted,
        ref.masks,
        lambda: swapped.append(start(ref.hidden, ref.both.at[c], sib)),
    )
    return swapped[0]


PLANE = [(dy, dz) for dz in range(NZ) for dy in range(NY) if (dy, dz) != (0, 0)]


def plane_peers(me):
    return [me.at(dy=dy, dz=dz) for dy, dz in PLANE]


ORDER = (0, 2, 6, 4, 3, 5, 1, 7)
STRAIGHT = 7


def experts(me, sends, theirs, block_out, ref):
    start = sends.start
    hidden, hits, gates, second = ref.hidden, ref.hits, ref.gates, ref.second
    both, cells, routed, part, back = ref.both, ref.cells, ref.routed, ref.part, ref.back
    rel_r, rel_l, in_l, in_r = ref.rel_r, ref.rel_l, ref.in_l, ref.in_r
    sum_r, sum_l, total, picked, inbox = ref.sum_r, ref.sum_l, ref.total, ref.picked, ref.inbox
    x, y, z, c = me.x, me.y, me.z, me.c
    xr, xl, sib = me.at(dx=1), me.at(dx=-1), me.at(other=True)
    right, left, across = (x + 1) % NX, (x + NX - 1) % NX, (x + 2) % NX
    low, high = pl.ds(0, 2), pl.ds(2, 2)

    both[c] = hidden[...]
    pick = hits[0] + hits[1]
    theirs.wait_recv()
    rows = jnp.dot(pick, both[...].reshape(2 * ROWS, D), preferred_element_type=F32)
    cells[...] = rows.astype(BF).reshape(PLACES, 8, 128).reshape(NY, NZ, SUB, 128)
    routed[z, x, y] = cells[y, z]

    direct, sideways, relays, begun, closing = [], [], [], [], []
    returned = sends.slot()

    def group(i):
        return (z - ORDER[i] + NZ) % NZ

    def issue(i):
        dz = ORDER[i]
        direct.append(sends.slot())
        for dy in range(NY):
            if (dy, dz) != (0, 0):
                src = cells.at[(y + dy) % NY, (z + dz) % NZ]
                start(src, routed.at[z, x, y], me.at(dy=dy, dz=dz), direct[i])

    def spread(i):
        sends.arrive(direct[i], (NY - (ORDER[i] == 0)) * SUB)
        block = routed.at[group(i), x]
        sideways.append((start(block, block, xr), start(block, block, xl)))

    def relay(i):
        g = group(i)
        relays.append(sends.slot())
        sideways[i][0].wait_recv()
        one = routed.at[g, left, low]
        start(one, one, xr, relays[i])
        sideways[i][1].wait_recv()
        two = routed.at[g, right, high]
        start(two, two, xl, relays[i])

    def compute(i):
        g = group(i)
        sends.arrive(relays[i], NY * SUB)
        count = NX * NY * CELL
        rows = routed[g].reshape(count * 8, 128).reshape(count, 8, 128).reshape(count, D)
        result = None
        for up, down in ((ref.up_own, ref.dn_own), (ref.up_sib, ref.dn_sib)):
            upward = jnp.dot(rows, up[...], preferred_element_type=F32)
            activated = (upward / (1.0 + jnp.exp(-upward))).astype(BF)
            term = jnp.dot(activated, down[...], preferred_element_type=F32)
            result = term if result is None else result + term
        part[g] = result.astype(BF).reshape(count, 8, 128).reshape(NX, NY, SUB, 128)
        closing.append(sends.slot())
        if i >= STRAIGHT:
            start(part.at[g, across, low], rel_r.at[g], me.at(dx=2), closing[i])
            start(part.at[g, across, high], rel_l.at[g], me.at(dx=2), closing[i])
            start(part.at[g, right], in_l.at[g], xr, closing[i])
            start(part.at[g, left], in_r.at[g], xl, closing[i])
            return
        begun.append(
            (
                start(part.at[g, across, low], rel_r.at[g], xr),
                start(part.at[g, across, high], rel_l.at[g], xl),
            )
        )
        start(part.at[g, right, high], in_l.at[g, high], xr, closing[i])
        start(part.at[g, left, low], in_r.at[g, low], xl, closing[i])

    def add(i):
        g = group(i)
        if i >= STRAIGHT:
            return
        begun[i][0].wait_recv()
        sum_r[g] = (part[g, right, low].astype(F32) + rel_r[g].astype(F32)).astype(BF)
        start(sum_r.at[g], in_l.at[g, low], xr, closing[i])
        begun[i][1].wait_recv()
        sum_l[g] = (part[g, left, high].astype(F32) + rel_l[g].astype(F32)).astype(BF)
        start(sum_l.at[g], in_r.at[g, high], xl, closing[i])

    def close(i):
        g = group(i)
        sends.arrive(closing[i], (2 + (i >= STRAIGHT)) * NY * SUB)
        added = part[g, x].astype(F32) + in_l[g].astype(F32) + in_r[g].astype(F32)
        if i >= STRAIGHT:
            added = added + jnp.concatenate([rel_r[g], rel_l[g]], axis=0).astype(F32)
        total[g] = added.astype(BF)
        for dy in range(NY):
            src = total.at[g, (y + dy) % NY]
            if (dy, ORDER[i]) == (0, 0):
                back[y, z] = total[g, y]
            else:
                start(src, back.at[y, z], me.at(dy=dy, dz=-ORDER[i]), returned)

    ahead = 2
    for i in range(ahead):
        issue(i)
    for t in range(NZ + 3):
        if t + ahead < NZ:
            issue(t + ahead)
        if t < NZ:
            spread(t)
        if 1 <= t <= NZ:
            relay(t - 1)
        if 2 <= t <= NZ + 1:
            compute(t - 2)
        if 3 <= t <= NZ + 2:
            add(t - 3)
        if 4 <= t:
            close(t - 4)
    close(NZ - 1)
    sends.arrive(returned, (NY * NZ - 1) * SUB)

    rows = back[...].reshape(PLACES * 8, 128).reshape(PLACES, 8, 128).reshape(PLACES, D)

    def take(k, core):
        columns = pl.ds(pl.multiple_of(core * ROWS, ROWS), ROWS)
        return lax.dot_general(
            hits[k, :, columns], rows, (((0,), (0,)), ((), ())), preferred_element_type=F32
        )

    given = []
    for k in range(TOP):
        picked[k] = take(k, 1 - c).astype(BF)
        given.append(start(picked.at[k], inbox.at[k], sib))
    result = second[...].astype(F32)
    mine = [take(k, c) for k in range(TOP)]
    for k in range(TOP):
        given[k].wait_recv()
        result = result + gates[:, k : k + 1] * (mine[k] + inbox[k].astype(F32))
    block_out[...] = result.astype(BF)


def local(frames, lengths, w_qkv, w_out, conv_w, w_router, expert_ids, w_up, w_down):
    result = pl.pallas_call(
        block_kernel,
        out_shape=jax.ShapeDtypeStruct((ROWS, D), BF),
        in_specs=[SMEM, VMEM] + [HBM] * 7,
        out_specs=VMEM,
        scratch_shapes=[pltpu.VMEM(*shape) for shape in SCRATCH.values()]
        + [
            pltpu.SemaphoreType.DMA((SEND_SLOTS,)),
            pltpu.SemaphoreType.DMA((RECV_SLOTS,)),
            pltpu.SemaphoreType.DMA((9,)),
        ],
        compiler_params=pltpu.CompilerParams(
            collective_id=0, has_side_effects=True, vmem_limit_bytes=60 << 20
        ),
        name="block",
    )(lengths, expert_ids.T, frames, conv_w, w_router.T, w_qkv, w_out, w_up, w_down)
    return jnp.maximum(result, jnp.finfo(BF).min)


def solution(mesh):
    in_specs = (
        P(("dp", "expert"), None),
        P(("dp", "expert"), None),
        P("expert", None),
        P("expert", None),
        P(),
        P(),
        P(("dp", "expert"), None),
        P("expert", None, "dp"),
        P("expert", "dp", None),
    )
    out_specs = P(("dp", "expert"), None)
    return jax.shard_map(local, mesh=mesh, in_specs=in_specs, out_specs=out_specs, check_vma=False)
```

```python
import math
import types

import jax
import jax.numpy as jnp
from jax import lax
from jax.experimental import pallas as pl
from jax.experimental.pallas import tpu as pltpu
from jax.sharding import PartitionSpec as P

HEAD_DIM = 64
ROWS = 128
D = 1024
TOP = 2
NX, NY, NZ = 4, 4, 8
EXPERT_DEVS = NY * NZ
CAP = 5
CELL = 2 * CAP
SUB = CELL * D // 128
QCOLS = 384
OCOLS = 512
NOTES = 16
PLACES = EXPERT_DEVS * CELL
MESH = pl.DeviceIdType.MESH
HBM = pl.BlockSpec(memory_space=pltpu.HBM)
VMEM = pl.BlockSpec(memory_space=pltpu.VMEM)
SMEM = pl.BlockSpec(memory_space=pltpu.SMEM)
BF = jnp.bfloat16
F32 = jnp.float32


def normalize(values):
    mean_value = jnp.mean(values, axis=-1, keepdims=True)
    centred = values - mean_value
    variance = jnp.mean(centred * centred, axis=-1, keepdims=True)
    return centred * lax.rsqrt(variance + 1e-05)


class Place:
    def __init__(self):
        dp, ex = lax.axis_index("dp"), lax.axis_index("expert")
        self.dp, self.ex = dp, ex
        self.x, self.c = dp // 2, dp % 2
        self.y, self.z = ex // NZ, ex % NZ

    def at(self, dx=0, dy=0, dz=0, other=False):
        x, y, z = (self.x + dx + NX) % NX, (self.y + dy + NY) % NY, (self.z + dz + NZ) % NZ
        c = 1 - self.c if other else self.c
        return (x * 2 + c, y * NZ + z)


class Sends:
    def __init__(self, send_sem, recv_sem, ruler):
        self.send_sem, self.recv_sem, self.ruler = send_sem, recv_sem, ruler
        self.slots, self.sent = 0, [0]

    def slot(self):
        self.slots += 1
        assert self.slots <= self.recv_sem.shape[0]
        return self.slots - 1

    def start(self, src, dst, device, slot=None):
        slot = self.slot() if slot is None else slot
        length = math.prod(src.shape) // 128
        if self.sent[-1] + length > self.ruler.shape[0]:
            self.sent.append(0)
        self.sent[-1] += length
        copy = pltpu.make_async_remote_copy(
            src_ref=src,
            dst_ref=dst,
            send_sem=self.send_sem.at[len(self.sent) - 1],
            recv_sem=self.recv_sem.at[slot],
            device_id=device,
            device_id_type=MESH,
        )
        copy.start()
        return copy

    def measure(self, length, sem):
        piece = self.ruler.at[pl.ds(0, length)]
        pltpu.make_async_copy(piece, piece, sem).wait()

    def arrive(self, slot, length):
        self.measure(length, self.recv_sem.at[slot])

    def finish(self):
        for n, length in enumerate(self.sent):
            self.measure(length, self.send_sem.at[n])


def greet(devices):
    barrier = pltpu.get_barrier_semaphore()
    for device in devices:
        pl.semaphore_signal(barrier, inc=1, device_id=device, device_id_type=MESH)
    pl.semaphore_wait(barrier, len(devices))


def run_tasks(tasks):
    waiting = [(next(task, None), task) for task in tasks]
    waiting = [entry for entry in waiting if entry[0] is not None]
    while waiting:
        first = min(range(len(waiting)), key=lambda n: waiting[n][0][0])
        (_, copy), task = waiting.pop(first)
        if copy is not None:
            copy.wait_recv()
        following = next(task, None)
        if following is not None:
            waiting.append((following, task))


def write_notes(lengths, ids, notes):
    rows = lax.broadcasted_iota(jnp.int32, (8, ROWS), 0)
    lanes = lax.broadcasted_iota(jnp.int32, (8, ROWS), 1)
    marks = jnp.zeros((8, ROWS), F32)
    begin = jnp.int32(0)
    for u in range(4):
        end = begin + lengths[0, u]
        inside = (rows == u) & (lanes >= begin) & (lanes < end)
        marks = jnp.where(inside, 1.0, marks)
        begin = end
    for k in range(TOP):
        marks = jnp.where(rows == 4 + k, ids[k : k + 1, :].astype(F32), marks)
    full = jnp.concatenate([marks, jnp.zeros((NOTES - 8, ROWS), F32)], axis=0)
    notes[...] = full.astype(BF)


def attend(qkv, marks):
    first_head = lax.broadcasted_iota(jnp.int32, (ROWS, 128), 1) < HEAD_DIM
    same = lax.dot_general(marks, marks, (((0,), (0,)), ((), ())), preferred_element_type=F32)
    allowed = same > 0.5
    q, k, v = (qkv[:, 128 * i : 128 * i + 128] for i in range(3))
    q = q * jnp.asarray(HEAD_DIM ** (-0.5), BF)
    mixed = []
    for h in range(2):
        own = first_head == (h == 0)
        scores = lax.dot_general(
            jnp.where(own, q, jnp.zeros_like(q)),
            k,
            (((1,), (1,)), ((), ())),
            preferred_element_type=F32,
        )
        scores = jnp.where(allowed, scores, -1e30)
        expo = jnp.exp(scores - jnp.max(scores, axis=-1, keepdims=True)).astype(BF)
        mixed.append(
            jnp.dot(expo, jnp.where(own, v, jnp.ones_like(v)), preferred_element_type=F32)
        )
    sums = jnp.where(first_head, mixed[1], mixed[0])
    return (jnp.where(first_head, mixed[0], mixed[1]) / pltpu.roll(sums, 64, 1)).astype(BF)


def plan(dp, notes, hits, masks):
    core = dp % 2
    each = lax.broadcasted_iota(jnp.int32, (2 * EXPERT_DEVS, ROWS), 0)
    square = (ROWS, ROWS)
    at_row = lax.broadcasted_iota(jnp.int32, square, 0)
    at_lane = lax.broadcasted_iota(jnp.int32, square, 1)
    marks = notes[dp, :4, :].astype(F32)
    same = lax.dot_general(marks, marks, (((0,), (0,)), ((), ())), preferred_element_type=F32)
    begin = jnp.min(jnp.where(same > 0.5, at_lane, ROWS), axis=1, keepdims=True)
    end = jnp.max(jnp.where(same > 0.5, at_lane + 1, 0), axis=1, keepdims=True)
    low = jnp.broadcast_to(begin, square) - at_row + 15
    high = jnp.broadcast_to(end, square) - at_row + 15
    for j in range(31):
        masks[j] = jnp.where((low <= j) & (j < high), 1.0, 0.0)

    before = (at_row < at_lane).astype(BF)
    place = lax.broadcasted_iota(jnp.int32, (PLACES, ROWS), 0)
    for s in range(2):
        names = notes[dp // 2 * 2 + s, 4:8, :].astype(F32).astype(jnp.int32)
        held = jnp.zeros((2 * EXPERT_DEVS, 1), F32)
        for k in range(TOP):
            name = names[k : k + 1]
            ones = jnp.where(name == each, 1.0, 0.0)
            earlier = jnp.dot(ones.astype(BF), before, preferred_element_type=F32) + held
            rank = jnp.sum(ones * earlier, axis=0, keepdims=True).astype(jnp.int32)
            held = held + jnp.sum(ones, axis=1, keepdims=True)
            slot = name // 2 * CELL + s * CAP + rank
            slot = jnp.where(name % 2 == core, slot, -1)
            hits[k, :, pl.ds(s * ROWS, ROWS)] = jnp.where(place == slot, 1.0, 0.0).astype(BF)


def middle(
    frames, rows, wo, conv_w, w_router, ids, second, hidden, gates, shifted, masks, swap
):
    square = (ROWS, ROWS)
    at_row = lax.broadcasted_iota(jnp.int32, square, 0)
    at_lane = lax.broadcasted_iota(jnp.int32, square, 1)
    halves = [
        jnp.dot(rows, wo[n].reshape(D, OCOLS), preferred_element_type=F32) for n in range(2)
    ]
    added = jnp.concatenate(halves, axis=1)
    first = (frames[...].astype(F32) + added).astype(BF).astype(F32)
    conv_in = normalize(first)

    edge = jnp.zeros((16, D), F32)
    padded = jnp.concatenate([edge, conv_in, edge], axis=0)
    for s in range(8):
        shifted[s] = padded[s : s + 152]

    def columns(i, carry):
        lanes = pl.ds(pl.multiple_of(i * 128, 128), 128)
        total = jnp.zeros((ROWS, 128), F32)
        for j in range(31):
            window = shifted[(j + 1) % 8, pl.ds((j + 1) // 8 * 8, ROWS), lanes]
            total = total + (conv_w[pl.ds(j, 1), lanes] * window) * masks[j]
        shifted[0, pl.ds(0, ROWS), lanes] = total
        return carry

    lax.fori_loop(0, D // 128, columns, 0)
    conv_out = shifted[0, pl.ds(0, ROWS), :]
    after = (first + conv_out / (1.0 + jnp.exp(-conv_out))).astype(BF)
    second[...] = after
    normed = normalize(after.astype(F32)).astype(BF)
    hidden[...] = normed
    swap()

    logits = lax.dot_general(
        w_router[...], normed, (((1,), (1,)), ((), ())), preferred_element_type=F32
    )
    each = lax.broadcasted_iota(jnp.int32, (2 * EXPERT_DEVS, ROWS), 0)
    for k in range(TOP):
        chosen = jnp.where(ids[k : k + 1, :] == each, logits, 0.0)
        gate = 1.0 / (1.0 + jnp.exp(-jnp.sum(chosen, axis=0, keepdims=True)))
        turned = jnp.where(at_row == at_lane, jnp.broadcast_to(gate, square), 0.0)
        gates[:, k : k + 1] = jnp.sum(turned, axis=1, keepdims=True)


SCRATCH = dict(
    frames=((ROWS, D), BF),
    conv_w=((31, D), F32),
    w_router=((2 * EXPERT_DEVS, D), BF),
    second=((ROWS, D), BF),
    hidden=((ROWS, D), BF),
    gates=((ROWS, TOP), F32),
    hits=((TOP, PLACES, 2 * ROWS), BF),
    up_sib=((D, 512), BF),
    dn_sib=((512, D), BF),
    up_own=((D, 512), BF),
    dn_own=((512, D), BF),
    xc=((ROWS, D), BF),
    xg=((8, ROWS, D), BF),
    notes=((NOTES, ROWS), BF),
    ng=((8, NOTES, ROWS), BF),
    wq=((NY, NZ, 32, QCOLS), BF),
    wo=((2, NY, NZ, 32, OCOLS), BF),
    mixed=((8, ROWS, 128), BF),
    heads=((8, ROWS, 128), BF),
    shifted=((8, 152, D), F32),
    masks=((31, ROWS, ROWS), F32),
    both=((2, ROWS, D), BF),
    cells=((NY, NZ, SUB, 128), BF),
    routed=((NZ, NX, NY, SUB, 128), BF),
    part=((NZ, NX, NY, SUB, 128), BF),
    back=((NY, NZ, SUB, 128), BF),
    rel_r=((NZ, 2, SUB, 128), BF),
    rel_l=((NZ, 2, SUB, 128), BF),
    in_l=((NZ, NY, SUB, 128), BF),
    in_r=((NZ, NY, SUB, 128), BF),
    sum_r=((NZ, 2, SUB, 128), BF),
    sum_l=((NZ, 2, SUB, 128), BF),
    total=((NZ, NY, SUB, 128), BF),
    picked=((TOP, ROWS, D), BF),
    inbox=((TOP, ROWS, D), BF),
    ruler=((20480, 128), BF),
)
SEND_SLOTS, RECV_SLOTS = 3, 119


def block_kernel(
    lengths, ids, frames, conv_w, w_router, wqkv, wout, wup, wdn, block_out, *scratch
):
    send_sem, recv_sem, local_sem = scratch[len(SCRATCH) :]
    ref = types.SimpleNamespace(**dict(zip(SCRATCH, scratch)))
    me = Place()
    sib = me.at(other=True)
    others = [((me.dp + o) % 8, me.ex) for o in range(1, 8)]
    half = pl.ds(pl.multiple_of(me.c * OCOLS, 128), OCOLS)
    loads = [
        (frames, ref.frames),
        (wout.at[:, half], ref.wo.at[me.c, me.y, me.z]),
        (wup.at[me.c], ref.up_own),
        (wdn.at[me.c], ref.dn_own),
        (conv_w, ref.conv_w),
        (w_router, ref.w_router),
    ]
    for part in range(3):
        columns = pl.ds(pl.multiple_of(part * D + me.dp * 128, 128), 128)
        loads.append((wqkv.at[:, columns], ref.wq.at[me.y, me.z, :, pl.ds(part * 128, 128)]))
    loads = [
        pltpu.make_async_copy(src, dst, local_sem.at[n]) for n, (src, dst) in enumerate(loads)
    ]
    for n in (6, 7, 8, 1, 0):
        loads[n].start()
    greet(plane_peers(me) + others)
    sends = Sends(send_sem, recv_sem, ref.ruler)
    for copy in loads[1:2] + loads[6:]:
        copy.wait()
    for copy in loads[2:6]:
        copy.start()
    theirs = front(me, sends, others, loads, lengths, ids, wup, wdn, ref)
    for copy in loads[2:4]:
        copy.wait()
    experts(me, sends, theirs, block_out, ref)
    sends.finish()


def front(me, sends, others, loads, lengths, ids, wup, wdn, ref):
    start = sends.start
    xc, xg, notes, ng, wq, wo = ref.xc, ref.xg, ref.notes, ref.ng, ref.wq, ref.wo
    mixed, heads = ref.mixed, ref.heads
    x, c, y, z, dp = me.x, me.c, me.y, me.z, me.dp
    sib = me.at(other=True)
    xr, xl = me.at(dx=1), me.at(dx=-1)
    yu, yd = me.at(dy=1), me.at(dy=-1)
    zu, zd = me.at(dz=1), me.at(dz=-1)
    def yy(d):
        return (y + d + NY) % NY

    def zz(d):
        return (z + d + NZ) % NZ

    swaps, noted, given, heard, ready = *(sends.slot() for _ in range(4)), set()

    def out_weights():
        def block(dy, dz):
            return wo.at[c, yy(dy), zz(dz)]

        def share(dy, dz):
            start(block(dy, dz), block(dy, dz), sib, given)

        def along_z(dy, time):
            up = start(block(dy, 0), block(dy, 0), zu)
            down = start(block(dy, 0), block(dy, 0), zd)
            share(dy, 0)
            for s in range(1, 4):
                yield time + 3.6 * s, up
                if s < 3 or dy in (0, 2):
                    up = start(block(dy, -s), block(dy, -s), zu)
                share(dy, -s)
                yield time + 3.6 * s + 0.1, down
                if s < 3 or dy in (1, -1):
                    down = start(block(dy, s), block(dy, s), zd)
                share(dy, s)
            yield time + 14.4, up if dy in (0, 2) else down
            share(dy, 4)

        def from_above():
            yield 1.9, to_d
            yield from along_z(1, 2.0)

        def from_across():
            yield 2.4, over
            yield from along_z(2, 2.5)

        to_u = start(block(0, 0), block(0, 0), yu)
        to_d = start(block(0, 0), block(0, 0), yd)
        over = start(block(0, 0), block(0, 0), me.at(dy=2))

        def from_below():
            yield 1.9, to_u
            yield from along_z(-1, 2.0)

        return [along_z(0, 0.0), from_below(), from_above(), from_across()]

    def qkv_weights():
        def block(dy, dz):
            return wq.at[yy(dy), zz(dz)]

        def available(dz):
            one, slot = block(0, dz), sends.slot()
            start(one, one, yu, slot)
            start(one, one, yd, slot)
            if len(spread) >= 5:
                start(one, one, me.at(dy=2), last)
            spread.append((dz, slot))

        def pass_on(n, time):
            dz, slot = spread[n]
            yield time, None
            sends.arrive(slot, 2 * 32 * QCOLS // 128)
            if n >= 5:
                return
            one = block(-1, dz) if dz in (0, 1, 2, -3) else block(1, dz)
            start(one, one, yu if dz in (0, 1, 2, -3) else yd, last)

        spread, last = [], sends.slot()
        order = (1, -1, 2, -2, 3, -3, 4)
        direct = [
            start(block(0, 0), block(0, 0), me.at(dz=dz)) for dz in order
        ]
        available(0)
        for n, dz in enumerate(order):
            yield 2.0 + 0.5 * n, direct[n]
            available(-dz)
            if n >= 3:
                yield from pass_on(n - 3, 2.1 + 0.5 * n)
        for n in range(4, 8):
            yield from pass_on(n, 4.6 + 0.5 * n)
        yield 8.8, None
        sends.arrive(last, NZ * 32 * QCOLS // 128)
        ready.add("w")

    def row_blocks():
        loads[0].wait()
        xc[...] = normalize(ref.frames[...].astype(F32)).astype(BF)
        xg[dp] = xc[...]
        low, high = pl.ds(0, 64), pl.ds(64, 64)
        left = xg.at[((x + NX - 1) % NX) * 2 + c]
        right = xg.at[((x + 1) % NX) * 2 + c]
        across = xg.at[((x + 2) % NX) * 2 + c]
        r_low = start(xc.at[low], xg.at[dp, low], xr)
        l_high = start(xc.at[high], xg.at[dp, high], xl)
        to_sib = start(xc, xg.at[dp], sib)
        r_high = start(xc.at[high], xg.at[dp, high], xr)
        l_low = start(xc.at[low], xg.at[dp, low], xl)
        write_notes(lengths, ids, notes)
        ng[dp] = notes[...]
        for device in others:
            start(notes, ng.at[dp], device, noted)
        start(wup.at[1 - c], ref.up_sib, sib, swaps)
        start(wdn.at[1 - c], ref.dn_sib, sib, swaps)
        yield 5.5, r_low
        over_r = start(left.at[low], left.at[low], xr)
        yield 5.5, l_high
        over_l = start(right.at[high], right.at[high], xl)
        yield 8.5, r_high
        left_sib = start(left, left, sib)
        yield 8.5, l_low
        right_sib = start(right, right, sib)
        yield 8.6, to_sib
        yield 8.6, None
        sends.arrive(noted, 7 * NOTES)
        ready.add(0)
        ready.add(1)
        plan(dp, ng, ref.hits, ref.masks)
        yield 10.0, over_r
        yield 10.0, over_l
        across_sib = start(across, across, sib)
        yield 10.5, left_sib
        yield 10.5, right_sib
        ready.add(2)
        yield 12.0, across_sib
        ready.add(3)

    def attention():
        pairs = (
            (dp, x * 2 + 1 - c),
            ((x + NX - 1) % NX * 2 + c, (x + 1) % NX * 2 + c),
            ((x + NX - 1) % NX * 2 + 1 - c, (x + 1) % NX * 2 + 1 - c),
            ((x + 2) % NX * 2 + c, (x + 2) % NX * 2 + 1 - c),
        )
        for n, pair in enumerate(pairs):
            yield (9.0, 9.6, 10.6, 12.1)[n], None
            assert "w" in ready and n in ready
            rows = jnp.concatenate([xg[b] for b in pair], axis=0)
            qkv = jnp.dot(rows, wq[...].reshape(D, QCOLS), preferred_element_type=F32).astype(BF)
            for m, b in enumerate(pair):
                marks = ng[b, :4, :].astype(F32)
                result = attend(qkv[m * ROWS : (m + 1) * ROWS], marks)
                if (n, m) == (0, 0):
                    heads[dp] = result
                else:
                    mixed[b] = result
                    start(mixed.at[b], heads.at[dp], (b, me.ex), heard)

    run_tasks([qkv_weights(), *out_weights(), row_blocks(), attention()])
    sends.arrive(given, D * OCOLS // 128)
    sends.arrive(heard, 7 * ROWS)
    sends.arrive(swaps, 2 * D * 512 // 128)
    rows = jnp.concatenate([heads[b] for b in range(8)], axis=1)
    swapped = []
    loads[4].wait()
    loads[5].wait()
    middle(
        ref.frames,
        rows,
        wo,
        ref.conv_w,
        ref.w_router,
        ids,
        ref.second,
        ref.hidden,
        ref.gates,
        ref.shifted,
        ref.masks,
        lambda: swapped.append(start(ref.hidden, ref.both.at[c], sib)),
    )
    return swapped[0]


PLANE = [(dy, dz) for dz in range(NZ) for dy in range(NY) if (dy, dz) != (0, 0)]


def plane_peers(me):
    return [me.at(dy=dy, dz=dz) for dy, dz in PLANE]


ORDER = (0, 2, 6, 4, 3, 5, 1, 7)
STRAIGHT = 7


def experts(me, sends, theirs, block_out, ref):
    start = sends.start
    hidden, hits, gates, second = ref.hidden, ref.hits, ref.gates, ref.second
    both, cells, routed, part, back = ref.both, ref.cells, ref.routed, ref.part, ref.back
    rel_r, rel_l, in_l, in_r = ref.rel_r, ref.rel_l, ref.in_l, ref.in_r
    sum_r, sum_l, total, picked, inbox = ref.sum_r, ref.sum_l, ref.total, ref.picked, ref.inbox
    x, y, z, c = me.x, me.y, me.z, me.c
    xr, xl, sib = me.at(dx=1), me.at(dx=-1), me.at(other=True)
    right, left, across = (x + 1) % NX, (x + NX - 1) % NX, (x + 2) % NX
    low, high = pl.ds(0, 2), pl.ds(2, 2)

    both[c] = hidden[...]
    pick = hits[0] + hits[1]
    theirs.wait_recv()
    rows = jnp.dot(pick, both[...].reshape(2 * ROWS, D), preferred_element_type=F32)
    cells[...] = rows.astype(BF).reshape(PLACES, 8, 128).reshape(NY, NZ, SUB, 128)
    routed[z, x, y] = cells[y, z]

    direct, sideways, relays, begun, closing = [], [], [], [], []
    returned = sends.slot()

    def group(i):
        return (z - ORDER[i] + NZ) % NZ

    def issue(i):
        dz = ORDER[i]
        direct.append(sends.slot())
        for dy in range(NY):
            if (dy, dz) != (0, 0):
                src = cells.at[(y + dy) % NY, (z + dz) % NZ]
                start(src, routed.at[z, x, y], me.at(dy=dy, dz=dz), direct[i])

    def spread(i):
        sends.arrive(direct[i], (NY - (ORDER[i] == 0)) * SUB)
        block = routed.at[group(i), x]
        sideways.append((start(block, block, xr), start(block, block, xl)))

    def relay(i):
        g = group(i)
        relays.append(sends.slot())
        sideways[i][0].wait_recv()
        one = routed.at[g, left, low]
        start(one, one, xr, relays[i])
        sideways[i][1].wait_recv()
        two = routed.at[g, right, high]
        start(two, two, xl, relays[i])

    def compute(i):
        g = group(i)
        sends.arrive(relays[i], NY * SUB)
        count = NX * NY * CELL
        rows = routed[g].reshape(count * 8, 128).reshape(count, 8, 128).reshape(count, D)
        result = None
        for up, down in ((ref.up_own, ref.dn_own), (ref.up_sib, ref.dn_sib)):
            upward = jnp.dot(rows, up[...], preferred_element_type=F32)
            activated = (upward / (1.0 + jnp.exp(-upward))).astype(BF)
            term = jnp.dot(activated, down[...], preferred_element_type=F32)
            result = term if result is None else result + term
        part[g] = result.astype(BF).reshape(count, 8, 128).reshape(NX, NY, SUB, 128)
        closing.append(sends.slot())
        if i >= STRAIGHT:
            start(part.at[g, across, low], rel_r.at[g], me.at(dx=2), closing[i])
            start(part.at[g, across, high], rel_l.at[g], me.at(dx=2), closing[i])
            start(part.at[g, right], in_l.at[g], xr, closing[i])
            start(part.at[g, left], in_r.at[g], xl, closing[i])
            return
        begun.append(
            (
                start(part.at[g, across, low], rel_r.at[g], xr),
                start(part.at[g, across, high], rel_l.at[g], xl),
            )
        )
        start(part.at[g, right, high], in_l.at[g, high], xr, closing[i])
        start(part.at[g, left, low], in_r.at[g, low], xl, closing[i])

    def add(i):
        g = group(i)
        if i >= STRAIGHT:
            return
        begun[i][0].wait_recv()
        sum_r[g] = (part[g, right, low].astype(F32) + rel_r[g].astype(F32)).astype(BF)
        start(sum_r.at[g], in_l.at[g, low], xr, closing[i])
        begun[i][1].wait_recv()
        sum_l[g] = (part[g, left, high].astype(F32) + rel_l[g].astype(F32)).astype(BF)
        start(sum_l.at[g], in_r.at[g, high], xl, closing[i])

    def close(i):
        g = group(i)
        sends.arrive(closing[i], (2 + (i >= STRAIGHT)) * NY * SUB)
        added = part[g, x].astype(F32) + in_l[g].astype(F32) + in_r[g].astype(F32)
        if i >= STRAIGHT:
            added = added + jnp.concatenate([rel_r[g], rel_l[g]], axis=0).astype(F32)
        total[g] = added.astype(BF)
        for dy in range(NY):
            src = total.at[g, (y + dy) % NY]
            if (dy, ORDER[i]) == (0, 0):
                back[y, z] = total[g, y]
            else:
                start(src, back.at[y, z], me.at(dy=dy, dz=-ORDER[i]), returned)

    ahead = 2
    for i in range(ahead):
        issue(i)
    for t in range(NZ + 3):
        if t + ahead < NZ:
            issue(t + ahead)
        if t < NZ:
            spread(t)
        if 1 <= t <= NZ:
            relay(t - 1)
        if 2 <= t <= NZ + 1:
            compute(t - 2)
        if 3 <= t <= NZ + 2:
            add(t - 3)
        if 4 <= t:
            close(t - 4)
    close(NZ - 1)
    sends.arrive(returned, (NY * NZ - 1) * SUB)

    rows = back[...].reshape(PLACES * 8, 128).reshape(PLACES, 8, 128).reshape(PLACES, D)

    def take(k, core):
        columns = pl.ds(pl.multiple_of(core * ROWS, ROWS), ROWS)
        return lax.dot_general(
            hits[k, :, columns], rows, (((0,), (0,)), ((), ())), preferred_element_type=F32
        )

    given = []
    for k in range(TOP):
        picked[k] = take(k, 1 - c).astype(BF)
        given.append(start(picked.at[k], inbox.at[k], sib))
    result = second[...].astype(F32)
    mine = [take(k, c) for k in range(TOP)]
    for k in range(TOP):
        given[k].wait_recv()
        result = result + gates[:, k : k + 1] * (mine[k] + inbox[k].astype(F32))
    block_out[...] = result.astype(BF)


def local(frames, lengths, w_qkv, w_out, conv_w, w_router, expert_ids, w_up, w_down):
    result = pl.pallas_call(
        block_kernel,
        out_shape=jax.ShapeDtypeStruct((ROWS, D), BF),
        in_specs=[SMEM, VMEM] + [HBM] * 7,
        out_specs=VMEM,
        scratch_shapes=[pltpu.VMEM(*shape) for shape in SCRATCH.values()]
        + [
            pltpu.SemaphoreType.DMA((SEND_SLOTS,)),
            pltpu.SemaphoreType.DMA((RECV_SLOTS,)),
            pltpu.SemaphoreType.DMA((9,)),
        ],
        compiler_params=pltpu.CompilerParams(
            collective_id=0, has_side_effects=True, vmem_limit_bytes=60 << 20
        ),
        name="block",
    )(lengths, expert_ids.T, frames, conv_w, w_router.T, w_qkv, w_out, w_up, w_down)
    return jnp.maximum(result, jnp.finfo(BF).min)


def solution(mesh):
    in_specs = (
        P(("dp", "expert"), None),
        P(("dp", "expert"), None),
        P("expert", None),
        P("expert", None),
        P(),
        P(),
        P(("dp", "expert"), None),
        P("expert", None, "dp"),
        P("expert", "dp", None),
    )
    out_specs = P(("dp", "expert"), None)
    return jax.shard_map(local, mesh=mesh, in_specs=in_specs, out_specs=out_specs, check_vma=False)
```
